32 devices in a mesh: dp: 16 (over z, x, core), outer: 2 (over y).
Axes of the slice: x: 2, y: 2, z: 4, core: 2. Of those that a mesh axis runs over, the one named last changes fastest.
Arguments:
- clip_frames: bfloat16 [256, 4, 8, 8, 256], P(('dp', 'outer')), may hold values from -6 to 6
- valid_mask: int32 [256, 4, 8, 8], P(('dp', 'outer')), may hold values from 0 to 1, as said below
- labels: int32 [256], P(('dp', 'outer')), may hold values from 0 to 399
- clip_keep: int32 [256], P(('dp', 'outer')), may hold values from 0 to 1, as said below
- step_count: int32 [1], replicated, may hold values from 1 to 20
- w_entry: float32 [256, 512], P(None, ('dp', 'outer')), may hold values from -0.375 to 0.375
- w_spatial: float32 [9, 512, 1152], P(None, ('dp', 'outer')), may hold values from -0.09375 to 0.09375
- w_temporal: float32 [3, 1152, 512], P(None, None, ('dp', 'outer')), may hold values from -0.109375 to 0.109375
- w_head: float32 [512, 400], P(('dp', 'outer')), may hold values from -0.25 to 0.25
- small_params: float32 [3728], replicated, may hold values from 0.5 to 1.5
- entry_first: float32 [256, 512], P(None, ('dp', 'outer')), may hold values from -0.005859375 to 0.005859375
- entry_second: float32 [256, 512], P(None, ('dp', 'outer')), may hold values from 1.4424324e-07 to 5.76973e-07
- spatial_first: float32 [9, 512, 1152], P(None, ('dp', 'outer')), may hold values from -0.001953125 to 0.001953125
- spatial_second: float32 [9, 512, 1152], P(None, ('dp', 'outer')), may hold values from 1.9073486e-08 to 7.6293944e-08
- temporal_first: float32 [3, 1152, 512], P(None, None, ('dp', 'outer')), may hold values from -0.009765625 to 0.009765625
- temporal_second: float32 [3, 1152, 512], P(None, None, ('dp', 'outer')), may hold values from 4.7683716e-07 to 1.9073486e-06
- head_first: float32 [512, 400], P(('dp', 'outer')), may hold values from -0.0390625 to 0.0390625
- head_second: float32 [512, 400], P(('dp', 'outer')), may hold values from 6.25e-06 to 2.5e-05
- small_first: float32 [3728], replicated
- small_second: float32 [3728], replicated
Outputs:
- loss: float32 [], replicated
- entry_new: float32 [256, 512], P(None, ('dp', 'outer'))
- entry_first_new: float32 [256, 512], P(None, ('dp', 'outer'))
- entry_second_new: float32 [256, 512], P(None, ('dp', 'outer'))
- spatial_new: float32 [9, 512, 1152], P(None, ('dp', 'outer'))
- spatial_first_new: float32 [9, 512, 1152], P(None, ('dp', 'outer'))
- spatial_second_new: float32 [9, 512, 1152], P(None, ('dp', 'outer'))
- temporal_new: float32 [3, 1152, 512], P(None, None, ('dp', 'outer'))
- temporal_first_new: float32 [3, 1152, 512], P(None, None, ('dp', 'outer'))
- temporal_second_new: float32 [3, 1152, 512], P(None, None, ('dp', 'outer'))
- head_new: float32 [512, 400], P(('dp', 'outer'))
- head_first_new: float32 [512, 400], P(('dp', 'outer'))
- head_second_new: float32 [512, 400], P(('dp', 'outer'))
- small_new: float32 [3728], replicated
- small_first_new: float32 [3728], replicated
- small_second_new: float32 [3728], replicated
- entry_copy: bfloat16 [256, 512], P(None, ('dp', 'outer'))
- spatial_copy: bfloat16 [9, 512, 1152], P(None, ('dp', 'outer'))
- temporal_copy: bfloat16 [3, 1152, 512], P(None, None, ('dp', 'outer'))
- head_copy: bfloat16 [512, 400], P(('dp', 'outer'))
The draws below stay inside these ranges and needn't reach their ends.
Inputs may be any that keep to these rules, and one draw needn't show every extreme that they name: `valid_mask`: the valid positions of a clip form a box: its first k frames with k at least half of 4, and a centered block of rows and columns, at least half of 8 and of 8 long. `clip_keep`: the first clip is kept.
All inputs are finite; a program needn't handle non-finite values.
Results may differ from the reference program's by a relative error of at most 0.025.
The reference program's roundings to bfloat16 on the way count: a program that leaves them out, or rounds other values in their place, can miss the bound.
Values may be sent and summed in bfloat16 or wider, within the bound.
No kernel may reach another device: no remote copies, remote signals or barrier semaphores. Data moves between devices by JAX's collectives and lax.ppermute only.
A program may use at most 256 MiB of HBM per device.

```python
import math
import jax
import jax.numpy as jnp
from jax import lax

CHAN_IN = 256
CHANNELS = 512
HIDDEN_SIZE = 1152
CLASSES = 400
FRAMES = 4
HEIGHT = 8
BREADTH = 8
CLIPS = 256
SMALL_COUNT = 3728


def draw_valid_mask(key, part):
    keys = jax.random.split(key, 3)
    frame_len = jax.random.randint(keys[0], (CLIPS,), (FRAMES + 1) // 2, FRAMES + 1)
    row_len = jax.random.randint(keys[1], (CLIPS,), (HEIGHT + 1) // 2, HEIGHT + 1)
    col_len = jax.random.randint(keys[2], (CLIPS,), (BREADTH + 1) // 2, BREADTH + 1)
    row_start = (HEIGHT - row_len) // 2
    col_start = (BREADTH - col_len) // 2
    frame_pos = jnp.arange(FRAMES)[None, :, None, None]
    row_pos = jnp.arange(HEIGHT)[None, None, :, None]
    col_pos = jnp.arange(BREADTH)[None, None, None, :]
    inside = frame_pos < frame_len[:, None, None, None]
    inside = inside & (row_pos >= row_start[:, None, None, None]) & (row_pos < (row_start + row_len)[:, None, None, None])
    inside = inside & (col_pos >= col_start[:, None, None, None]) & (col_pos < (col_start + col_len)[:, None, None, None])
    return inside.astype(jnp.int32)


def draw_clip_keep(key, part):
    picks = jax.random.randint(key, (CLIPS,), 0, 4)
    keep_flag = (picks > 0) | (jnp.arange(CLIPS) == 0)
    return keep_flag.astype(jnp.int32)


def small_scales():
    positions = float(CLIPS * FRAMES * HEIGHT * BREADTH)
    gain_one = 1.5 / (positions * HIDDEN_SIZE) ** 0.5
    shift_one = 0.5 / (float(CLIPS) * HIDDEN_SIZE) ** 0.5
    gain_two = 1.3 / (positions * CHANNELS) ** 0.5
    shift_two = 0.6 / (float(CLIPS) * CHANNELS) ** 0.5
    bias_scale = 1.0 / (float(CLIPS) * CLASSES) ** 0.5
    return jnp.concatenate([jnp.full((HIDDEN_SIZE,), gain_one, jnp.float32), jnp.full((HIDDEN_SIZE,), shift_one, jnp.float32), jnp.full((CHANNELS,), gain_two, jnp.float32), jnp.full((CHANNELS,), shift_two, jnp.float32), jnp.full((CLASSES,), bias_scale, jnp.float32)])


def draw_small_first(key, part):
    noise = jnp.clip(jax.random.normal(jax.random.fold_in(key, 11), (SMALL_COUNT,), jnp.float32), -4.0, 4.0)
    return small_scales() * noise


def draw_small_second(key, part):
    factor = jnp.exp(jax.random.uniform(jax.random.fold_in(key, 13), (SMALL_COUNT,), jnp.float32, 0.0, 1.3862944))
    scales = small_scales()
    return scales * scales * factor


def touch_ends(result, key, least, high):
    dims = result.shape
    place = [jax.random.randint(jax.random.fold_in(key, axis), (), 0, dims[axis]) for axis in range(len(dims))]
    result = result.at[tuple(place)].set(least)
    longest = dims.index(max(dims))
    place[longest] = (place[longest] + 1) % dims[longest]
    return result.at[tuple(place)].set(high)


def level_of(own_key, dims, pieces, least, top_value):
    def one(position, shards_of):
        heights = jax.random.uniform(jax.random.fold_in(jax.random.fold_in(own_key, 6), position), (shards_of,), jnp.float32, least / len(pieces), top_value / len(pieces))
        return jnp.repeat(jnp.exp(heights), dims[position] // shards_of).reshape((-1,) + (1,) * (len(dims) - position - 1))

    level = one(*pieces[0])
    for cut in pieces[1:]:
        level = level * one(*cut)
    return level


def gaussian(rng, dims, deviation, bound, pieces=(), held_as=jnp.bfloat16):
    drawn = deviation * jax.random.normal(rng, dims, jnp.float32)
    if pieces:
        drawn = drawn * level_of(rng, dims, pieces, -0.22, 0.18)
    return jnp.clip(drawn, -bound, bound).astype(held_as)


def setup_inputs(seed: int = 0) -> dict:
    key_of = jax.random.split(jax.random.key(seed), 21)
    return {
        "clip_frames": gaussian(key_of[0], (CLIPS, FRAMES, HEIGHT, BREADTH, CHAN_IN), 1.0, 6.0, ((0, 32),)),
        "valid_mask": draw_valid_mask(jax.random.fold_in(key_of[20], 71), 0),
        "labels": touch_ends(jax.random.randint(key_of[2], (CLIPS,), 0, CLASSES), jax.random.fold_in(key_of[2], 1), 0, CLASSES - 1).astype(jnp.int32),
        "clip_keep": draw_clip_keep(jax.random.fold_in(key_of[20], 71), 0),
        "step_count": jax.random.randint(key_of[4], (1,), 1, 21).astype(jnp.int32),
        "w_entry": gaussian(key_of[5], (CHAN_IN, CHANNELS), CHAN_IN ** -0.5, 0.375, ((1, 32),), jnp.float32),
        "w_spatial": gaussian(key_of[6], (9, CHANNELS, HIDDEN_SIZE), (9 * CHANNELS) ** -0.5, 0.09375, ((1, 32),), jnp.float32),
        "w_temporal": gaussian(key_of[7], (3, HIDDEN_SIZE, CHANNELS), (3 * HIDDEN_SIZE) ** -0.5, 0.109375, ((2, 32),), jnp.float32),
        "w_head": gaussian(key_of[8], (CHANNELS, CLASSES), CHANNELS ** -0.5, 0.25, ((0, 32),), jnp.float32),
        "small_params": jnp.clip(1.0 + 0.1 * jax.random.normal(key_of[9], (SMALL_COUNT,), jnp.float32), 0.5, 1.5),
        "entry_first": gaussian(key_of[10], (CHAN_IN, CHANNELS), (2.2 / (CLIPS * FRAMES * HEIGHT * BREADTH * CHANNELS) ** 0.5), 0.005859375, ((1, 32),), jnp.float32),
        "entry_second": jnp.clip(jnp.exp(math.log(5.769729796156753e-07) - 1.3862944 * jax.random.uniform(key_of[11], (CHAN_IN, CHANNELS), jnp.float32) ** level_of(key_of[11], (CHAN_IN, CHANNELS), ((1, 32),), -0.2, 0.2)), 1.4424324490391882e-07, 5.769729796156753e-07),
        "spatial_first": gaussian(key_of[12], (9, CHANNELS, HIDDEN_SIZE), (1.8 * (CHANNELS / (CLIPS * FRAMES * HEIGHT * BREADTH)) ** 0.5 / HIDDEN_SIZE), 0.001953125, ((1, 32),), jnp.float32),
        "spatial_second": jnp.clip(jnp.exp(math.log(7.629394360719743e-08) - 1.3862944 * jax.random.uniform(key_of[13], (9, CHANNELS, HIDDEN_SIZE), jnp.float32) ** level_of(key_of[13], (9, CHANNELS, HIDDEN_SIZE), ((1, 32),), -0.2, 0.2)), 1.907348590179936e-08, 7.629394360719743e-08),
        "temporal_first": gaussian(key_of[14], (3, HIDDEN_SIZE, CHANNELS), (0.25 / (CLIPS * CHANNELS) ** 0.5), 0.009765625, ((2, 32),), jnp.float32),
        "temporal_second": jnp.clip(jnp.exp(math.log(1.9073486328125e-06) - 1.3862944 * jax.random.uniform(key_of[15], (3, HIDDEN_SIZE, CHANNELS), jnp.float32) ** level_of(key_of[15], (3, HIDDEN_SIZE, CHANNELS), ((2, 32),), -0.2, 0.2)), 4.76837158203125e-07, 1.9073486328125e-06),
        "head_first": gaussian(key_of[16], (CHANNELS, CLASSES), (0.8 / (CLIPS * CLASSES) ** 0.5), 0.0390625, ((0, 32),), jnp.float32),
        "head_second": jnp.clip(jnp.exp(math.log(2.499999936844688e-05) - 1.3862944 * jax.random.uniform(key_of[17], (CHANNELS, CLASSES), jnp.float32) ** level_of(key_of[17], (CHANNELS, CLASSES), ((0, 32),), -0.2, 0.2)), 6.24999984211172e-06, 2.499999936844688e-05),
        "small_first": draw_small_first(jax.random.fold_in(key_of[20], 71), 0),
        "small_second": draw_small_second(jax.random.fold_in(key_of[20], 71), 0),
    }


EPSILON = 1e-05
ADAM_EPS = 1e-08
DECAY_RATE = 0.1
SMOOTHING = 0.1

@jax.custom_vjp
def low(v):
    return lax.optimization_barrier(v.astype(jnp.bfloat16)).astype(jnp.float32)

@jax.custom_vjp
def low_back(v):
    return v

def low_keep(v):
    return (low(v), None)

def low_pass(kept, grad):
    return (grad,)

def back_keep(v):
    return (v, None)

def back_low(kept, grad):
    return (low(grad),)
low.defvjp(low_keep, low_pass)
low_back.defvjp(back_keep, back_low)

def spatial_conv(field, kernel):
    padded = jnp.pad(field, ((0, 0), (0, 0), (1, 1), (1, 1), (0, 0)))
    total = jnp.zeros(field.shape[:4] + (kernel.shape[2],), jnp.float32)
    for offset in range(9):
        window = padded[:, :, offset // 3:offset // 3 + HEIGHT, offset % 3:offset % 3 + BREADTH, :]
        total = total + jnp.einsum('nfhwc,cm->nfhwm', window, kernel[offset], precision=lax.Precision.HIGHEST)
    return total

def temporal_conv(field, kernel):
    padded = jnp.pad(field, ((0, 0), (1, 1), (0, 0), (0, 0), (0, 0)))
    total = jnp.zeros(field.shape[:4] + (kernel.shape[2],), jnp.float32)
    for offset in range(3):
        window = padded[:, offset:offset + FRAMES]
        total = total + jnp.einsum('nfhwc,cm->nfhwm', window, kernel[offset], precision=lax.Precision.HIGHEST)
    return total

def batch_norm(value, valid, count, gain, shift):
    mean_val = lax.optimization_barrier(jnp.sum(value * valid, axis=(0, 1, 2, 3))) / count
    variance = lax.optimization_barrier(jnp.sum(value * value * valid, axis=(0, 1, 2, 3))) / count - mean_val * mean_val
    return gain * ((value - mean_val) * lax.rsqrt(variance + EPSILON)) + shift

def adamw(master, grad, first, second, rate, decay, correction):
    first_new = 0.5 * first + 0.5 * grad
    second_new = 0.5 * second + 0.5 * grad * grad
    master_new = master - rate * (first_new / correction / (jnp.sqrt(second_new / correction) + ADAM_EPS) + decay * master)
    return (master_new, first_new, second_new)

def reference(clip_frames, valid_mask, labels, clip_keep, step_count, w_entry, w_spatial, w_temporal, w_head, small_params, entry_first, entry_second, spatial_first, spatial_second, temporal_first, temporal_second, head_first, head_second, small_first, small_second):
    frames32 = clip_frames.astype(jnp.float32)
    valid = valid_mask.astype(jnp.float32)[..., None]
    count = jnp.sum(valid)
    keep_float = clip_keep.astype(jnp.float32)
    kept = jnp.sum(keep_float)
    clip_count = lax.optimization_barrier(jnp.sum(valid, axis=(1, 2, 3)))
    target = (1.0 - SMOOTHING) * (labels[:, None] == jnp.arange(CLASSES)[None, :]).astype(jnp.float32) + SMOOTHING / CLASSES

    def forward(params):
        entry_w, spatial_w, temporal_w, head_w, small = params
        gain_one = small[:HIDDEN_SIZE]
        shift_one = small[HIDDEN_SIZE:2 * HIDDEN_SIZE]
        gain_two = small[2 * HIDDEN_SIZE:2 * HIDDEN_SIZE + CHANNELS]
        shift_two = small[2 * HIDDEN_SIZE + CHANNELS:2 * HIDDEN_SIZE + 2 * CHANNELS]
        bias = small[2 * HIDDEN_SIZE + 2 * CHANNELS:]
        entry = low_back(jnp.einsum('nfhwc,cd->nfhwd', frames32, low(entry_w), precision=lax.Precision.HIGHEST))
        field = entry * valid
        conv_one = low_back(spatial_conv(low(field), low(spatial_w)))
        first = jnp.maximum(batch_norm(conv_one, valid, count, gain_one, shift_one), 0.0) * valid
        conv_two = low_back(temporal_conv(low(first), low(temporal_w)))
        second = jnp.maximum(batch_norm(conv_two, valid, count, gain_two, shift_two) + field, 0.0) * valid
        pooled = lax.optimization_barrier(jnp.sum(second, axis=(1, 2, 3))) / clip_count
        logits = low_back(jnp.dot(low(pooled), low(head_w), precision=lax.Precision.HIGHEST, preferred_element_type=jnp.float32)) + bias
        log_prob = jax.nn.log_softmax(logits, axis=-1)
        per_clip = -lax.optimization_barrier(jnp.sum(target * log_prob, axis=-1))
        return jnp.sum(keep_float * per_clip) / kept
    params = (w_entry, w_spatial, w_temporal, w_head, small_params)
    loss, pullback = jax.vjp(forward, params)
    grads = pullback(jnp.ones((), jnp.float32))[0]
    correction = 1.0 - jnp.power(0.5, step_count[0].astype(jnp.float32))
    entry_out = adamw(w_entry, grads[0], entry_first, entry_second, 0.06, DECAY_RATE, correction)
    spatial_out = adamw(w_spatial, grads[1], spatial_first, spatial_second, 0.02, DECAY_RATE, correction)
    temporal_out = adamw(w_temporal, grads[2], temporal_first, temporal_second, 0.02, DECAY_RATE, correction)
    head_out = adamw(w_head, grads[3], head_first, head_second, 0.05, DECAY_RATE, correction)
    small_out = adamw(small_params, grads[4], small_first, small_second, 0.5, 0.0, correction)
    return (loss, entry_out[0], entry_out[1], entry_out[2], spatial_out[0], spatial_out[1], spatial_out[2], temporal_out[0], temporal_out[1], temporal_out[2], head_out[0], head_out[1], head_out[2], small_out[0], small_out[1], small_out[2], entry_out[0].astype(jnp.bfloat16), spatial_out[0].astype(jnp.bfloat16), temporal_out[0].astype(jnp.bfloat16), head_out[0].astype(jnp.bfloat16))
```

```python
import functools

import jax
import jax.numpy as jnp
from jax import lax
from jax.experimental import pallas as pl
from jax.experimental.pallas import tpu as pltpu
from jax.sharding import PartitionSpec as P

CHANNELS = 512
HIDDEN = 1152
CLASSES = 400
CHAN_IN = 256

EPSILON = 1e-05
ADAM_EPS = 1e-08
DECAY_RATE = 0.1
SMOOTHING = 0.1

AXES = ("dp", "outer")
BF = jnp.bfloat16
F32 = jnp.float32
MIB = 1 << 20
EXACT = lax.Precision.HIGHEST


def wide(column, times):
    return jnp.concatenate([column] * times, axis=1)


def dot_nn(left, right):
    return lax.dot_general(left, right, (((1,), (0,)), ((), ())), preferred_element_type=F32)


def dot_nt(left, right):
    return lax.dot_general(left, right, (((1,), (1,)), ((), ())), preferred_element_type=F32)


def dot_tn(left, right):
    return lax.dot_general(left, right, (((0,), (0,)), ((), ())), preferred_element_type=F32)


def to_owner_order(row, order):
    return lax.dot_general(
        row, order, (((1,), (0,)), ((), ())), precision=EXACT, preferred_element_type=F32
    )


def to_local_order(row, order):
    return lax.dot_general(
        row, order, (((1,), (1,)), ((), ())), precision=EXACT, preferred_element_type=F32
    )


def fold(value, step):
    return jnp.sum(value.reshape(value.shape[0] // step, step, value.shape[1]), axis=0)


def whole(shape):
    return pl.BlockSpec(shape, lambda *_: (0,) * len(shape))


def call(kernel, name, grid, in_specs, out_specs, out_shape, scratch=(), aliases=None, vmem=40, flops=0):
    return pl.pallas_call(
        kernel,
        name=name,
        grid=grid,
        in_specs=in_specs,
        out_specs=out_specs,
        out_shape=out_shape,
        scratch_shapes=list(scratch),
        input_output_aliases=aliases or {},
        compiler_params=pltpu.CompilerParams(vmem_limit_bytes=vmem * MIB),
        cost_estimate=pl.CostEstimate(flops=flops, bytes_accessed=20 * MIB, transcendentals=0),
    )


def entry_kernel(count, side, clips, x_ref, valid_ref, *refs):
    pieces, (field_ref, cols_ref, conv_ref, w_ref, e_ref) = refs[:count], refs[count:]

    @pl.when(pl.program_id(0) == 0)
    def _():
        at = 0
        for piece in pieces:
            rows = piece.shape[0]
            for b in range(3):
                w_ref[b * CHANNELS + at : b * CHANNELS + at + rows, :] = piece[
                    :, b * HIDDEN : (b + 1) * HIDDEN
                ]
            e_ref[at : at + rows, :] = piece[:, 3 * HIDDEN :]
            at += rows

    value = dot_nt(x_ref[...], e_ref[...]) * wide(valid_ref[...], CHANNELS // 128)
    field_ref[...] = value
    rows = value.shape[0]
    group = side * clips
    grid3 = value.reshape(rows // group, group, CHANNELS)
    edge = jnp.zeros((rows // group, clips, CHANNELS), F32)
    left = jnp.concatenate([edge, grid3[:, : group - clips]], axis=1).reshape(rows, CHANNELS)
    right = jnp.concatenate([grid3[:, clips:], edge], axis=1).reshape(rows, CHANNELS)
    cols_ref[:, :CHANNELS] = left.astype(BF)
    cols_ref[:, CHANNELS : 2 * CHANNELS] = value.astype(BF)
    cols_ref[:, 2 * CHANNELS :] = right.astype(BF)
    conv_ref[...] = dot_nn(cols_ref[...], w_ref[...])


def spatial_kernel(count, tap_row, group, cols_ref, conv_ref, *refs):
    pieces, refs = refs[:count], refs[count:]
    step = pl.program_id(0)
    if tap_row == 0:
        out_ref, w_ref = refs
    else:
        valid_ref, keep_ref, out_ref, stats_ref, w_ref, acc_ref = refs

    @pl.when(step == 0)
    def _():
        at = 0
        for piece in pieces:
            rows = piece.shape[0]
            for b in range(3):
                w_ref[b * CHANNELS + at : b * CHANNELS + at + rows, :] = piece[
                    :, b * HIDDEN : (b + 1) * HIDDEN
                ]
            at += rows

    rows = cols_ref.shape[0]
    if tap_row == 0:
        out_ref[:group] = conv_ref[:group]
        out_ref[group:] = conv_ref[group:] + dot_nn(cols_ref[: rows - group], w_ref[...])
        return
    out_ref[rows - group :] = conv_ref[rows - group :]
    out_ref[: rows - group] = conv_ref[: rows - group] + dot_nn(cols_ref[group:], w_ref[...])

    @pl.when(step == 0)
    def _():
        acc_ref[...] = jnp.zeros_like(acc_ref)

    value = out_ref[...]
    kept = value * wide(valid_ref[...], HIDDEN // 128)
    acc_ref[:, :HIDDEN] += fold(kept, 8)
    acc_ref[:, HIDDEN : 2 * HIDDEN] += fold(kept * value, 8)
    acc_ref[:, 2 * HIDDEN : 2 * HIDDEN + 128] += fold(valid_ref[...], 8)

    @pl.when(step == pl.num_programs(0) - 1)
    def _():
        acc_ref[:, 2 * HIDDEN + 128 :] = fold(keep_ref[...], 8)
        stats_ref[...] = jnp.sum(acc_ref[...], axis=0, keepdims=True)


def temporal_kernel(
    count, frames, recv_ref, conv_ref, valid_ref, valid_out_ref, gain_ref, shift_ref, order_ref, *refs
):
    pieces, refs = refs[:count], refs[count:]
    first_ref, two_ref, stats_ref, coef_ref, head_ref, w_ref, first_all, acc_ref = refs
    step = pl.program_id(0)
    per = conv_ref.shape[0]

    @pl.when(step == 0)
    def _():
        at = 0
        for piece in pieces:
            rows = piece.shape[0]
            head_ref[at : at + rows, :] = piece[:, :CHANNELS]
            w_ref[at : at + rows, :] = piece[:, CHANNELS:]
            at += rows
        total = jnp.sum(recv_ref[...], axis=0)
        count_all = total[:, 2 * HIDDEN : 2 * HIDDEN + 128]
        wide_count = wide(count_all, HIDDEN // 128)
        mean = total[:, :HIDDEN] / wide_count
        variance = total[:, HIDDEN : 2 * HIDDEN] / wide_count - mean * mean
        coef_ref[...] = jnp.zeros_like(coef_ref)
        coef_ref[0:1, :HIDDEN] = mean
        coef_ref[1:2, :HIDDEN] = lax.rsqrt(variance + EPSILON)
        coef_ref[2:3, :HIDDEN] = gain_ref[...]
        coef_ref[3:4, :HIDDEN] = shift_ref[...]
        coef_ref[0:1, HIDDEN:] = count_all
        coef_ref[1:2, HIDDEN:] = total[:, 2 * HIDDEN + 128 :]
        acc_ref[...] = jnp.zeros_like(acc_ref)

    @pl.when(step < frames)
    def _():
        normed = (conv_ref[...] - coef_ref[0:1, :HIDDEN]) * coef_ref[1:2, :HIDDEN]
        pre = coef_ref[2:3, :HIDDEN] * normed + coef_ref[3:4, :HIDDEN]
        first = (jnp.maximum(pre, 0.0) * wide(valid_ref[...], HIDDEN // 128)).astype(BF)
        first_ref[...] = first
        first_all[pl.ds(pl.multiple_of(step * per, per), per), :] = first

    def frame(start, taps):
        pieces_at = [
            first_all[pl.ds(pl.multiple_of(start + k * per, per), per), :] for k in range(len(taps))
        ]
        lanes = slice(taps[0] * HIDDEN, (taps[-1] + 1) * HIDDEN)
        value = dot_nt(jnp.concatenate(pieces_at, axis=1), w_ref[:, lanes])
        two_ref[...] = value
        kept = value * wide(valid_out_ref[...], CHANNELS // 128)
        acc_ref[:, :CHANNELS] += fold(kept, 8)
        acc_ref[:, CHANNELS:] += fold(kept * value, 8)

    @pl.when(step == 1)
    def _():
        frame(0, (1, 2))

    @pl.when(jnp.logical_and(step > 1, step < frames))
    def _():
        frame((step - 2) * per, (0, 1, 2))

    @pl.when(step == frames)
    def _():
        frame((frames - 2) * per, (0, 1))
        sums = jnp.sum(acc_ref[...], axis=0, keepdims=True)
        stats_ref[:, :CHANNELS] = to_owner_order(sums[:, :CHANNELS], order_ref[...])
        stats_ref[:, CHANNELS:] = to_owner_order(sums[:, CHANNELS:], order_ref[...])


def head_kernel(
    clips, recv_ref, two_ref, field_ref, valid_ref, coef_ref, gain_ref, shift_ref, order_ref,
    head_ref, bias_ref, target_ref, keep_ref,
    dpool_ref, stats_ref, coef_two_ref, keep_grad_ref, send_grad_ref, acc_ref, size_ref,
):
    step = pl.program_id(0)

    @pl.when(step == 0)
    def _():
        total = jnp.sum(recv_ref[...], axis=0)
        count = wide(coef_ref[0:1, HIDDEN:], CHANNELS // 128)
        mean = to_local_order(total[:, :CHANNELS], order_ref[...]) / count
        square = to_local_order(total[:, CHANNELS:], order_ref[...]) / count
        coef_two_ref[...] = jnp.zeros_like(coef_two_ref)
        coef_two_ref[0:1, :] = mean
        coef_two_ref[1:2, :] = lax.rsqrt(square - mean * mean + EPSILON)
        coef_two_ref[2:3, :] = to_local_order(gain_ref[...], order_ref[...])
        coef_two_ref[3:4, :] = to_local_order(shift_ref[...], order_ref[...])
        acc_ref[...] = jnp.zeros_like(acc_ref)
        size_ref[...] = jnp.zeros_like(size_ref)

    valid = wide(valid_ref[...], CHANNELS // 128)
    normed = (two_ref[...] - coef_two_ref[0:1, :]) * coef_two_ref[1:2, :]
    pre = coef_two_ref[2:3, :] * normed + coef_two_ref[3:4, :] + field_ref[...]
    mask = jnp.where(pre > 0.0, valid, 0.0)
    acc_ref[0] += fold(jnp.maximum(pre, 0.0) * valid, clips)
    acc_ref[1] += fold(mask, clips)
    acc_ref[2] += fold(mask * normed, clips)
    size_ref[...] += fold(valid_ref[...], clips)

    @pl.when(step == pl.num_programs(0) - 1)
    def _():
        size = wide(size_ref[...], CHANNELS // 128)
        pooled_low = (acc_ref[0] / size).astype(BF)
        head = head_ref[...]
        logits = dot_nn(pooled_low, head) + bias_ref[...]
        shifted = logits - jnp.max(logits, axis=1, keepdims=True)
        log_prob = shifted - jnp.log(jnp.sum(jnp.exp(shifted), axis=1, keepdims=True))
        target = target_ref[...]
        per_clip = -jnp.sum(target * log_prob, axis=1, keepdims=True)
        keep = wide(keep_ref[...], CHANNELS // 128)
        loss = jnp.sum(keep * per_clip, axis=0, keepdims=True)
        kept = wide(coef_ref[1:2, HIDDEN:], CHANNELS // 128)
        d_logits = keep * (jnp.exp(log_prob) - target) / kept
        d_low = d_logits.astype(BF)
        grad = dot_tn(pooled_low.astype(F32), d_low.astype(F32)).astype(BF)
        half = grad.shape[0] // 2
        keep_grad_ref[...] = grad[:half]
        send_grad_ref[...] = grad[half:]
        d_pooled = dot_nt(d_low, head) / size
        dpool_ref[...] = d_pooled
        sums_one = jnp.sum(acc_ref[1] * d_pooled, axis=0, keepdims=True)
        sums_two = jnp.sum(acc_ref[2] * d_pooled, axis=0, keepdims=True)
        stats_ref[:, :CHANNELS] = to_owner_order(sums_one, order_ref[...])
        stats_ref[:, CHANNELS : 2 * CHANNELS] = to_owner_order(sums_two, order_ref[...])
        lane = lax.broadcasted_iota(jnp.int32, (1, CHANNELS), 1)
        stats_ref[:, 2 * CHANNELS :] = jnp.where(
            lane < CLASSES, jnp.sum(d_logits, axis=0, keepdims=True), loss
        )


def first_back_kernel(
    count, frames, clips, recv_ref, two_ref, field_ref, valid_ref, coef_ref, coef_two_ref, dpool_ref,
    order_ref, conv_ref, valid_out_ref, *refs
):
    pieces, refs = refs[:count], refs[count:]
    dtwo_ref, mask_ref, dpre_ref, stats_ref, w_ref, dtwo_all, back_ref, acc_ref = refs
    step = pl.program_id(0)
    per = conv_ref.shape[0]

    @pl.when(step == 0)
    def _():
        at = 0
        for piece in pieces:
            rows = piece.shape[0]
            for t in range(3):
                w_ref[t * CHANNELS + at : t * CHANNELS + at + rows, :] = piece[
                    :, CHANNELS + t * HIDDEN : CHANNELS + (t + 1) * HIDDEN
                ]
            at += rows
        total = jnp.sum(recv_ref[...], axis=0)
        each = wide(coef_ref[0:1, HIDDEN:], CHANNELS // 128)
        back_ref[0:1, :] = to_local_order(total[:, :CHANNELS], order_ref[...]) / each
        back_ref[1:2, :] = to_local_order(total[:, CHANNELS : 2 * CHANNELS], order_ref[...]) / each
        acc_ref[...] = jnp.zeros_like(acc_ref)

    @pl.when(step < frames)
    def _():
        valid = wide(valid_ref[...], CHANNELS // 128)
        gain = coef_two_ref[2:3, :]
        inverse = coef_two_ref[1:2, :]
        normed = (two_ref[...] - coef_two_ref[0:1, :]) * inverse
        pre = gain * normed + coef_two_ref[3:4, :] + field_ref[...]
        mask = jnp.where(pre > 0.0, valid, 0.0)
        spread = jnp.broadcast_to(dpool_ref[...][None], (per // clips, clips, CHANNELS))
        d_pre = mask * spread.reshape(per, CHANNELS)
        low = (
            valid * (gain * inverse) * (d_pre - back_ref[0:1, :] - normed * back_ref[1:2, :])
        ).astype(BF)
        mask_ref[...] = mask.astype(BF)
        dtwo_ref[...] = low
        dtwo_all[pl.ds(pl.multiple_of(step * per, per), per), :] = low

    def frame(last, taps):
        pieces_at = [
            dtwo_all[pl.ds(pl.multiple_of(last - k * per, per), per), :] for k in range(len(taps))
        ]
        d_first = dot_nn(
            jnp.concatenate(pieces_at, axis=1),
            w_ref[taps[0] * CHANNELS : (taps[-1] + 1) * CHANNELS, :],
        )
        normed = (conv_ref[...] - coef_ref[0:1, :HIDDEN]) * coef_ref[1:2, :HIDDEN]
        pre = coef_ref[2:3, :HIDDEN] * normed + coef_ref[3:4, :HIDDEN]
        d_pre = jnp.where(pre > 0.0, d_first, 0.0) * wide(valid_out_ref[...], HIDDEN // 128)
        dpre_ref[...] = d_pre
        acc_ref[:, :HIDDEN] += fold(d_pre, 8)
        acc_ref[:, HIDDEN:] += fold(d_pre * normed, 8)

    @pl.when(step == 1)
    def _():
        frame(per, (0, 1))

    @pl.when(jnp.logical_and(step > 1, step < frames))
    def _():
        frame(step * per, (0, 1, 2))

    @pl.when(step == frames)
    def _():
        frame((frames - 1) * per, (1, 2))
        stats_ref[...] = jnp.sum(acc_ref[...], axis=0, keepdims=True)


def conv_back_kernel(recv_ref, conv_ref, dpre_ref, valid_ref, coef_ref, out_ref, back_ref):
    @pl.when(pl.program_id(0) == 0)
    def _():
        total = jnp.sum(recv_ref[...], axis=0)
        each = wide(coef_ref[0:1, HIDDEN:], HIDDEN // 128)
        back_ref[0:1, :] = total[:, :HIDDEN] / each
        back_ref[1:2, :] = total[:, HIDDEN:] / each

    inverse = coef_ref[1:2, :HIDDEN]
    normed = (conv_ref[...] - coef_ref[0:1, :HIDDEN]) * inverse
    value = dpre_ref[...] - back_ref[0:1, :] - normed * back_ref[1:2, :]
    scale = coef_ref[2:3, :HIDDEN] * inverse
    out_ref[...] = (wide(valid_ref[...], HIDDEN // 128) * scale * value).astype(BF)


def temporal_grad_kernel(per, dtwo_ref, first_ref, keep_ref, send_ref):
    rows = dtwo_ref.shape[0]
    half = CHANNELS // 2

    def tap(low_out, low_in, size):
        grad = dot_tn(dtwo_ref[low_out : low_out + size], first_ref[low_in : low_in + size]).astype(BF)
        keep_ref[...] = grad[:half]
        send_ref[...] = grad[half:]

    step = pl.program_id(0)
    pl.when(step == 0)(lambda: tap(per, 0, rows - per))
    pl.when(step == 1)(lambda: tap(0, 0, rows))
    pl.when(step == 2)(lambda: tap(0, per, rows - per))


def spatial_grad_kernel(tap_row, per, group, cols_ref, d_ref, keep_ref, send_ref):
    rows = d_ref.shape[0]
    half = CHANNELS // 2
    if tap_row == 1:
        grad = dot_tn(cols_ref[...], d_ref[...])
    else:
        left, right = (0, group) if tap_row == 0 else (group, 0)
        size = per - group
        cols = jnp.concatenate(
            [cols_ref[f + left : f + left + size] for f in range(0, rows, per)], axis=0
        )
        back = jnp.concatenate(
            [d_ref[f + right : f + right + size] for f in range(0, rows, per)], axis=0
        )
        grad = dot_tn(cols, back)
    grad = grad.astype(BF)
    keep_ref[...] = grad[:half]
    send_ref[...] = grad[half:]


def field_back_kernel(count, tap_col, per, group, clips, d_ref, *refs):
    piece_refs, refs = refs[: 3 * count], refs[3 * count :]
    if tap_col == 1:
        out_ref, w_ref, pad_ref = refs
    elif tap_col == 0:
        acc_in_ref, out_ref, w_ref, pad_ref = refs
    else:
        (acc_in_ref, mask_ref, dpool_ref, valid_ref, x_ref, order_ref,
         out_ref, w_ref, pad_ref, grad_ref) = refs
    step = pl.program_id(0)

    @pl.when(step == 0)
    def _():
        for a in range(3):
            at = 0
            for piece in piece_refs[a * count : (a + 1) * count]:
                rows = piece.shape[0]
                w_ref[at : at + rows, a * HIDDEN : (a + 1) * HIDDEN] = piece[...]
                at += rows
        pad_ref[:group] = jnp.zeros((group, HIDDEN), BF)
        pad_ref[group + per :] = jnp.zeros((group, HIDDEN), BF)

    pad_ref[group : group + per] = d_ref[...]
    left = jnp.concatenate(
        [pad_ref[(2 - a) * group : (2 - a) * group + per] for a in range(3)], axis=1
    )
    value = dot_nt(left, w_ref[...])
    if tap_col == 1:
        out_ref[...] = value
        return
    value = value.reshape(per // group, group, CHANNELS)
    edge = jnp.zeros((per // group, clips, CHANNELS), F32)
    if tap_col == 0:
        value = jnp.concatenate([value[:, clips:], edge], axis=1)
    else:
        value = jnp.concatenate([edge, value[:, : group - clips]], axis=1)
    value = acc_in_ref[...] + value.reshape(per, CHANNELS)
    if tap_col == 0:
        out_ref[...] = value
        return
    spread = jnp.broadcast_to(dpool_ref[...][None], (per // clips, clips, CHANNELS))
    value = value + mask_ref[...].astype(F32) * spread.reshape(per, CHANNELS)
    d_entry = (value * wide(valid_ref[...], CHANNELS // 128)).astype(BF)
    grad = dot_tn(d_entry, x_ref[...])

    @pl.when(step == 0)
    def _():
        grad_ref[...] = grad

    @pl.when(step > 0)
    def _():
        grad_ref[...] += grad

    @pl.when(step == pl.num_programs(0) - 1)
    def _():
        out_ref[...] = dot_tn(order_ref[...].astype(BF), grad_ref[...].astype(BF)).astype(BF)


def split_four(devices):
    def pairs(move):
        result = []
        for source in range(devices):
            z, x, core, y = source >> 3, (source >> 2) & 1, (source >> 1) & 1, source & 1
            z, x, core, y = move(z, x, core, y)
            result.append((source, ((z * 2 + x) * 2 + core) * 2 + y))
        return result

    along_z = [pairs(lambda z, x, c, y, k=k: ((z + k) % 4, x, c, y)) for k in range(4)]
    back_z = [pairs(lambda z, x, c, y, k=k: ((z - k) % 4, x, c, y)) for k in range(4)]
    early = pairs(lambda z, x, c, y: (z, 1 - x, c, y) if c == 0 else (z, x, c, 1 - y))
    late = pairs(lambda z, x, c, y: (z, x, c, 1 - y) if c == 0 else (z, 1 - x, c, y))
    core = pairs(lambda z, x, c, y: (z, x, 1 - c, y))
    return along_z, back_z, early, late, core


class Slice:
    def __init__(self, devices):
        self.devices = devices
        self.along_z, self.back_z, self.early, self.late, self.core = split_four(devices)

    def send(self, value, pairs):
        return lax.ppermute(value, AXES, pairs)

    def order(self, rows):
        channel = jnp.arange(CHANNELS)
        block, inside = channel // rows, channel % rows
        other, j, i, k = block >> 4, (block >> 3) & 1, (block >> 2) & 1, block & 3
        at, y = lax.axis_index("dp"), lax.axis_index("outer")
        core = (at & 1) ^ other
        x = ((at >> 1) & 1) ^ jnp.where(core == 0, i, j)
        y = y ^ jnp.where(core == 0, j, i)
        z = ((at >> 2) - k) & 3
        return (((z * 2 + x) * 2 + core) * 2 + y) * rows + inside

    def gather_z(self, shard):
        return jnp.concatenate(
            [shard] + [self.send(shard, self.along_z[k]) for k in (1, 2, 3)], axis=0
        )

    def gather(self, shard):
        column = self.gather_z(shard)
        half = jnp.concatenate([column, self.send(column, self.early)], axis=0)
        rest = self.send(half, self.late)
        return [half, rest, self.send(half, self.core), self.send(rest, self.core)]

    def add_halves(self, keep, came):
        total = keep.astype(F32) + came.astype(F32)
        half = total.shape[0] // 2
        return total[:half].astype(BF), total[half:].astype(BF)

    def scatter(self, keep, send, extra=None):
        came = self.send(send, self.core)
        if extra is not None:
            keep = jnp.concatenate([extra[0], keep], axis=1)
            came = jnp.concatenate([self.send(extra[1], self.core), came], axis=1)
        keep, send = self.add_halves(keep, came)
        keep, send = self.add_halves(keep, self.send(send, self.late))
        total = keep.astype(F32) + self.send(send, self.early).astype(F32)
        rows = total.shape[0] // 4
        result = total[:rows]
        for k in (1, 2, 3):
            part = total[k * rows : (k + 1) * rows].astype(BF)
            result = result + self.send(part, self.back_z[k]).astype(F32)
        return result


class Plain:
    def __init__(self, devices):
        self.devices = devices

    def order(self, rows):
        return jnp.arange(CHANNELS)

    def gather(self, shard):
        return [lax.all_gather(shard, AXES, axis=0, tiled=True)]

    def scatter(self, keep, send, extra=None):
        value = jnp.concatenate([keep, send], axis=0)
        if extra is not None:
            value = jnp.concatenate([jnp.concatenate(extra, axis=0), value], axis=1)
        return lax.psum_scatter(value.astype(F32), AXES, scatter_dimension=0, tiled=True)


def share_rows(row, devices):
    spread = jnp.broadcast_to(row[None], (devices,) + row.shape)
    return lax.all_to_all(spread, AXES, 0, 0)


def adamw(master, grad, first, second, rate, decay, correction):
    first_new = 0.5 * first + 0.5 * grad
    second_new = 0.5 * second + 0.5 * grad * grad
    master_new = master - rate * (
        first_new / correction / (jnp.sqrt(second_new / correction) + ADAM_EPS) + decay * master
    )
    return (master_new, first_new, second_new)


def on_device(
    links,
    clip_frames,
    valid_mask,
    labels,
    clip_keep,
    step_count,
    w_entry,
    w_spatial,
    w_temporal,
    w_head,
    small_params,
    entry_first,
    entry_second,
    spatial_first,
    spatial_second,
    temporal_first,
    temporal_second,
    head_first,
    head_second,
    small_first,
    small_second,
):
    clips, frames, height, breadth, _ = clip_frames.shape
    shard = w_spatial.shape[1]
    group = breadth * clips
    per = height * group
    rows = frames * per
    shape = jax.ShapeDtypeStruct

    def flat(taps):
        return taps.astype(BF).transpose(1, 0, 2).reshape(shard, -1)

    entry_t = w_entry.T
    temporal_t = w_temporal.transpose(0, 2, 1)
    head_pad = jnp.pad(w_head.astype(BF), ((0, 0), (0, CHANNELS - CLASSES)))
    pieces_mid = links.gather(jnp.concatenate([flat(w_spatial[3:6]), entry_t.astype(BF)], axis=1))
    pieces_top = links.gather(flat(w_spatial[0:3]))
    pieces_low = links.gather(flat(w_spatial[6:9]))
    pieces_time = links.gather(jnp.concatenate([head_pad, flat(temporal_t)], axis=1))
    count = len(pieces_mid)

    index = links.order(shard)
    order = (index[:, None] == jnp.arange(CHANNELS)[None, :]).astype(F32)
    gain_one = small_params[None, :HIDDEN]
    shift_one = small_params[None, HIDDEN : 2 * HIDDEN]
    gain_two = small_params[None, 2 * HIDDEN : 2 * HIDDEN + CHANNELS]
    shift_two = small_params[None, 2 * HIDDEN + CHANNELS : 2 * HIDDEN + 2 * CHANNELS]
    bias = jnp.pad(
        small_params[None, 2 * HIDDEN + 2 * CHANNELS :],
        ((0, 0), (0, CHANNELS - CLASSES)),
        constant_values=-1e30,
    )
    x = clip_frames.transpose(1, 2, 3, 0, 4).reshape(rows, CHAN_IN)
    valid = jnp.broadcast_to(
        valid_mask.astype(F32).transpose(1, 2, 3, 0).reshape(rows, 1), (rows, 128)
    )
    keep = jnp.broadcast_to(clip_keep.astype(F32)[:, None], (clips, 128))
    lane = jnp.arange(CHANNELS)[None, :]
    target = jnp.where(
        lane < CLASSES,
        (1.0 - SMOOTHING) * (labels[:, None] == lane).astype(F32) + SMOOTHING / CLASSES,
        0.0,
    )

    def at(width, where=lambda i: i):
        return pl.BlockSpec((per, width), lambda i: (where(i), 0))

    def piece_specs(pieces):
        return [whole(p.shape) for p in pieces]

    def now(i):
        return jnp.minimum(i, frames - 1)

    def before(i):
        return jnp.maximum(i - 1, 0)

    conv_flops = 2 * rows * 3 * CHANNELS * HIDDEN

    field, cols, conv = call(
        functools.partial(entry_kernel, count, breadth, clips),
        "entry_and_middle_taps",
        (frames,),
        [at(CHAN_IN), at(128)] + piece_specs(pieces_mid),
        [at(CHANNELS), at(3 * CHANNELS), at(HIDDEN)],
        [shape((rows, CHANNELS), F32), shape((rows, 3 * CHANNELS), BF), shape((rows, HIDDEN), F32)],
        [pltpu.VMEM((3 * CHANNELS, HIDDEN), BF), pltpu.VMEM((CHANNELS, CHAN_IN), BF)],
        flops=conv_flops,
    )(x, valid, *pieces_mid)
    conv = call(
        functools.partial(spatial_kernel, count, 0, group),
        "upper_taps",
        (frames,),
        [at(3 * CHANNELS), at(HIDDEN)] + piece_specs(pieces_top),
        at(HIDDEN),
        shape((rows, HIDDEN), F32),
        [pltpu.VMEM((3 * CHANNELS, HIDDEN), BF)],
        aliases={1: 0},
        flops=conv_flops,
    )(cols, conv, *pieces_top)
    conv, stats = call(
        functools.partial(spatial_kernel, count, 2, group),
        "lower_taps",
        (frames,),
        [at(3 * CHANNELS), at(HIDDEN)] + piece_specs(pieces_low) + [at(128), whole((clips, 128))],
        [at(HIDDEN), whole((1, 2 * HIDDEN + 256))],
        [shape((rows, HIDDEN), F32), shape((1, 2 * HIDDEN + 256), F32)],
        [pltpu.VMEM((3 * CHANNELS, HIDDEN), BF), pltpu.VMEM((8, 2 * HIDDEN + 256), F32)],
        aliases={1: 0},
        flops=conv_flops,
    )(cols, conv, *pieces_low, valid, keep)
    all_stats = share_rows(stats, links.devices)

    first, two, stats_two, coef, head = call(
        functools.partial(temporal_kernel, count, frames),
        "norm_and_temporal",
        (frames + 1,),
        [whole(all_stats.shape), at(HIDDEN, now), at(128, now), at(128, before)]
        + [whole((1, HIDDEN))] * 2
        + [whole((CHANNELS, CHANNELS))]
        + piece_specs(pieces_time),
        [
            at(HIDDEN, now),
            at(CHANNELS, before),
            whole((1, 2 * CHANNELS)),
            whole((8, HIDDEN + 128)),
            whole((CHANNELS, CHANNELS)),
        ],
        [
            shape((rows, HIDDEN), BF),
            shape((rows, CHANNELS), F32),
            shape((1, 2 * CHANNELS), F32),
            shape((8, HIDDEN + 128), F32),
            shape((CHANNELS, CHANNELS), BF),
        ],
        [
            pltpu.VMEM((CHANNELS, 3 * HIDDEN), BF),
            pltpu.VMEM((rows, HIDDEN), BF),
            pltpu.VMEM((8, 2 * CHANNELS), F32),
        ],
        flops=conv_flops,
    )(all_stats, conv, valid, valid, gain_one, shift_one, order, *pieces_time)
    all_two = share_rows(stats_two, links.devices)

    half = CHANNELS // 2
    dpool, stats_three, coef_two, head_keep, head_send = call(
        functools.partial(head_kernel, clips),
        "norm_head_and_back",
        (frames,),
        [whole(all_two.shape), at(CHANNELS), at(CHANNELS), at(128), whole((8, HIDDEN + 128))]
        + [whole((1, CHANNELS))] * 2
        + [whole((CHANNELS, CHANNELS))] * 2
        + [whole((1, CHANNELS)), whole((clips, CHANNELS)), whole((clips, 128))],
        [
            whole((clips, CHANNELS)),
            whole((1, 3 * CHANNELS)),
            whole((8, CHANNELS)),
            whole((half, CHANNELS)),
            whole((half, CHANNELS)),
        ],
        [
            shape((clips, CHANNELS), F32),
            shape((1, 3 * CHANNELS), F32),
            shape((8, CHANNELS), F32),
            shape((half, CHANNELS), BF),
            shape((half, CHANNELS), BF),
        ],
        [pltpu.VMEM((3, clips, CHANNELS), F32), pltpu.VMEM((clips, 128), F32)],
    )(all_two, two, field, valid, coef, gain_two, shift_two, order, head, bias, target, keep)
    all_three = share_rows(stats_three, links.devices)

    dtwo, mask, dpre, stats_four = call(
        functools.partial(first_back_kernel, count, frames, clips),
        "temporal_back",
        (frames + 1,),
        [
            whole(all_three.shape),
            at(CHANNELS, now),
            at(CHANNELS, now),
            at(128, now),
            whole((8, HIDDEN + 128)),
            whole((8, CHANNELS)),
            whole((clips, CHANNELS)),
            whole((CHANNELS, CHANNELS)),
            at(HIDDEN, before),
            at(128, before),
        ]
        + piece_specs(pieces_time),
        [at(CHANNELS, now), at(CHANNELS, now), at(HIDDEN, before), whole((1, 2 * HIDDEN))],
        [
            shape((rows, CHANNELS), BF),
            shape((rows, CHANNELS), BF),
            shape((rows, HIDDEN), F32),
            shape((1, 2 * HIDDEN), F32),
        ],
        [
            pltpu.VMEM((3 * CHANNELS, HIDDEN), BF),
            pltpu.VMEM((rows, CHANNELS), BF),
            pltpu.VMEM((8, CHANNELS), F32),
            pltpu.VMEM((8, 2 * HIDDEN), F32),
        ],
        flops=conv_flops,
    )(all_three, two, field, valid, coef, coef_two, dpool, order, conv, valid, *pieces_time)
    all_four = share_rows(stats_four, links.devices)

    pair = [shape((half, 3 * HIDDEN), BF)] * 2
    pair_specs = [pl.BlockSpec((half, HIDDEN), lambda i: (0, i))] * 2
    time_keep, time_send = call(
        functools.partial(temporal_grad_kernel, per),
        "temporal_gradient",
        (3,),
        [whole((rows, CHANNELS)), whole((rows, HIDDEN))],
        pair_specs,
        pair,
        flops=conv_flops,
    )(dtwo, first)
    time_share = links.scatter(time_keep, time_send, (head_keep, head_send))

    dconv = call(
        conv_back_kernel,
        "spatial_norm_back",
        (frames,),
        [whole(all_four.shape), at(HIDDEN), at(HIDDEN), at(128), whole((8, HIDDEN + 128))],
        at(HIDDEN),
        shape((rows, HIDDEN), BF),
        [pltpu.VMEM((8, HIDDEN), F32)],
    )(all_four, conv, dpre, valid, coef)

    def spatial_grad(tap_row):
        return call(
            functools.partial(spatial_grad_kernel, tap_row, per, group),
            "spatial_gradient",
            (3,),
            [pl.BlockSpec((rows, CHANNELS), lambda i: (0, i)), whole((rows, HIDDEN))],
            pair_specs,
            pair,
            flops=conv_flops,
        )(cols, dconv)

    shares = {}
    for tap_row in (1, 0, 2):
        shares[tap_row] = links.scatter(*spatial_grad(tap_row))

    def field_back(tap_col, extra, extra_specs, out_spec, out_shape, scratch=()):
        pieces = pieces_top + pieces_mid + pieces_low
        return call(
            functools.partial(field_back_kernel, count, tap_col, per, group, clips),
            "field_back",
            (frames,),
            [at(HIDDEN)]
            + [pl.BlockSpec((p.shape[0], HIDDEN), lambda i: (0, tap_col)) for p in pieces]
            + extra_specs,
            out_spec,
            out_shape,
            [
                pltpu.VMEM((CHANNELS, 3 * HIDDEN), BF),
                pltpu.VMEM((per + 2 * group, HIDDEN), BF),
                *scratch,
            ],
            flops=conv_flops,
        )(dconv, *pieces, *extra)

    partial = shape((rows, CHANNELS), F32)
    back = field_back(1, [], [], at(CHANNELS), partial)
    back = field_back(0, [back], [at(CHANNELS)], at(CHANNELS), partial)
    grad_entry = field_back(
        2,
        [back, mask, dpool, valid, x, order],
        [
            at(CHANNELS),
            at(CHANNELS),
            whole((clips, CHANNELS)),
            at(128),
            at(CHAN_IN),
            whole((CHANNELS, CHANNELS)),
        ],
        whole((CHANNELS, CHAN_IN)),
        shape((CHANNELS, CHAN_IN), BF),
        [pltpu.VMEM((CHANNELS, CHAN_IN), F32)],
    )
    entry_parts = lax.all_to_all(grad_entry.reshape(links.devices, shard, CHAN_IN), AXES, 0, 0)
    entry_share = jnp.sum(entry_parts.astype(F32), axis=0)

    def taps(share):
        return share.reshape(shard, 3, HIDDEN).transpose(1, 0, 2)

    correction = 1.0 - jnp.power(0.5, step_count[0].astype(F32))
    total_three = jnp.sum(all_three, axis=(0, 1))
    total_four = jnp.sum(all_four, axis=(0, 1))
    small_grad = jnp.concatenate(
        [
            total_four[HIDDEN:],
            total_four[:HIDDEN],
            total_three[CHANNELS : 2 * CHANNELS],
            total_three[:CHANNELS],
            total_three[2 * CHANNELS : 2 * CHANNELS + CLASSES],
        ]
    )
    loss = total_three[2 * CHANNELS + CLASSES] / coef[1, HIDDEN]
    spatial_grad_share = jnp.concatenate([taps(shares[a]) for a in range(3)], axis=0)
    temporal_share = taps(time_share[:, CHANNELS:]).transpose(0, 2, 1)
    entry_out = adamw(
        w_entry, entry_share.T, entry_first, entry_second, 0.06, DECAY_RATE, correction
    )
    spatial_out = adamw(
        w_spatial, spatial_grad_share, spatial_first, spatial_second, 0.02, DECAY_RATE, correction
    )
    temporal_out = adamw(
        w_temporal, temporal_share, temporal_first, temporal_second, 0.02, DECAY_RATE, correction
    )
    head_out = adamw(
        w_head, time_share[:, :CLASSES], head_first, head_second, 0.05, DECAY_RATE, correction
    )
    small_out = adamw(small_params, small_grad, small_first, small_second, 0.5, 0.0, correction)
    return (
        loss,
        *entry_out,
        *spatial_out,
        *temporal_out,
        *head_out,
        *small_out,
        entry_out[0].astype(BF),
        spatial_out[0].astype(BF),
        temporal_out[0].astype(BF),
        head_out[0].astype(BF),
    )


def solution(mesh):
    devices = mesh.shape["dp"] * mesh.shape["outer"]
    small_slice = mesh.shape["dp"] == 16 and mesh.shape["outer"] == 2
    links = Slice(devices) if small_slice else Plain(devices)
    both = ("dp", "outer")
    entry, spatial, temporal, head = (
        P(None, both),
        P(None, both, None),
        P(None, None, both),
        P(both, None),
    )
    placed = (
        P(both, None, None, None, None),
        P(both, None, None, None),
        P(both),
        P(both),
        P(),
        entry,
        spatial,
        temporal,
        head,
        P(),
        entry,
        entry,
        spatial,
        spatial,
        temporal,
        temporal,
        head,
        head,
        P(),
        P(),
    )
    return jax.shard_map(
        functools.partial(on_device, links),
        mesh=mesh,
        in_specs=placed,
        out_specs=(
            P(),
            *([entry] * 3),
            *([spatial] * 3),
            *([temporal] * 3),
            *([head] * 3),
            P(),
            P(),
            P(),
            entry,
            spatial,
            temporal,
            head,
        ),
        check_vma=False,
    )
```

```python
import functools

import jax
import jax.numpy as jnp
from jax import lax
from jax.experimental import pallas as pl
from jax.experimental.pallas import tpu as pltpu
from jax.sharding import PartitionSpec as P

CHANNELS = 512
HIDDEN = 1152
CLASSES = 400
CHAN_IN = 256

EPSILON = 1e-05
ADAM_EPS = 1e-08
DECAY_RATE = 0.1
SMOOTHING = 0.1

AXES = ("dp", "outer")
BF = jnp.bfloat16
F32 = jnp.float32
MIB = 1 << 20
EXACT = lax.Precision.HIGHEST


def wide(column, times):
    return jnp.concatenate([column] * times, axis=1)


def dot_nn(left, right):
    return lax.dot_general(left, right, (((1,), (0,)), ((), ())), preferred_element_type=F32)


def dot_nt(left, right):
    return lax.dot_general(left, right, (((1,), (1,)), ((), ())), preferred_element_type=F32)


def dot_tn(left, right):
    return lax.dot_general(left, right, (((0,), (0,)), ((), ())), preferred_element_type=F32)


def to_owner_order(row, order):
    return lax.dot_general(
        row, order, (((1,), (0,)), ((), ())), precision=EXACT, preferred_element_type=F32
    )


def to_local_order(row, order):
    return lax.dot_general(
        row, order, (((1,), (1,)), ((), ())), precision=EXACT, preferred_element_type=F32
    )


def fold(value, step):
    return jnp.sum(value.reshape(value.shape[0] // step, step, value.shape[1]), axis=0)


def whole(shape):
    return pl.BlockSpec(shape, lambda *_: (0,) * len(shape))


def call(
    kernel, name, grid, in_specs, out_specs, out_shape, scratch=(), aliases=None, vmem=40, flops=0,
    gates=(),
):
    first, last = len(in_specs), len(in_specs) + len(gates)

    def gated(*refs):
        kernel(*refs[:first], *refs[last:])

    run = pl.pallas_call(
        gated,
        name=name,
        grid=grid,
        in_specs=list(in_specs) + [pl.BlockSpec(memory_space=pl.ANY)] * len(gates),
        out_specs=out_specs,
        out_shape=out_shape,
        scratch_shapes=list(scratch),
        input_output_aliases=aliases or {},
        compiler_params=pltpu.CompilerParams(vmem_limit_bytes=vmem * MIB),
        cost_estimate=pl.CostEstimate(flops=flops, bytes_accessed=20 * MIB, transcendentals=0),
    )
    return lambda *operands: run(*operands, *gates)


def entry_kernel(count, side, clips, x_ref, valid_ref, *refs):
    pieces, (field_ref, cols_ref, conv_ref, w_ref, e_ref) = refs[:count], refs[count:]

    @pl.when(pl.program_id(0) == 0)
    def _():
        at = 0
        for piece in pieces:
            rows = piece.shape[0]
            for b in range(3):
                w_ref[b * CHANNELS + at : b * CHANNELS + at + rows, :] = piece[
                    :, b * HIDDEN : (b + 1) * HIDDEN
                ]
            e_ref[at : at + rows, :] = piece[:, 3 * HIDDEN :]
            at += rows

    value = dot_nt(x_ref[...], e_ref[...]) * wide(valid_ref[...], CHANNELS // 128)
    field_ref[...] = value
    rows = value.shape[0]
    group = side * clips
    grid3 = value.reshape(rows // group, group, CHANNELS)
    edge = jnp.zeros((rows // group, clips, CHANNELS), F32)
    left = jnp.concatenate([edge, grid3[:, : group - clips]], axis=1).reshape(rows, CHANNELS)
    right = jnp.concatenate([grid3[:, clips:], edge], axis=1).reshape(rows, CHANNELS)
    cols_ref[:, :CHANNELS] = left.astype(BF)
    cols_ref[:, CHANNELS : 2 * CHANNELS] = value.astype(BF)
    cols_ref[:, 2 * CHANNELS :] = right.astype(BF)
    conv_ref[...] = dot_nn(cols_ref[...], w_ref[...])


def spatial_kernel(count, tap_row, group, cols_ref, conv_ref, *refs):
    pieces, refs = refs[:count], refs[count:]
    step = pl.program_id(0)
    if tap_row == 0:
        out_ref, w_ref = refs
    else:
        valid_ref, keep_ref, out_ref, stats_ref, w_ref, acc_ref = refs

    @pl.when(step == 0)
    def _():
        at = 0
        for piece in pieces:
            rows = piece.shape[0]
            for b in range(3):
                w_ref[b * CHANNELS + at : b * CHANNELS + at + rows, :] = piece[
                    :, b * HIDDEN : (b + 1) * HIDDEN
                ]
            at += rows

    rows = cols_ref.shape[0]
    if tap_row == 0:
        out_ref[:group] = conv_ref[:group]
        out_ref[group:] = conv_ref[group:] + dot_nn(cols_ref[: rows - group], w_ref[...])
        return
    out_ref[rows - group :] = conv_ref[rows - group :]
    out_ref[: rows - group] = conv_ref[: rows - group] + dot_nn(cols_ref[group:], w_ref[...])

    @pl.when(step == 0)
    def _():
        acc_ref[...] = jnp.zeros_like(acc_ref)

    value = out_ref[...]
    kept = value * wide(valid_ref[...], HIDDEN // 128)
    acc_ref[:, :HIDDEN] += fold(kept, 8)
    acc_ref[:, HIDDEN : 2 * HIDDEN] += fold(kept * value, 8)
    acc_ref[:, 2 * HIDDEN : 2 * HIDDEN + 128] += fold(valid_ref[...], 8)

    @pl.when(step == pl.num_programs(0) - 1)
    def _():
        acc_ref[:, 2 * HIDDEN + 128 :] = fold(keep_ref[...], 8)
        stats_ref[...] = jnp.sum(acc_ref[...], axis=0, keepdims=True)


def temporal_kernel(
    count, frames, recv_ref, conv_ref, valid_ref, valid_out_ref, gain_ref, shift_ref, order_ref, *refs
):
    pieces, refs = refs[:count], refs[count:]
    first_ref, two_ref, stats_ref, coef_ref, head_ref, w_ref, first_all, acc_ref = refs
    step = pl.program_id(0)
    per = conv_ref.shape[0]

    @pl.when(step == 0)
    def _():
        at = 0
        for piece in pieces:
            rows = piece.shape[0]
            head_ref[at : at + rows, :] = piece[:, :CHANNELS]
            w_ref[at : at + rows, :] = piece[:, CHANNELS:]
            at += rows
        total = jnp.sum(recv_ref[...], axis=0)
        count_all = total[:, 2 * HIDDEN : 2 * HIDDEN + 128]
        wide_count = wide(count_all, HIDDEN // 128)
        mean = total[:, :HIDDEN] / wide_count
        variance = total[:, HIDDEN : 2 * HIDDEN] / wide_count - mean * mean
        coef_ref[...] = jnp.zeros_like(coef_ref)
        coef_ref[0:1, :HIDDEN] = mean
        coef_ref[1:2, :HIDDEN] = lax.rsqrt(variance + EPSILON)
        coef_ref[2:3, :HIDDEN] = gain_ref[...]
        coef_ref[3:4, :HIDDEN] = shift_ref[...]
        coef_ref[0:1, HIDDEN:] = count_all
        coef_ref[1:2, HIDDEN:] = total[:, 2 * HIDDEN + 128 :]
        acc_ref[...] = jnp.zeros_like(acc_ref)

    @pl.when(step < frames)
    def _():
        normed = (conv_ref[...] - coef_ref[0:1, :HIDDEN]) * coef_ref[1:2, :HIDDEN]
        pre = coef_ref[2:3, :HIDDEN] * normed + coef_ref[3:4, :HIDDEN]
        first = (jnp.maximum(pre, 0.0) * wide(valid_ref[...], HIDDEN // 128)).astype(BF)
        first_ref[...] = first
        first_all[pl.ds(pl.multiple_of(step * per, per), per), :] = first

    def frame(start, taps):
        pieces_at = [
            first_all[pl.ds(pl.multiple_of(start + k * per, per), per), :] for k in range(len(taps))
        ]
        lanes = slice(taps[0] * HIDDEN, (taps[-1] + 1) * HIDDEN)
        value = dot_nt(jnp.concatenate(pieces_at, axis=1), w_ref[:, lanes])
        two_ref[...] = value
        kept = value * wide(valid_out_ref[...], CHANNELS // 128)
        acc_ref[:, :CHANNELS] += fold(kept, 8)
        acc_ref[:, CHANNELS:] += fold(kept * value, 8)

    @pl.when(step == 1)
    def _():
        frame(0, (1, 2))

    @pl.when(jnp.logical_and(step > 1, step < frames))
    def _():
        frame((step - 2) * per, (0, 1, 2))

    @pl.when(step == frames)
    def _():
        frame((frames - 2) * per, (0, 1))
        sums = jnp.sum(acc_ref[...], axis=0, keepdims=True)
        stats_ref[:, :CHANNELS] = to_owner_order(sums[:, :CHANNELS], order_ref[...])
        stats_ref[:, CHANNELS:] = to_owner_order(sums[:, CHANNELS:], order_ref[...])


def head_kernel(
    clips, recv_ref, two_ref, field_ref, valid_ref, coef_ref, gain_ref, shift_ref, order_ref,
    head_ref, bias_ref, target_ref, keep_ref,
    dpool_ref, stats_ref, coef_two_ref, keep_grad_ref, send_grad_ref, acc_ref, size_ref,
):
    step = pl.program_id(0)

    @pl.when(step == 0)
    def _():
        total = jnp.sum(recv_ref[...], axis=0)
        count = wide(coef_ref[0:1, HIDDEN:], CHANNELS // 128)
        mean = to_local_order(total[:, :CHANNELS], order_ref[...]) / count
        square = to_local_order(total[:, CHANNELS:], order_ref[...]) / count
        coef_two_ref[...] = jnp.zeros_like(coef_two_ref)
        coef_two_ref[0:1, :] = mean
        coef_two_ref[1:2, :] = lax.rsqrt(square - mean * mean + EPSILON)
        coef_two_ref[2:3, :] = to_local_order(gain_ref[...], order_ref[...])
        coef_two_ref[3:4, :] = to_local_order(shift_ref[...], order_ref[...])
        acc_ref[...] = jnp.zeros_like(acc_ref)
        size_ref[...] = jnp.zeros_like(size_ref)

    valid = wide(valid_ref[...], CHANNELS // 128)
    normed = (two_ref[...] - coef_two_ref[0:1, :]) * coef_two_ref[1:2, :]
    pre = coef_two_ref[2:3, :] * normed + coef_two_ref[3:4, :] + field_ref[...]
    mask = jnp.where(pre > 0.0, valid, 0.0)
    acc_ref[0] += fold(jnp.maximum(pre, 0.0) * valid, clips)
    acc_ref[1] += fold(mask, clips)
    acc_ref[2] += fold(mask * normed, clips)
    size_ref[...] += fold(valid_ref[...], clips)

    @pl.when(step == pl.num_programs(0) - 1)
    def _():
        size = wide(size_ref[...], CHANNELS // 128)
        pooled_low = (acc_ref[0] / size).astype(BF)
        head = head_ref[...]
        logits = dot_nn(pooled_low, head) + bias_ref[...]
        shifted = logits - jnp.max(logits, axis=1, keepdims=True)
        log_prob = shifted - jnp.log(jnp.sum(jnp.exp(shifted), axis=1, keepdims=True))
        target = target_ref[...]
        per_clip = -jnp.sum(target * log_prob, axis=1, keepdims=True)
        keep = wide(keep_ref[...], CHANNELS // 128)
        loss = jnp.sum(keep * per_clip, axis=0, keepdims=True)
        kept = wide(coef_ref[1:2, HIDDEN:], CHANNELS // 128)
        d_logits = keep * (jnp.exp(log_prob) - target) / kept
        d_low = d_logits.astype(BF)
        grad = dot_tn(pooled_low.astype(F32), d_low.astype(F32)).astype(BF)
        half = grad.shape[0] // 2
        keep_grad_ref[...] = grad[:half]
        send_grad_ref[...] = grad[half:]
        d_pooled = dot_nt(d_low, head) / size
        dpool_ref[...] = d_pooled
        sums_one = jnp.sum(acc_ref[1] * d_pooled, axis=0, keepdims=True)
        sums_two = jnp.sum(acc_ref[2] * d_pooled, axis=0, keepdims=True)
        stats_ref[:, :CHANNELS] = to_owner_order(sums_one, order_ref[...])
        stats_ref[:, CHANNELS : 2 * CHANNELS] = to_owner_order(sums_two, order_ref[...])
        lane = lax.broadcasted_iota(jnp.int32, (1, CHANNELS), 1)
        stats_ref[:, 2 * CHANNELS :] = jnp.where(
            lane < CLASSES, jnp.sum(d_logits, axis=0, keepdims=True), loss
        )


def first_back_kernel(
    count, frames, clips, recv_ref, two_ref, field_ref, valid_ref, coef_ref, coef_two_ref, dpool_ref,
    order_ref, conv_ref, valid_out_ref, *refs
):
    pieces, refs = refs[:count], refs[count:]
    dtwo_ref, mask_ref, dpre_ref, stats_ref, w_ref, dtwo_all, back_ref, acc_ref = refs
    step = pl.program_id(0)
    per = conv_ref.shape[0]

    @pl.when(step == 0)
    def _():
        at = 0
        for piece in pieces:
            rows = piece.shape[0]
            for t in range(3):
                w_ref[t * CHANNELS + at : t * CHANNELS + at + rows, :] = piece[
                    :, CHANNELS + t * HIDDEN : CHANNELS + (t + 1) * HIDDEN
                ]
            at += rows
        total = jnp.sum(recv_ref[...], axis=0)
        each = wide(coef_ref[0:1, HIDDEN:], CHANNELS // 128)
        back_ref[0:1, :] = to_local_order(total[:, :CHANNELS], order_ref[...]) / each
        back_ref[1:2, :] = to_local_order(total[:, CHANNELS : 2 * CHANNELS], order_ref[...]) / each
        acc_ref[...] = jnp.zeros_like(acc_ref)

    @pl.when(step < frames)
    def _():
        valid = wide(valid_ref[...], CHANNELS // 128)
        gain = coef_two_ref[2:3, :]
        inverse = coef_two_ref[1:2, :]
        normed = (two_ref[...] - coef_two_ref[0:1, :]) * inverse
        pre = gain * normed + coef_two_ref[3:4, :] + field_ref[...]
        mask = jnp.where(pre > 0.0, valid, 0.0)
        spread = jnp.broadcast_to(dpool_ref[...][None], (per // clips, clips, CHANNELS))
        d_pre = mask * spread.reshape(per, CHANNELS)
        low = (
            valid * (gain * inverse) * (d_pre - back_ref[0:1, :] - normed * back_ref[1:2, :])
        ).astype(BF)
        mask_ref[...] = mask.astype(BF)
        dtwo_ref[...] = low
        dtwo_all[pl.ds(pl.multiple_of(step * per, per), per), :] = low

    def frame(last, taps):
        pieces_at = [
            dtwo_all[pl.ds(pl.multiple_of(last - k * per, per), per), :] for k in range(len(taps))
        ]
        d_first = dot_nn(
            jnp.concatenate(pieces_at, axis=1),
            w_ref[taps[0] * CHANNELS : (taps[-1] + 1) * CHANNELS, :],
        )
        normed = (conv_ref[...] - coef_ref[0:1, :HIDDEN]) * coef_ref[1:2, :HIDDEN]
        pre = coef_ref[2:3, :HIDDEN] * normed + coef_ref[3:4, :HIDDEN]
        d_pre = jnp.where(pre > 0.0, d_first, 0.0) * wide(valid_out_ref[...], HIDDEN // 128)
        dpre_ref[...] = d_pre
        acc_ref[:, :HIDDEN] += fold(d_pre, 8)
        acc_ref[:, HIDDEN:] += fold(d_pre * normed, 8)

    @pl.when(step == 1)
    def _():
        frame(per, (0, 1))

    @pl.when(jnp.logical_and(step > 1, step < frames))
    def _():
        frame(step * per, (0, 1, 2))

    @pl.when(step == frames)
    def _():
        frame((frames - 1) * per, (1, 2))
        stats_ref[...] = jnp.sum(acc_ref[...], axis=0, keepdims=True)


def conv_back_kernel(recv_ref, conv_ref, dpre_ref, valid_ref, coef_ref, out_ref, back_ref):
    @pl.when(pl.program_id(0) == 0)
    def _():
        total = jnp.sum(recv_ref[...], axis=0)
        each = wide(coef_ref[0:1, HIDDEN:], HIDDEN // 128)
        back_ref[0:1, :] = total[:, :HIDDEN] / each
        back_ref[1:2, :] = total[:, HIDDEN:] / each

    inverse = coef_ref[1:2, :HIDDEN]
    normed = (conv_ref[...] - coef_ref[0:1, :HIDDEN]) * inverse
    value = dpre_ref[...] - back_ref[0:1, :] - normed * back_ref[1:2, :]
    scale = coef_ref[2:3, :HIDDEN] * inverse
    out_ref[...] = (wide(valid_ref[...], HIDDEN // 128) * scale * value).astype(BF)


def temporal_grad_kernel(per, dtwo_ref, first_ref, keep_ref, send_ref):
    rows = dtwo_ref.shape[0]
    half = CHANNELS // 2

    def tap(low_out, low_in, size):
        grad = dot_tn(dtwo_ref[low_out : low_out + size], first_ref[low_in : low_in + size]).astype(BF)
        keep_ref[...] = grad[:half]
        send_ref[...] = grad[half:]

    step = pl.program_id(0)
    pl.when(step == 0)(lambda: tap(per, 0, rows - per))
    pl.when(step == 1)(lambda: tap(0, 0, rows))
    pl.when(step == 2)(lambda: tap(0, per, rows - per))


def spatial_grad_kernel(tap_row, per, group, cols_ref, d_ref, keep_ref, send_ref):
    rows = d_ref.shape[0]
    half = CHANNELS // 2
    if tap_row == 1:
        grad = dot_tn(cols_ref[...], d_ref[...])
    else:
        left, right = (0, group) if tap_row == 0 else (group, 0)
        size = per - group
        cols = jnp.concatenate(
            [cols_ref[f + left : f + left + size] for f in range(0, rows, per)], axis=0
        )
        back = jnp.concatenate(
            [d_ref[f + right : f + right + size] for f in range(0, rows, per)], axis=0
        )
        grad = dot_tn(cols, back)
    grad = grad.astype(BF)
    keep_ref[...] = grad[:half]
    send_ref[...] = grad[half:]


def field_back_kernel(count, tap_col, per, group, clips, d_ref, *refs):
    piece_refs, refs = refs[: 3 * count], refs[3 * count :]
    if tap_col == 1:
        out_ref, w_ref, pad_ref = refs
    elif tap_col == 0:
        acc_in_ref, out_ref, w_ref, pad_ref = refs
    else:
        (acc_in_ref, mask_ref, dpool_ref, valid_ref, x_ref, order_ref,
         out_ref, w_ref, pad_ref, grad_ref) = refs
    step = pl.program_id(0)

    @pl.when(step == 0)
    def _():
        for a in range(3):
            at = 0
            for piece in piece_refs[a * count : (a + 1) * count]:
                rows = piece.shape[0]
                w_ref[at : at + rows, a * HIDDEN : (a + 1) * HIDDEN] = piece[...]
                at += rows
        pad_ref[:group] = jnp.zeros((group, HIDDEN), BF)
        pad_ref[group + per :] = jnp.zeros((group, HIDDEN), BF)

    pad_ref[group : group + per] = d_ref[...]
    left = jnp.concatenate(
        [pad_ref[(2 - a) * group : (2 - a) * group + per] for a in range(3)], axis=1
    )
    value = dot_nt(left, w_ref[...])
    if tap_col == 1:
        out_ref[...] = value
        return
    value = value.reshape(per // group, group, CHANNELS)
    edge = jnp.zeros((per // group, clips, CHANNELS), F32)
    if tap_col == 0:
        value = jnp.concatenate([value[:, clips:], edge], axis=1)
    else:
        value = jnp.concatenate([edge, value[:, : group - clips]], axis=1)
    value = acc_in_ref[...] + value.reshape(per, CHANNELS)
    if tap_col == 0:
        out_ref[...] = value
        return
    spread = jnp.broadcast_to(dpool_ref[...][None], (per // clips, clips, CHANNELS))
    value = value + mask_ref[...].astype(F32) * spread.reshape(per, CHANNELS)
    d_entry = (value * wide(valid_ref[...], CHANNELS // 128)).astype(BF)
    grad = dot_tn(d_entry, x_ref[...])

    @pl.when(step == 0)
    def _():
        grad_ref[...] = grad

    @pl.when(step > 0)
    def _():
        grad_ref[...] += grad

    @pl.when(step == pl.num_programs(0) - 1)
    def _():
        out_ref[...] = dot_tn(order_ref[...].astype(BF), grad_ref[...].astype(BF)).astype(BF)


def wait_for(value, others):
    return lax.optimization_barrier((value, *others))[0]


def split_four(devices):
    def pairs(move):
        result = []
        for source in range(devices):
            z, x, core, y = source >> 3, (source >> 2) & 1, (source >> 1) & 1, source & 1
            z, x, core, y = move(z, x, core, y)
            result.append((source, ((z * 2 + x) * 2 + core) * 2 + y))
        return result

    along_z = [pairs(lambda z, x, c, y, k=k: ((z + k) % 4, x, c, y)) for k in range(4)]
    back_z = [pairs(lambda z, x, c, y, k=k: ((z - k) % 4, x, c, y)) for k in range(4)]
    early = pairs(lambda z, x, c, y: (z, 1 - x, c, y) if c == 0 else (z, x, c, 1 - y))
    late = pairs(lambda z, x, c, y: (z, x, c, 1 - y) if c == 0 else (z, 1 - x, c, y))
    core = pairs(lambda z, x, c, y: (z, x, 1 - c, y))
    return along_z, back_z, early, late, core


class Slice:
    def __init__(self, devices):
        self.devices = devices
        self.along_z, self.back_z, self.early, self.late, self.core = split_four(devices)

    def send(self, value, pairs):
        return lax.ppermute(value, AXES, pairs)

    def order(self, rows):
        channel = jnp.arange(CHANNELS)
        block, inside = channel // rows, channel % rows
        other, j, i, k = block >> 4, (block >> 3) & 1, (block >> 2) & 1, block & 3
        at, y = lax.axis_index("dp"), lax.axis_index("outer")
        core = (at & 1) ^ other
        x = ((at >> 1) & 1) ^ jnp.where(core == 0, i, j)
        y = y ^ jnp.where(core == 0, j, i)
        z = ((at >> 2) - k) & 3
        return (((z * 2 + x) * 2 + core) * 2 + y) * rows + inside

    def gather(self, shard, after=()):
        shard = wait_for(shard, after)
        came = [self.send(shard, self.along_z[k]) for k in (1, 2, 3)]
        after = yield
        column = jnp.concatenate([shard] + [wait_for(part, after) for part in came], axis=0)
        came = self.send(column, self.early)
        after = yield [column]
        half = jnp.concatenate([column, wait_for(came, after)], axis=0)
        rest = self.send(half, self.late)
        other = self.send(half, self.core)
        after = yield [half, other]
        rest = wait_for(rest, after)
        yield [half, rest, other, self.send(rest, self.core)]

    def add_halves(self, keep, came):
        half = keep.shape[0] // 2
        kept = keep[:half].astype(F32) + came[:half].astype(F32)
        sent = keep[half:].astype(F32) + came[half:].astype(F32)
        return kept.astype(BF), sent.astype(BF)

    def scatter(self, keep, send, extra=None):
        came = self.send(send, self.core)
        if extra is not None:
            came = jnp.concatenate([self.send(extra[1], self.core), came], axis=1)
        after = yield
        if extra is not None:
            keep = jnp.concatenate([extra[0], keep], axis=1)
        keep, send = self.add_halves(keep, wait_for(came, after))
        came = self.send(send, self.late)
        after = yield [keep, send]
        keep, send = self.add_halves(keep, wait_for(came, after))
        came = self.send(send, self.early)
        after = yield [keep, send]
        total = keep.astype(F32) + wait_for(came, after).astype(F32)
        rows = total.shape[0] // 4
        result = total[:rows]
        parts = [total[k * rows : (k + 1) * rows].astype(BF) for k in (1, 2, 3)]
        came = [self.send(part, pairs) for part, pairs in zip(parts, self.back_z[1:], strict=True)]
        after = yield [result, *parts]
        for part in came:
            result = result + wait_for(part, after).astype(F32)
        yield [result]


class Plain:
    def __init__(self, devices):
        self.devices = devices

    def order(self, rows):
        return jnp.arange(CHANNELS)

    def gather(self, shard, after=()):
        result = [lax.all_gather(shard, AXES, axis=0, tiled=True)]
        yield
        yield result
        yield [*result, *result]
        yield result

    def scatter(self, keep, send, extra=None):
        value = jnp.concatenate([keep, send], axis=0)
        if extra is not None:
            value = jnp.concatenate([jnp.concatenate(extra, axis=0), value], axis=1)
        result = [lax.psum_scatter(value.astype(F32), AXES, scatter_dimension=0, tiled=True)]
        while True:
            yield result


def spread_row(row, devices):
    return jnp.broadcast_to(row[None], (devices,) + row.shape)


def share_rows(row, devices):
    return lax.all_to_all(spread_row(row, devices), AXES, 0, 0)


def adamw(master, grad, first, second, rate, decay, correction):
    first_new = 0.5 * first + 0.5 * grad
    second_new = 0.5 * second + 0.5 * grad * grad
    master_new = master - rate * (
        first_new / correction / (jnp.sqrt(second_new / correction) + ADAM_EPS) + decay * master
    )
    return (master_new, first_new, second_new)


def on_device(
    links,
    clip_frames,
    valid_mask,
    labels,
    clip_keep,
    step_count,
    w_entry,
    w_spatial,
    w_temporal,
    w_head,
    small_params,
    entry_first,
    entry_second,
    spatial_first,
    spatial_second,
    temporal_first,
    temporal_second,
    head_first,
    head_second,
    small_first,
    small_second,
):
    clips, frames, height, breadth, _ = clip_frames.shape
    shard = w_spatial.shape[1]
    group = breadth * clips
    per = height * group
    rows = frames * per
    shape = jax.ShapeDtypeStruct

    def flat(taps):
        return taps.astype(BF).transpose(1, 0, 2).reshape(shard, -1)

    entry_t = w_entry.T
    temporal_t = w_temporal.transpose(0, 2, 1)
    head_pad = jnp.pad(w_head.astype(BF), ((0, 0), (0, CHANNELS - CLASSES)))
    load_mid = links.gather(jnp.concatenate([flat(w_spatial[3:6]), entry_t.astype(BF)], axis=1))
    next(load_mid)
    column_mid = load_mid.send([])
    load_top = links.gather(flat(w_spatial[0:3]), column_mid)
    next(load_top)
    half_mid, other_mid = load_mid.send([])
    column_top = load_top.send([half_mid])
    load_low = links.gather(flat(w_spatial[6:9]), [*column_top, other_mid])
    next(load_low)
    column_low = load_low.send([])
    head_time = jnp.concatenate([head_pad, flat(temporal_t)], axis=1)
    load_time = links.gather(head_time, column_low)
    next(load_time)
    ready = load_top.send(column_low)
    pieces_mid = load_mid.send([])
    count = len(pieces_mid)

    index = links.order(shard)
    order = (index[:, None] == jnp.arange(CHANNELS)[None, :]).astype(F32)
    gain_one = small_params[None, :HIDDEN]
    shift_one = small_params[None, HIDDEN : 2 * HIDDEN]
    gain_two = small_params[None, 2 * HIDDEN : 2 * HIDDEN + CHANNELS]
    shift_two = small_params[None, 2 * HIDDEN + CHANNELS : 2 * HIDDEN + 2 * CHANNELS]
    bias = jnp.pad(
        small_params[None, 2 * HIDDEN + 2 * CHANNELS :],
        ((0, 0), (0, CHANNELS - CLASSES)),
        constant_values=-1e30,
    )
    x = clip_frames.transpose(1, 2, 3, 0, 4).reshape(rows, CHAN_IN)
    valid = jnp.broadcast_to(
        valid_mask.astype(F32).transpose(1, 2, 3, 0).reshape(rows, 1), (rows, 128)
    )
    keep = jnp.broadcast_to(clip_keep.astype(F32)[:, None], (clips, 128))
    lane = jnp.arange(CHANNELS)[None, :]
    target = jnp.where(
        lane < CLASSES,
        (1.0 - SMOOTHING) * (labels[:, None] == lane).astype(F32) + SMOOTHING / CLASSES,
        0.0,
    )

    def at(width, where=lambda i: i):
        return pl.BlockSpec((per, width), lambda i: (where(i), 0))

    def piece_specs(pieces):
        return [whole(p.shape) for p in pieces]

    def now(i):
        return jnp.minimum(i, frames - 1)

    def before(i):
        return jnp.maximum(i - 1, 0)

    conv_flops = 2 * rows * 3 * CHANNELS * HIDDEN

    field, cols, conv = call(
        functools.partial(entry_kernel, count, breadth, clips),
        "entry_and_middle_taps",
        (frames,),
        [at(CHAN_IN), at(128)] + piece_specs(pieces_mid),
        [at(CHANNELS), at(3 * CHANNELS), at(HIDDEN)],
        [shape((rows, CHANNELS), F32), shape((rows, 3 * CHANNELS), BF), shape((rows, HIDDEN), F32)],
        [pltpu.VMEM((3 * CHANNELS, HIDDEN), BF), pltpu.VMEM((CHANNELS, CHAN_IN), BF)],
        flops=conv_flops,
        gates=[ready[0], *column_low],
    )(x, valid, *pieces_mid)
    ready = load_low.send([conv])
    pieces_top = load_top.send([conv])
    column_time = load_time.send([conv])
    conv = call(
        functools.partial(spatial_kernel, count, 0, group),
        "upper_taps",
        (frames,),
        [at(3 * CHANNELS), at(HIDDEN)] + piece_specs(pieces_top),
        at(HIDDEN),
        shape((rows, HIDDEN), F32),
        [pltpu.VMEM((3 * CHANNELS, HIDDEN), BF)],
        aliases={1: 0},
        flops=conv_flops,
        gates=[ready[0], *column_time],
    )(cols, conv, *pieces_top)
    pieces_low = load_low.send([conv])
    ready = load_time.send([conv])
    conv, stats = call(
        functools.partial(spatial_kernel, count, 2, group),
        "lower_taps",
        (frames,),
        [at(3 * CHANNELS), at(HIDDEN)] + piece_specs(pieces_low) + [at(128), whole((clips, 128))],
        [at(HIDDEN), whole((1, 2 * HIDDEN + 256))],
        [shape((rows, HIDDEN), F32), shape((1, 2 * HIDDEN + 256), F32)],
        [pltpu.VMEM((3 * CHANNELS, HIDDEN), BF), pltpu.VMEM((8, 2 * HIDDEN + 256), F32)],
        aliases={1: 0},
        flops=conv_flops,
        gates=ready[:1],
    )(cols, conv, *pieces_low, valid, keep)
    pieces_time = load_time.send([conv])
    all_stats = share_rows(stats, links.devices)

    first, two, stats_two, coef, head = call(
        functools.partial(temporal_kernel, count, frames),
        "norm_and_temporal",
        (frames + 1,),
        [whole(all_stats.shape), at(HIDDEN, now), at(128, now), at(128, before)]
        + [whole((1, HIDDEN))] * 2
        + [whole((CHANNELS, CHANNELS))]
        + piece_specs(pieces_time),
        [
            at(HIDDEN, now),
            at(CHANNELS, before),
            whole((1, 2 * CHANNELS)),
            whole((8, HIDDEN + 128)),
            whole((CHANNELS, CHANNELS)),
        ],
        [
            shape((rows, HIDDEN), BF),
            shape((rows, CHANNELS), F32),
            shape((1, 2 * CHANNELS), F32),
            shape((8, HIDDEN + 128), F32),
            shape((CHANNELS, CHANNELS), BF),
        ],
        [
            pltpu.VMEM((CHANNELS, 3 * HIDDEN), BF),
            pltpu.VMEM((rows, HIDDEN), BF),
            pltpu.VMEM((8, 2 * CHANNELS), F32),
        ],
        flops=conv_flops,
    )(all_stats, conv, valid, valid, gain_one, shift_one, order, *pieces_time)
    all_two = share_rows(stats_two, links.devices)

    half = CHANNELS // 2
    dpool, stats_three, coef_two, head_keep, head_send = call(
        functools.partial(head_kernel, clips),
        "norm_head_and_back",
        (frames,),
        [whole(all_two.shape), at(CHANNELS), at(CHANNELS), at(128), whole((8, HIDDEN + 128))]
        + [whole((1, CHANNELS))] * 2
        + [whole((CHANNELS, CHANNELS))] * 2
        + [whole((1, CHANNELS)), whole((clips, CHANNELS)), whole((clips, 128))],
        [
            whole((clips, CHANNELS)),
            whole((1, 3 * CHANNELS)),
            whole((8, CHANNELS)),
            whole((half, CHANNELS)),
            whole((half, CHANNELS)),
        ],
        [
            shape((clips, CHANNELS), F32),
            shape((1, 3 * CHANNELS), F32),
            shape((8, CHANNELS), F32),
            shape((half, CHANNELS), BF),
            shape((half, CHANNELS), BF),
        ],
        [pltpu.VMEM((3, clips, CHANNELS), F32), pltpu.VMEM((clips, 128), F32)],
    )(all_two, two, field, valid, coef, gain_two, shift_two, order, head, bias, target, keep)
    all_three = share_rows(stats_three, links.devices)

    dtwo, mask, dpre, stats_four = call(
        functools.partial(first_back_kernel, count, frames, clips),
        "temporal_back",
        (frames + 1,),
        [
            whole(all_three.shape),
            at(CHANNELS, now),
            at(CHANNELS, now),
            at(128, now),
            whole((8, HIDDEN + 128)),
            whole((8, CHANNELS)),
            whole((clips, CHANNELS)),
            whole((CHANNELS, CHANNELS)),
            at(HIDDEN, before),
            at(128, before),
        ]
        + piece_specs(pieces_time),
        [at(CHANNELS, now), at(CHANNELS, now), at(HIDDEN, before), whole((1, 2 * HIDDEN))],
        [
            shape((rows, CHANNELS), BF),
            shape((rows, CHANNELS), BF),
            shape((rows, HIDDEN), F32),
            shape((1, 2 * HIDDEN), F32),
        ],
        [
            pltpu.VMEM((3 * CHANNELS, HIDDEN), BF),
            pltpu.VMEM((rows, CHANNELS), BF),
            pltpu.VMEM((8, CHANNELS), F32),
            pltpu.VMEM((8, 2 * HIDDEN), F32),
        ],
        flops=conv_flops,
    )(all_three, two, field, valid, coef, coef_two, dpool, order, conv, valid, *pieces_time)
    spread_four = spread_row(stats_four, links.devices)
    all_four = lax.all_to_all(spread_four, AXES, 0, 0)

    pair = [shape((half, 3 * HIDDEN), BF)] * 2
    pair_specs = [pl.BlockSpec((half, HIDDEN), lambda i: (0, i))] * 2
    time_pair = call(
        functools.partial(temporal_grad_kernel, per),
        "temporal_gradient",
        (3,),
        [whole((rows, CHANNELS)), whole((rows, HIDDEN))],
        pair_specs,
        pair,
        flops=conv_flops,
        gates=[spread_four],
    )(dtwo, first)

    dconv = call(
        conv_back_kernel,
        "spatial_norm_back",
        (frames,),
        [whole(all_four.shape), at(HIDDEN), at(HIDDEN), at(128), whole((8, HIDDEN + 128))],
        at(HIDDEN),
        shape((rows, HIDDEN), BF),
        [pltpu.VMEM((8, HIDDEN), F32)],
        gates=time_pair,
    )(all_four, conv, dpre, valid, coef)

    def spatial_grad(tap_row, gates):
        return call(
            functools.partial(spatial_grad_kernel, tap_row, per, group),
            "spatial_gradient",
            (3,),
            [pl.BlockSpec((rows, CHANNELS), lambda i: (0, i)), whole((rows, HIDDEN))],
            pair_specs,
            pair,
            flops=conv_flops,
            gates=gates,
        )(cols, dconv)

    scatter_time = links.scatter(*time_pair, (head_keep, head_send))
    next(scatter_time)
    ready = scatter_time.send([dconv])
    mid_pair = spatial_grad(1, ready)
    scatter_mid = links.scatter(*mid_pair)
    next(scatter_mid)
    ready = scatter_time.send(mid_pair)
    top_pair = spatial_grad(0, ready)
    scatter_top = links.scatter(*top_pair)
    next(scatter_top)
    ready = scatter_time.send(top_pair) + scatter_mid.send(top_pair)
    low_pair = spatial_grad(2, ready)
    scatter_low = links.scatter(*low_pair)
    next(scatter_low)

    def field_back(tap_col, gates, extra, extra_specs, out_spec, out_shape, scratch=()):
        pieces = pieces_top + pieces_mid + pieces_low
        return call(
            functools.partial(field_back_kernel, count, tap_col, per, group, clips),
            "field_back",
            (frames,),
            [at(HIDDEN)]
            + [pl.BlockSpec((p.shape[0], HIDDEN), lambda i: (0, tap_col)) for p in pieces]
            + extra_specs,
            out_spec,
            out_shape,
            [
                pltpu.VMEM((CHANNELS, 3 * HIDDEN), BF),
                pltpu.VMEM((per + 2 * group, HIDDEN), BF),
                *scratch,
            ],
            flops=conv_flops,
            gates=gates,
        )(dconv, *pieces, *extra)

    partial = shape((rows, CHANNELS), F32)
    time_share = scatter_time.send(low_pair)
    ready = scatter_mid.send(low_pair) + scatter_top.send(low_pair)
    back = field_back(1, ready, [], [], at(CHANNELS), partial)
    ready = scatter_mid.send([back]) + scatter_top.send([back]) + scatter_low.send([back])
    back = field_back(0, ready, [back], [at(CHANNELS)], at(CHANNELS), partial)
    share_mid = scatter_mid.send([back])
    ready = scatter_top.send([back]) + scatter_low.send([back])
    grad_entry = field_back(
        2,
        ready,
        [back, mask, dpool, valid, x, order],
        [
            at(CHANNELS),
            at(CHANNELS),
            whole((clips, CHANNELS)),
            at(128),
            at(CHAN_IN),
            whole((CHANNELS, CHANNELS)),
        ],
        whole((CHANNELS, CHAN_IN)),
        shape((CHANNELS, CHAN_IN), BF),
        [pltpu.VMEM((CHANNELS, CHAN_IN), F32)],
    )
    entry_parts = lax.all_to_all(grad_entry.reshape(links.devices, shard, CHAN_IN), AXES, 0, 0)
    entry_share = jnp.sum(entry_parts.astype(F32), axis=0)
    share_top = scatter_top.send([grad_entry])
    scatter_low.send([grad_entry])
    share_low = scatter_low.send([])

    def taps(share):
        return share.reshape(shard, 3, HIDDEN).transpose(1, 0, 2)

    correction = 1.0 - jnp.power(0.5, step_count[0].astype(F32))
    total_three = jnp.sum(all_three, axis=(0, 1))
    total_four = jnp.sum(all_four, axis=(0, 1))
    small_grad = jnp.concatenate(
        [
            total_four[HIDDEN:],
            total_four[:HIDDEN],
            total_three[CHANNELS : 2 * CHANNELS],
            total_three[:CHANNELS],
            total_three[2 * CHANNELS : 2 * CHANNELS + CLASSES],
        ]
    )
    loss = total_three[2 * CHANNELS + CLASSES] / coef[1, HIDDEN]
    spatial_grad_share = jnp.concatenate(
        [taps(share[0]) for share in (share_top, share_mid, share_low)], axis=0
    )
    time_share = time_share[0]
    temporal_share = taps(time_share[:, CHANNELS:]).transpose(0, 2, 1)
    entry_out = adamw(
        w_entry, entry_share.T, entry_first, entry_second, 0.06, DECAY_RATE, correction
    )
    spatial_out = adamw(
        w_spatial, spatial_grad_share, spatial_first, spatial_second, 0.02, DECAY_RATE, correction
    )
    temporal_out = adamw(
        w_temporal, temporal_share, temporal_first, temporal_second, 0.02, DECAY_RATE, correction
    )
    head_out = adamw(
        w_head, time_share[:, :CLASSES], head_first, head_second, 0.05, DECAY_RATE, correction
    )
    small_out = adamw(small_params, small_grad, small_first, small_second, 0.5, 0.0, correction)
    return (
        loss,
        *entry_out,
        *spatial_out,
        *temporal_out,
        *head_out,
        *small_out,
        entry_out[0].astype(BF),
        spatial_out[0].astype(BF),
        temporal_out[0].astype(BF),
        head_out[0].astype(BF),
    )


def solution(mesh):
    devices = mesh.shape["dp"] * mesh.shape["outer"]
    small_slice = mesh.shape["dp"] == 16 and mesh.shape["outer"] == 2
    links = Slice(devices) if small_slice else Plain(devices)
    both = ("dp", "outer")
    entry, spatial, temporal, head = (
        P(None, both),
        P(None, both, None),
        P(None, None, both),
        P(both, None),
    )
    placed = (
        P(both, None, None, None, None),
        P(both, None, None, None),
        P(both),
        P(both),
        P(),
        entry,
        spatial,
        temporal,
        head,
        P(),
        entry,
        entry,
        spatial,
        spatial,
        temporal,
        temporal,
        head,
        head,
        P(),
        P(),
    )
    return jax.shard_map(
        functools.partial(on_device, links),
        mesh=mesh,
        in_specs=placed,
        out_specs=(
            P(),
            *([entry] * 3),
            *([spatial] * 3),
            *([temporal] * 3),
            *([head] * 3),
            P(),
            P(),
            P(),
            entry,
            spatial,
            temporal,
            head,
        ),
        check_vma=False,
    )
```

```python
import functools

import jax
import jax.numpy as jnp
from jax import lax
from jax.experimental import pallas as pl
from jax.experimental.pallas import tpu as pltpu
from jax.sharding import PartitionSpec as P

CHANNELS = 512
HIDDEN = 1152
CLASSES = 400
CHAN_IN = 256

EPSILON = 1e-05
ADAM_EPS = 1e-08
DECAY_RATE = 0.1
SMOOTHING = 0.1

AXES = ("dp", "outer")
BF = jnp.bfloat16
F32 = jnp.float32
MIB = 1 << 20
EXACT = lax.Precision.HIGHEST


def wide(column, times):
    return jnp.concatenate([column] * times, axis=1)


def dot_nn(left, right):
    return lax.dot_general(left, right, (((1,), (0,)), ((), ())), preferred_element_type=F32)


def dot_nt(left, right):
    return lax.dot_general(left, right, (((1,), (1,)), ((), ())), preferred_element_type=F32)


def dot_tn(left, right):
    return lax.dot_general(left, right, (((0,), (0,)), ((), ())), preferred_element_type=F32)


def to_owner_order(row, order):
    return lax.dot_general(
        row, order, (((1,), (0,)), ((), ())), precision=EXACT, preferred_element_type=F32
    )


def to_local_order(row, order):
    return lax.dot_general(
        row, order, (((1,), (1,)), ((), ())), precision=EXACT, preferred_element_type=F32
    )


def fold(value, step):
    return jnp.sum(value.reshape(value.shape[0] // step, step, value.shape[1]), axis=0)


def spread_row(ref, row):
    ref[...] = jnp.broadcast_to(row[None], ref.shape)


def whole(shape):
    return pl.BlockSpec(shape, lambda *_: (0,) * len(shape), pipeline_mode=pl.Buffered(1))


def result(shape):
    return pl.BlockSpec(shape, lambda *_: (0,) * len(shape))


def call(
    kernel, name, grid, in_specs, out_specs, out_shape, scratch=(), aliases=None, vmem=22, flops=0,
    gates=(), moved=20 * MIB,
):
    first, last = len(in_specs), len(in_specs) + len(gates)

    def gated(*refs):
        kernel(*refs[:first], *refs[last:])

    run = pl.pallas_call(
        gated,
        name=name,
        grid=grid,
        in_specs=list(in_specs) + [pl.BlockSpec(memory_space=pl.ANY)] * len(gates),
        out_specs=out_specs,
        out_shape=out_shape,
        scratch_shapes=list(scratch),
        input_output_aliases=aliases or {},
        compiler_params=pltpu.CompilerParams(vmem_limit_bytes=vmem * MIB),
        cost_estimate=pl.CostEstimate(flops=flops, bytes_accessed=moved, transcendentals=0),
    )
    return lambda *operands: run(*operands, *gates)


def entry_kernel(count, side, clips, x_ref, valid_ref, *refs):
    pieces, (field_ref, cols_ref, conv_ref, w_ref, e_ref) = refs[:count], refs[count:]

    @pl.when(pl.program_id(0) == 0)
    def _():
        at = 0
        for piece in pieces:
            rows = piece.shape[0]
            for b in range(3):
                w_ref[b * CHANNELS + at : b * CHANNELS + at + rows, :] = piece[
                    :, b * HIDDEN : (b + 1) * HIDDEN
                ]
            e_ref[at : at + rows, :] = piece[:, 3 * HIDDEN :]
            at += rows

    value = dot_nt(x_ref[...], e_ref[...]) * wide(valid_ref[...], CHANNELS // 128)
    field_ref[...] = value
    rows = value.shape[0]
    group = side * clips
    grid3 = value.reshape(rows // group, group, CHANNELS)
    edge = jnp.zeros((rows // group, clips, CHANNELS), F32)
    left = jnp.concatenate([edge, grid3[:, : group - clips]], axis=1).reshape(rows, CHANNELS)
    right = jnp.concatenate([grid3[:, clips:], edge], axis=1).reshape(rows, CHANNELS)
    cols_ref[:, :CHANNELS] = left.astype(BF)
    cols_ref[:, CHANNELS : 2 * CHANNELS] = value.astype(BF)
    cols_ref[:, 2 * CHANNELS :] = right.astype(BF)
    conv_ref[...] = dot_nn(cols_ref[...], w_ref[...])


def spatial_kernel(count, tap_row, group, cols_ref, conv_ref, *refs):
    pieces, refs = refs[:count], refs[count:]
    step = pl.program_id(0)
    if tap_row == 0:
        out_ref, w_ref = refs
    else:
        valid_ref, keep_ref, out_ref, stats_ref, w_ref, acc_ref = refs

    @pl.when(step == 0)
    def _():
        at = 0
        for piece in pieces:
            rows = piece.shape[0]
            for b in range(3):
                w_ref[b * CHANNELS + at : b * CHANNELS + at + rows, :] = piece[
                    :, b * HIDDEN : (b + 1) * HIDDEN
                ]
            at += rows

    rows = cols_ref.shape[0]
    if tap_row == 0:
        out_ref[:group] = conv_ref[:group]
        out_ref[group:] = conv_ref[group:] + dot_nn(cols_ref[: rows - group], w_ref[...])
        return
    out_ref[rows - group :] = conv_ref[rows - group :]
    out_ref[: rows - group] = conv_ref[: rows - group] + dot_nn(cols_ref[group:], w_ref[...])

    @pl.when(step == 0)
    def _():
        acc_ref[...] = jnp.zeros_like(acc_ref)

    value = out_ref[...]
    kept = value * wide(valid_ref[...], HIDDEN // 128)
    acc_ref[:, :HIDDEN] += fold(kept, 8)
    acc_ref[:, HIDDEN : 2 * HIDDEN] += fold(kept * value, 8)
    acc_ref[:, 2 * HIDDEN : 2 * HIDDEN + 128] += fold(valid_ref[...], 8)

    @pl.when(step == pl.num_programs(0) - 1)
    def _():
        acc_ref[:, 2 * HIDDEN + 128 :] = fold(keep_ref[...], 8)
        spread_row(stats_ref, jnp.sum(acc_ref[...], axis=0, keepdims=True))


def temporal_kernel(
    count, frames, recv_ref, conv_ref, valid_ref, valid_out_ref, gain_ref, shift_ref, order_ref, *refs
):
    pieces, refs = refs[:count], refs[count:]
    first_ref, two_ref, stats_ref, coef_ref, head_ref, w_ref, first_all, acc_ref = refs
    step = pl.program_id(0)
    per = conv_ref.shape[0]

    @pl.when(step == 0)
    def _():
        at = 0
        for piece in pieces:
            rows = piece.shape[0]
            head_ref[at : at + rows, :] = piece[:, :CHANNELS]
            w_ref[at : at + rows, :] = piece[:, CHANNELS:]
            at += rows
        total = jnp.sum(recv_ref[...], axis=0)
        count_all = total[:, 2 * HIDDEN : 2 * HIDDEN + 128]
        wide_count = wide(count_all, HIDDEN // 128)
        mean = total[:, :HIDDEN] / wide_count
        variance = total[:, HIDDEN : 2 * HIDDEN] / wide_count - mean * mean
        coef_ref[...] = jnp.zeros_like(coef_ref)
        coef_ref[0:1, :HIDDEN] = mean
        coef_ref[1:2, :HIDDEN] = lax.rsqrt(variance + EPSILON)
        coef_ref[2:3, :HIDDEN] = gain_ref[...]
        coef_ref[3:4, :HIDDEN] = shift_ref[...]
        coef_ref[0:1, HIDDEN:] = count_all
        coef_ref[1:2, HIDDEN:] = total[:, 2 * HIDDEN + 128 :]
        acc_ref[...] = jnp.zeros_like(acc_ref)

    @pl.when(step < frames)
    def _():
        normed = (conv_ref[...] - coef_ref[0:1, :HIDDEN]) * coef_ref[1:2, :HIDDEN]
        pre = coef_ref[2:3, :HIDDEN] * normed + coef_ref[3:4, :HIDDEN]
        first = (jnp.maximum(pre, 0.0) * wide(valid_ref[...], HIDDEN // 128)).astype(BF)
        first_ref[...] = first
        first_all[pl.ds(pl.multiple_of(step * per, per), per), :] = first

    def frame(start, taps):
        pieces_at = [
            first_all[pl.ds(pl.multiple_of(start + k * per, per), per), :] for k in range(len(taps))
        ]
        lanes = slice(taps[0] * HIDDEN, (taps[-1] + 1) * HIDDEN)
        value = dot_nt(jnp.concatenate(pieces_at, axis=1), w_ref[:, lanes])
        two_ref[...] = value
        kept = value * wide(valid_out_ref[...], CHANNELS // 128)
        acc_ref[:, :CHANNELS] += fold(kept, 8)
        acc_ref[:, CHANNELS:] += fold(kept * value, 8)

    @pl.when(step == 1)
    def _():
        frame(0, (1, 2))

    @pl.when(jnp.logical_and(step > 1, step < frames))
    def _():
        frame((step - 2) * per, (0, 1, 2))

    @pl.when(step == frames)
    def _():
        frame((frames - 2) * per, (0, 1))
        sums = jnp.sum(acc_ref[...], axis=0, keepdims=True)
        parts = [
            to_owner_order(sums[:, :CHANNELS], order_ref[...]),
            to_owner_order(sums[:, CHANNELS:], order_ref[...]),
        ]
        spread_row(stats_ref, jnp.concatenate(parts, axis=1))


def head_kernel(
    clips, recv_ref, two_ref, field_ref, valid_ref, coef_ref, gain_ref, shift_ref, order_ref,
    head_ref, bias_ref, target_ref, keep_ref,
    dpool_ref, stats_ref, coef_two_ref, keep_grad_ref, send_grad_ref, acc_ref, size_ref,
):
    step = pl.program_id(0)

    @pl.when(step == 0)
    def _():
        total = jnp.sum(recv_ref[...], axis=0)
        count = wide(coef_ref[0:1, HIDDEN:], CHANNELS // 128)
        mean = to_local_order(total[:, :CHANNELS], order_ref[...]) / count
        square = to_local_order(total[:, CHANNELS:], order_ref[...]) / count
        coef_two_ref[...] = jnp.zeros_like(coef_two_ref)
        coef_two_ref[0:1, :] = mean
        coef_two_ref[1:2, :] = lax.rsqrt(square - mean * mean + EPSILON)
        coef_two_ref[2:3, :] = to_local_order(gain_ref[...], order_ref[...])
        coef_two_ref[3:4, :] = to_local_order(shift_ref[...], order_ref[...])
        acc_ref[...] = jnp.zeros_like(acc_ref)
        size_ref[...] = jnp.zeros_like(size_ref)

    valid = wide(valid_ref[...], CHANNELS // 128)
    normed = (two_ref[...] - coef_two_ref[0:1, :]) * coef_two_ref[1:2, :]
    pre = coef_two_ref[2:3, :] * normed + coef_two_ref[3:4, :] + field_ref[...]
    mask = jnp.where(pre > 0.0, valid, 0.0)
    acc_ref[0] += fold(jnp.maximum(pre, 0.0) * valid, clips)
    acc_ref[1] += fold(mask, clips)
    acc_ref[2] += fold(mask * normed, clips)
    size_ref[...] += fold(valid_ref[...], clips)

    @pl.when(step == pl.num_programs(0) - 1)
    def _():
        size = wide(size_ref[...], CHANNELS // 128)
        pooled_low = (acc_ref[0] / size).astype(BF)
        head = head_ref[...]
        logits = dot_nn(pooled_low, head) + bias_ref[...]
        shifted = logits - jnp.max(logits, axis=1, keepdims=True)
        log_prob = shifted - jnp.log(jnp.sum(jnp.exp(shifted), axis=1, keepdims=True))
        target = target_ref[...]
        per_clip = -jnp.sum(target * log_prob, axis=1, keepdims=True)
        keep = wide(keep_ref[...], CHANNELS // 128)
        loss = jnp.sum(keep * per_clip, axis=0, keepdims=True)
        kept = wide(coef_ref[1:2, HIDDEN:], CHANNELS // 128)
        d_logits = keep * (jnp.exp(log_prob) - target) / kept
        d_low = d_logits.astype(BF)
        grad = dot_tn(pooled_low.astype(F32), d_low.astype(F32)).astype(BF)
        half = grad.shape[0] // 2
        keep_grad_ref[...] = grad[:half]
        send_grad_ref[...] = grad[half:]
        d_pooled = dot_nt(d_low, head) / size
        dpool_ref[...] = d_pooled
        sums_one = jnp.sum(acc_ref[1] * d_pooled, axis=0, keepdims=True)
        sums_two = jnp.sum(acc_ref[2] * d_pooled, axis=0, keepdims=True)
        lane = lax.broadcasted_iota(jnp.int32, (1, CHANNELS), 1)
        parts = [
            to_owner_order(sums_one, order_ref[...]),
            to_owner_order(sums_two, order_ref[...]),
            jnp.where(lane < CLASSES, jnp.sum(d_logits, axis=0, keepdims=True), loss),
        ]
        spread_row(stats_ref, jnp.concatenate(parts, axis=1))


def first_back_kernel(
    count, frames, clips, recv_ref, two_ref, field_ref, valid_ref, coef_ref, coef_two_ref, dpool_ref,
    order_ref, conv_ref, valid_out_ref, *refs
):
    pieces, refs = refs[:count], refs[count:]
    dtwo_ref, mask_ref, dpre_ref, stats_ref, total_ref, w_ref, dtwo_all, back_ref, acc_ref = refs
    step = pl.program_id(0)
    per = conv_ref.shape[0]

    @pl.when(step == 0)
    def _():
        at = 0
        for piece in pieces:
            rows = piece.shape[0]
            for t in range(3):
                w_ref[t * CHANNELS + at : t * CHANNELS + at + rows, :] = piece[
                    :, CHANNELS + t * HIDDEN : CHANNELS + (t + 1) * HIDDEN
                ]
            at += rows
        total = jnp.sum(recv_ref[...], axis=0)
        total_ref[...] = total
        each = wide(coef_ref[0:1, HIDDEN:], CHANNELS // 128)
        back_ref[0:1, :] = to_local_order(total[:, :CHANNELS], order_ref[...]) / each
        back_ref[1:2, :] = to_local_order(total[:, CHANNELS : 2 * CHANNELS], order_ref[...]) / each
        acc_ref[...] = jnp.zeros_like(acc_ref)

    @pl.when(step < frames)
    def _():
        valid = wide(valid_ref[...], CHANNELS // 128)
        gain = coef_two_ref[2:3, :]
        inverse = coef_two_ref[1:2, :]
        normed = (two_ref[...] - coef_two_ref[0:1, :]) * inverse
        pre = gain * normed + coef_two_ref[3:4, :] + field_ref[...]
        mask = jnp.where(pre > 0.0, valid, 0.0)
        spread = jnp.broadcast_to(dpool_ref[...][None], (per // clips, clips, CHANNELS))
        d_pre = mask * spread.reshape(per, CHANNELS)
        low = (
            valid * (gain * inverse) * (d_pre - back_ref[0:1, :] - normed * back_ref[1:2, :])
        ).astype(BF)
        mask_ref[...] = mask.astype(BF)
        dtwo_ref[...] = low
        dtwo_all[pl.ds(pl.multiple_of(step * per, per), per), :] = low

    def frame(last, taps):
        pieces_at = [
            dtwo_all[pl.ds(pl.multiple_of(last - k * per, per), per), :] for k in range(len(taps))
        ]
        d_first = dot_nn(
            jnp.concatenate(pieces_at, axis=1),
            w_ref[taps[0] * CHANNELS : (taps[-1] + 1) * CHANNELS, :],
        )
        normed = (conv_ref[...] - coef_ref[0:1, :HIDDEN]) * coef_ref[1:2, :HIDDEN]
        pre = coef_ref[2:3, :HIDDEN] * normed + coef_ref[3:4, :HIDDEN]
        d_pre = jnp.where(pre > 0.0, d_first, 0.0) * wide(valid_out_ref[...], HIDDEN // 128)
        dpre_ref[...] = d_pre
        acc_ref[:, :HIDDEN] += fold(d_pre, 8)
        acc_ref[:, HIDDEN:] += fold(d_pre * normed, 8)

    @pl.when(step == 1)
    def _():
        frame(per, (0, 1))

    @pl.when(jnp.logical_and(step > 1, step < frames))
    def _():
        frame(step * per, (0, 1, 2))

    @pl.when(step == frames)
    def _():
        frame((frames - 1) * per, (1, 2))
        spread_row(stats_ref, jnp.sum(acc_ref[...], axis=0, keepdims=True))


def conv_back_kernel(
    recv_ref, conv_ref, dpre_ref, valid_ref, coef_ref, out_ref, total_ref, back_ref
):
    @pl.when(pl.program_id(0) == 0)
    def _():
        total = jnp.sum(recv_ref[...], axis=0)
        total_ref[...] = total
        each = wide(coef_ref[0:1, HIDDEN:], HIDDEN // 128)
        back_ref[0:1, :] = total[:, :HIDDEN] / each
        back_ref[1:2, :] = total[:, HIDDEN:] / each

    inverse = coef_ref[1:2, :HIDDEN]
    normed = (conv_ref[...] - coef_ref[0:1, :HIDDEN]) * inverse
    value = dpre_ref[...] - back_ref[0:1, :] - normed * back_ref[1:2, :]
    scale = coef_ref[2:3, :HIDDEN] * inverse
    out_ref[...] = (wide(valid_ref[...], HIDDEN // 128) * scale * value).astype(BF)


def temporal_grad_kernel(per, dtwo_ref, first_ref, keep_ref, send_ref):
    rows = dtwo_ref.shape[0]
    half = CHANNELS // 2

    def tap(low_out, low_in, size):
        grad = dot_tn(dtwo_ref[low_out : low_out + size], first_ref[low_in : low_in + size]).astype(BF)
        keep_ref[...] = grad[:half]
        send_ref[...] = grad[half:]

    step = pl.program_id(0)
    pl.when(step == 0)(lambda: tap(per, 0, rows - per))
    pl.when(step == 1)(lambda: tap(0, 0, rows))
    pl.when(step == 2)(lambda: tap(0, per, rows - per))


def spatial_grad_kernel(tap_row, per, group, cols_ref, d_ref, keep_ref, send_ref):
    rows = d_ref.shape[0]
    half = CHANNELS // 2
    if tap_row == 1:
        grad = dot_tn(cols_ref[...], d_ref[...])
    else:
        left, right = (0, group) if tap_row == 0 else (group, 0)
        size = per - group
        cols = jnp.concatenate(
            [cols_ref[f + left : f + left + size] for f in range(0, rows, per)], axis=0
        )
        back = jnp.concatenate(
            [d_ref[f + right : f + right + size] for f in range(0, rows, per)], axis=0
        )
        grad = dot_tn(cols, back)
    grad = grad.astype(BF)
    keep_ref[...] = grad[:half]
    send_ref[...] = grad[half:]


def field_back_kernel(count, tap_col, per, group, clips, d_ref, *refs):
    piece_refs, refs = refs[: 3 * count], refs[3 * count :]
    if tap_col == 1:
        out_ref, w_ref, pad_ref = refs
    elif tap_col == 0:
        acc_in_ref, out_ref, w_ref, pad_ref = refs
    else:
        (acc_in_ref, mask_ref, dpool_ref, valid_ref, x_ref, order_ref,
         out_ref, w_ref, pad_ref, grad_ref) = refs
    step = pl.program_id(0)

    @pl.when(step == 0)
    def _():
        for a in range(3):
            at = 0
            for piece in piece_refs[a * count : (a + 1) * count]:
                rows = piece.shape[0]
                w_ref[at : at + rows, a * HIDDEN : (a + 1) * HIDDEN] = piece[...]
                at += rows
        pad_ref[:group] = jnp.zeros((group, HIDDEN), BF)
        pad_ref[group + per :] = jnp.zeros((group, HIDDEN), BF)

    pad_ref[group : group + per] = d_ref[...]
    left = jnp.concatenate(
        [pad_ref[(2 - a) * group : (2 - a) * group + per] for a in range(3)], axis=1
    )
    value = dot_nt(left, w_ref[...])
    if tap_col == 1:
        out_ref[...] = value
        return
    value = value.reshape(per // group, group, CHANNELS)
    edge = jnp.zeros((per // group, clips, CHANNELS), F32)
    if tap_col == 0:
        value = jnp.concatenate([value[:, clips:], edge], axis=1)
    else:
        value = jnp.concatenate([edge, value[:, : group - clips]], axis=1)
    value = acc_in_ref[...] + value.reshape(per, CHANNELS)
    if tap_col == 0:
        out_ref[...] = value
        return
    spread = jnp.broadcast_to(dpool_ref[...][None], (per // clips, clips, CHANNELS))
    value = value + mask_ref[...].astype(F32) * spread.reshape(per, CHANNELS)
    d_entry = (value * wide(valid_ref[...], CHANNELS // 128)).astype(BF)
    grad = dot_tn(d_entry, x_ref[...])

    @pl.when(step == 0)
    def _():
        grad_ref[...] = grad

    @pl.when(step > 0)
    def _():
        grad_ref[...] += grad

    @pl.when(step == pl.num_programs(0) - 1)
    def _():
        out_ref[...] = dot_tn(order_ref[...].astype(BF), grad_ref[...].astype(BF)).astype(BF)


def wait_for(value, others):
    return lax.optimization_barrier((value, *others))[0]


def split_four(devices):
    def pairs(move):
        result = []
        for source in range(devices):
            z, x, core, y = source >> 3, (source >> 2) & 1, (source >> 1) & 1, source & 1
            z, x, core, y = move(z, x, core, y)
            result.append((source, ((z * 2 + x) * 2 + core) * 2 + y))
        return result

    along_z = [pairs(lambda z, x, c, y, k=k: ((z + k) % 4, x, c, y)) for k in range(4)]
    back_z = [pairs(lambda z, x, c, y, k=k: ((z - k) % 4, x, c, y)) for k in range(4)]
    early = pairs(lambda z, x, c, y: (z, 1 - x, c, y) if c == 0 else (z, x, c, 1 - y))
    late = pairs(lambda z, x, c, y: (z, x, c, 1 - y) if c == 0 else (z, 1 - x, c, y))
    core = pairs(lambda z, x, c, y: (z, x, 1 - c, y))
    return along_z, back_z, early, late, core


class Slice:
    def __init__(self, devices):
        self.devices = devices
        self.along_z, self.back_z, self.early, self.late, self.core = split_four(devices)

    def send(self, value, pairs):
        return lax.ppermute(value, AXES, pairs)

    def order(self, rows):
        channel = jnp.arange(CHANNELS)
        block, inside = channel // rows, channel % rows
        other, j, i, k = block >> 4, (block >> 3) & 1, (block >> 2) & 1, block & 3
        at, y = lax.axis_index("dp"), lax.axis_index("outer")
        core = (at & 1) ^ other
        x = ((at >> 1) & 1) ^ jnp.where(core == 0, i, j)
        y = y ^ jnp.where(core == 0, j, i)
        z = ((at >> 2) - k) & 3
        return (((z * 2 + x) * 2 + core) * 2 + y) * rows + inside

    def gather(self, shard, after=()):
        shard = wait_for(shard, after)
        came = [self.send(shard, self.along_z[k]) for k in (1, 2, 3)]
        after = yield
        column = jnp.concatenate([shard] + [wait_for(part, after) for part in came], axis=0)
        came = self.send(column, self.early)
        after = yield [column]
        half = jnp.concatenate([column, wait_for(came, after)], axis=0)
        rest = self.send(half, self.late)
        other = self.send(half, self.core)
        after = yield [half, other]
        rest = wait_for(rest, after)
        yield [half, rest, other, self.send(rest, self.core)]

    def add_halves(self, keep, came):
        half = keep.shape[0] // 2
        kept = keep[:half].astype(F32) + came[:half].astype(F32)
        sent = keep[half:].astype(F32) + came[half:].astype(F32)
        return kept.astype(BF), sent.astype(BF)

    def scatter(self, keep, send, extra=None):
        came = self.send(send, self.core)
        if extra is not None:
            came = jnp.concatenate([self.send(extra[1], self.core), came], axis=1)
        after = yield
        if extra is not None:
            keep = jnp.concatenate([extra[0], keep], axis=1)
        keep, send = self.add_halves(keep, wait_for(came, after))
        came = self.send(send, self.late)
        after = yield [keep, send]
        keep, send = self.add_halves(keep, wait_for(came, after))
        came = self.send(send, self.early)
        after = yield [keep, send]
        total = keep.astype(F32) + wait_for(came, after).astype(F32)
        rows = total.shape[0] // 4
        result = total[:rows]
        parts = [total[k * rows : (k + 1) * rows].astype(BF) for k in (1, 2, 3)]
        came = [self.send(part, pairs) for part, pairs in zip(parts, self.back_z[1:], strict=True)]
        after = yield [result, *parts]
        for part in came:
            result = result + wait_for(part, after).astype(F32)
        yield [result]


class Plain:
    def __init__(self, devices):
        self.devices = devices

    def order(self, rows):
        return jnp.arange(CHANNELS)

    def gather(self, shard, after=()):
        result = [lax.all_gather(shard, AXES, axis=0, tiled=True)]
        yield
        yield result
        yield [*result, *result]
        yield result

    def scatter(self, keep, send, extra=None):
        value = jnp.concatenate([keep, send], axis=0)
        if extra is not None:
            value = jnp.concatenate([jnp.concatenate(extra, axis=0), value], axis=1)
        result = [lax.psum_scatter(value.astype(F32), AXES, scatter_dimension=0, tiled=True)]
        while True:
            yield result


def share_rows(spread):
    return lax.all_to_all(spread, AXES, 0, 0)


def adamw(master, grad, first, second, rate, decay, correction):
    first_new = 0.5 * first + 0.5 * grad
    second_new = 0.5 * second + 0.5 * grad * grad
    master_new = master - rate * (
        first_new / correction / (jnp.sqrt(second_new / correction) + ADAM_EPS) + decay * master
    )
    return (master_new, first_new, second_new)


def on_device(
    links,
    clip_frames,
    valid_mask,
    labels,
    clip_keep,
    step_count,
    w_entry,
    w_spatial,
    w_temporal,
    w_head,
    small_params,
    entry_first,
    entry_second,
    spatial_first,
    spatial_second,
    temporal_first,
    temporal_second,
    head_first,
    head_second,
    small_first,
    small_second,
):
    clips, frames, height, breadth, _ = clip_frames.shape
    shard = w_spatial.shape[1]
    group = breadth * clips
    per = height * group
    rows = frames * per
    shape = jax.ShapeDtypeStruct

    def flat(taps):
        return taps.astype(BF).transpose(1, 0, 2).reshape(shard, -1)

    entry_t = w_entry.T
    temporal_t = w_temporal.transpose(0, 2, 1)
    head_pad = jnp.pad(w_head.astype(BF), ((0, 0), (0, CHANNELS - CLASSES)))
    load_mid = links.gather(jnp.concatenate([flat(w_spatial[3:6]), entry_t.astype(BF)], axis=1))
    next(load_mid)
    column_mid = load_mid.send([])
    load_top = links.gather(flat(w_spatial[0:3]), column_mid)
    next(load_top)
    half_mid, other_mid = load_mid.send([])
    column_top = load_top.send([half_mid])
    load_low = links.gather(flat(w_spatial[6:9]), [*column_top, other_mid])
    next(load_low)
    column_low = load_low.send([])
    head_time = jnp.concatenate([head_pad, flat(temporal_t)], axis=1)
    load_time = links.gather(head_time, column_low)
    next(load_time)
    ready = load_top.send(column_low)
    pieces_mid = load_mid.send([])
    count = len(pieces_mid)

    index = links.order(shard)
    order = (index[:, None] == jnp.arange(CHANNELS)[None, :]).astype(F32)
    gain_one = small_params[None, :HIDDEN]
    shift_one = small_params[None, HIDDEN : 2 * HIDDEN]
    gain_two = small_params[None, 2 * HIDDEN : 2 * HIDDEN + CHANNELS]
    shift_two = small_params[None, 2 * HIDDEN + CHANNELS : 2 * HIDDEN + 2 * CHANNELS]
    bias = jnp.pad(
        small_params[None, 2 * HIDDEN + 2 * CHANNELS :],
        ((0, 0), (0, CHANNELS - CLASSES)),
        constant_values=-1e30,
    )
    x = clip_frames.transpose(1, 2, 3, 0, 4).reshape(rows, CHAN_IN)
    valid = jnp.broadcast_to(
        valid_mask.astype(F32).transpose(1, 2, 3, 0).reshape(rows, 1), (rows, 128)
    )
    keep = jnp.broadcast_to(clip_keep.astype(F32)[:, None], (clips, 128))
    lane = jnp.arange(CHANNELS)[None, :]
    target = jnp.where(
        lane < CLASSES,
        (1.0 - SMOOTHING) * (labels[:, None] == lane).astype(F32) + SMOOTHING / CLASSES,
        0.0,
    )

    correction = 1.0 - jnp.power(0.5, step_count[0].astype(F32))
    correction = jnp.broadcast_to(correction, (1, 128))
    prepared = [order, gain_one, shift_one, gain_two, shift_two, bias, target, keep, correction]

    def at(width, where=lambda i: i):
        return pl.BlockSpec((per, width), lambda i: (where(i), 0))

    def piece_specs(pieces):
        return [whole(p.shape) for p in pieces]

    def now(i):
        return jnp.minimum(i, frames - 1)

    def before(i):
        return jnp.maximum(i - 1, 0)

    conv_flops = 2 * rows * 3 * CHANNELS * HIDDEN

    field, cols, conv = call(
        functools.partial(entry_kernel, count, breadth, clips),
        "entry_and_middle_taps",
        (frames,),
        [at(CHAN_IN), at(128)] + piece_specs(pieces_mid),
        [at(CHANNELS), at(3 * CHANNELS), at(HIDDEN)],
        [shape((rows, CHANNELS), F32), shape((rows, 3 * CHANNELS), BF), shape((rows, HIDDEN), F32)],
        [pltpu.VMEM((3 * CHANNELS, HIDDEN), BF), pltpu.VMEM((CHANNELS, CHAN_IN), BF)],
        flops=conv_flops,
        gates=[ready[0], *column_low, *prepared],
    )(x, valid, *pieces_mid)
    ready = load_low.send([conv])
    pieces_top = load_top.send([conv])
    column_time = load_time.send([conv])
    conv = call(
        functools.partial(spatial_kernel, count, 0, group),
        "upper_taps",
        (frames,),
        [at(3 * CHANNELS), at(HIDDEN)] + piece_specs(pieces_top),
        at(HIDDEN),
        shape((rows, HIDDEN), F32),
        [pltpu.VMEM((3 * CHANNELS, HIDDEN), BF)],
        aliases={1: 0},
        flops=conv_flops,
        gates=[ready[0], *column_time],
    )(cols, conv, *pieces_top)
    pieces_low = load_low.send([conv])
    ready = load_time.send([conv])
    conv, stats = call(
        functools.partial(spatial_kernel, count, 2, group),
        "lower_taps",
        (frames,),
        [at(3 * CHANNELS), at(HIDDEN)] + piece_specs(pieces_low) + [at(128), whole((clips, 128))],
        [at(HIDDEN), result((links.devices, 1, 2 * HIDDEN + 256))],
        [shape((rows, HIDDEN), F32), shape((links.devices, 1, 2 * HIDDEN + 256), F32)],
        [pltpu.VMEM((3 * CHANNELS, HIDDEN), BF), pltpu.VMEM((8, 2 * HIDDEN + 256), F32)],
        aliases={1: 0},
        flops=conv_flops,
        gates=ready[:1],
    )(cols, conv, *pieces_low, valid, keep)
    pieces_time = load_time.send([conv])
    stats = wait_for(stats, ready[1:])
    all_stats = share_rows(stats)
    pieces_time = [wait_for(piece, [all_stats]) for piece in pieces_time]

    first, two, stats_two, coef, head = call(
        functools.partial(temporal_kernel, count, frames),
        "norm_and_temporal",
        (frames + 1,),
        [whole(all_stats.shape), at(HIDDEN, now), at(128, now), at(128, before)]
        + [whole((1, HIDDEN))] * 2
        + [whole((CHANNELS, CHANNELS))]
        + piece_specs(pieces_time),
        [
            at(HIDDEN, now),
            at(CHANNELS, before),
            result((links.devices, 1, 2 * CHANNELS)),
            result((8, HIDDEN + 128)),
            result((CHANNELS, CHANNELS)),
        ],
        [
            shape((rows, HIDDEN), BF),
            shape((rows, CHANNELS), F32),
            shape((links.devices, 1, 2 * CHANNELS), F32),
            shape((8, HIDDEN + 128), F32),
            shape((CHANNELS, CHANNELS), BF),
        ],
        [
            pltpu.VMEM((CHANNELS, 3 * HIDDEN), BF),
            pltpu.VMEM((rows, HIDDEN), BF),
            pltpu.VMEM((8, 2 * CHANNELS), F32),
        ],
        vmem=26,
        flops=conv_flops,
    )(all_stats, conv, valid, valid, gain_one, shift_one, order, *pieces_time)
    all_two = share_rows(stats_two)

    half = CHANNELS // 2
    dpool, stats_three, coef_two, head_keep, head_send = call(
        functools.partial(head_kernel, clips),
        "norm_head_and_back",
        (frames,),
        [whole(all_two.shape), at(CHANNELS), at(CHANNELS), at(128), whole((8, HIDDEN + 128))]
        + [whole((1, CHANNELS))] * 2
        + [whole((CHANNELS, CHANNELS))] * 2
        + [whole((1, CHANNELS)), whole((clips, CHANNELS)), whole((clips, 128))],
        [
            result((clips, CHANNELS)),
            result((links.devices, 1, 3 * CHANNELS)),
            result((8, CHANNELS)),
            result((half, CHANNELS)),
            result((half, CHANNELS)),
        ],
        [
            shape((clips, CHANNELS), F32),
            shape((links.devices, 1, 3 * CHANNELS), F32),
            shape((8, CHANNELS), F32),
            shape((half, CHANNELS), BF),
            shape((half, CHANNELS), BF),
        ],
        [pltpu.VMEM((3, clips, CHANNELS), F32), pltpu.VMEM((clips, 128), F32)],
    )(all_two, two, field, valid, coef, gain_two, shift_two, order, head, bias, target, keep)
    all_three = share_rows(stats_three)

    dtwo, mask, dpre, stats_four, total_three = call(
        functools.partial(first_back_kernel, count, frames, clips),
        "temporal_back",
        (frames + 1,),
        [
            whole(all_three.shape),
            at(CHANNELS, now),
            at(CHANNELS, now),
            at(128, now),
            whole((8, HIDDEN + 128)),
            whole((8, CHANNELS)),
            whole((clips, CHANNELS)),
            whole((CHANNELS, CHANNELS)),
            at(HIDDEN, before),
            at(128, before),
        ]
        + piece_specs(pieces_time),
        [at(CHANNELS, now), at(CHANNELS, now), at(HIDDEN, before), result((links.devices, 1, 2 * HIDDEN)),
         result((1, 3 * CHANNELS))],
        [
            shape((rows, CHANNELS), BF),
            shape((rows, CHANNELS), BF),
            shape((rows, HIDDEN), F32),
            shape((links.devices, 1, 2 * HIDDEN), F32),
            shape((1, 3 * CHANNELS), F32),
        ],
        [
            pltpu.VMEM((3 * CHANNELS, HIDDEN), BF),
            pltpu.VMEM((rows, CHANNELS), BF),
            pltpu.VMEM((8, CHANNELS), F32),
            pltpu.VMEM((8, 2 * HIDDEN), F32),
        ],
        vmem=28,
        flops=conv_flops,
    )(all_three, two, field, valid, coef, coef_two, dpool, order, conv, valid, *pieces_time)
    all_four = share_rows(stats_four)

    pair = [shape((half, 3 * HIDDEN), BF)] * 2
    pair_specs = [pl.BlockSpec((half, HIDDEN), lambda i: (0, i))] * 2
    time_pair = call(
        functools.partial(temporal_grad_kernel, per),
        "temporal_gradient",
        (3,),
        [whole((rows, CHANNELS)), whole((rows, HIDDEN))],
        pair_specs,
        pair,
        gates=[all_four],
        flops=conv_flops,
    )(dtwo, first)

    dconv, total_four = call(
        conv_back_kernel,
        "spatial_norm_back",
        (frames,),
        [whole(all_four.shape), at(HIDDEN), at(HIDDEN), at(128), whole((8, HIDDEN + 128))],
        [at(HIDDEN), result((1, 2 * HIDDEN))],
        [shape((rows, HIDDEN), BF), shape((1, 2 * HIDDEN), F32)],
        [pltpu.VMEM((8, HIDDEN), F32)],
        gates=time_pair,
    )(all_four, conv, dpre, valid, coef)

    def spatial_grad(tap_row, gates):
        return call(
            functools.partial(spatial_grad_kernel, tap_row, per, group),
            "spatial_gradient",
            (3,),
            [pl.BlockSpec((rows, CHANNELS), lambda i: (0, i)), whole((rows, HIDDEN))],
            pair_specs,
            pair,
            flops=conv_flops,
            gates=gates,
        )(cols, dconv)

    scatter_time = links.scatter(*time_pair, (head_keep, head_send))
    next(scatter_time)
    ready = scatter_time.send([dconv])
    mid_pair = spatial_grad(1, ready)
    scatter_mid = links.scatter(*mid_pair)
    next(scatter_mid)
    ready = scatter_time.send(mid_pair)
    top_pair = spatial_grad(0, ready)
    scatter_top = links.scatter(*top_pair)
    next(scatter_top)
    ready = scatter_time.send(top_pair) + scatter_mid.send(top_pair)
    low_pair = spatial_grad(2, ready)
    scatter_low = links.scatter(*low_pair)
    next(scatter_low)

    def field_back(tap_col, gates, extra, extra_specs, out_spec, out_shape, scratch=()):
        pieces = pieces_top + pieces_mid + pieces_low
        return call(
            functools.partial(field_back_kernel, count, tap_col, per, group, clips),
            "field_back",
            (frames,),
            [at(HIDDEN)]
            + [pl.BlockSpec((p.shape[0], HIDDEN), lambda i: (0, tap_col)) for p in pieces]
            + extra_specs,
            out_spec,
            out_shape,
            [
                pltpu.VMEM((CHANNELS, 3 * HIDDEN), BF),
                pltpu.VMEM((per + 2 * group, HIDDEN), BF),
                *scratch,
            ],
            flops=conv_flops,
            gates=gates,
        )(dconv, *pieces, *extra)

    partial = shape((rows, CHANNELS), F32)
    time_share = scatter_time.send(low_pair)
    ready = scatter_mid.send(low_pair) + scatter_top.send(low_pair)
    back = field_back(1, ready, [], [], at(CHANNELS), partial)
    ready = scatter_mid.send([back]) + scatter_top.send([back]) + scatter_low.send([back])
    back = field_back(0, ready, [back], [at(CHANNELS)], at(CHANNELS), partial)
    share_mid = scatter_mid.send([back])
    ready = scatter_top.send([back]) + scatter_low.send([back])
    grad_entry = field_back(
        2,
        ready,
        [back, mask, dpool, valid, x, order],
        [
            at(CHANNELS),
            at(CHANNELS),
            whole((clips, CHANNELS)),
            at(128),
            at(CHAN_IN),
            whole((CHANNELS, CHANNELS)),
        ],
        result((CHANNELS, CHAN_IN)),
        shape((CHANNELS, CHAN_IN), BF),
        [pltpu.VMEM((CHANNELS, CHAN_IN), F32)],
    )
    entry_parts = lax.all_to_all(grad_entry.reshape(links.devices, shard, CHAN_IN), AXES, 0, 0)
    entry_share = jnp.sum(entry_parts.astype(F32), axis=0)
    share_top = scatter_top.send([grad_entry])
    scatter_low.send([grad_entry])
    share_low = scatter_low.send([])

    def taps(share):
        return share.reshape(shard, 3, HIDDEN).transpose(1, 0, 2)

    correction = correction[0, 0]
    total_three = wait_for(total_three, [grad_entry])[0]
    total_four = wait_for(total_four, [grad_entry])[0]
    small_grad = jnp.concatenate(
        [
            total_four[HIDDEN:],
            total_four[:HIDDEN],
            total_three[CHANNELS : 2 * CHANNELS],
            total_three[:CHANNELS],
            total_three[2 * CHANNELS : 2 * CHANNELS + CLASSES],
        ]
    )
    loss = total_three[2 * CHANNELS + CLASSES] / coef[1, HIDDEN]
    spatial_grad_share = jnp.concatenate(
        [taps(share[0]) for share in (share_top, share_mid, share_low)], axis=0
    )
    time_share = time_share[0]
    temporal_share = taps(time_share[:, CHANNELS:]).transpose(0, 2, 1)
    entry_out = adamw(
        w_entry, entry_share.T, entry_first, entry_second, 0.06, DECAY_RATE, correction
    )
    spatial_out = adamw(
        w_spatial, spatial_grad_share, spatial_first, spatial_second, 0.02, DECAY_RATE, correction
    )
    temporal_out = adamw(
        w_temporal, temporal_share, temporal_first, temporal_second, 0.02, DECAY_RATE, correction
    )
    head_out = adamw(
        w_head, time_share[:, :CLASSES], head_first, head_second, 0.05, DECAY_RATE, correction
    )
    small_out = adamw(small_params, small_grad, small_first, small_second, 0.5, 0.0, correction)
    return (
        loss,
        *entry_out,
        *spatial_out,
        *temporal_out,
        *head_out,
        *small_out,
        entry_out[0].astype(BF),
        spatial_out[0].astype(BF),
        temporal_out[0].astype(BF),
        head_out[0].astype(BF),
    )


def solution(mesh):
    devices = mesh.shape["dp"] * mesh.shape["outer"]
    small_slice = mesh.shape["dp"] == 16 and mesh.shape["outer"] == 2
    links = Slice(devices) if small_slice else Plain(devices)
    both = ("dp", "outer")
    entry, spatial, temporal, head = (
        P(None, both),
        P(None, both, None),
        P(None, None, both),
        P(both, None),
    )
    placed = (
        P(both, None, None, None, None),
        P(both, None, None, None),
        P(both),
        P(both),
        P(),
        entry,
        spatial,
        temporal,
        head,
        P(),
        entry,
        entry,
        spatial,
        spatial,
        temporal,
        temporal,
        head,
        head,
        P(),
        P(),
    )
    return jax.shard_map(
        functools.partial(on_device, links),
        mesh=mesh,
        in_specs=placed,
        out_specs=(
            P(),
            *([entry] * 3),
            *([spatial] * 3),
            *([temporal] * 3),
            *([head] * 3),
            P(),
            P(),
            P(),
            entry,
            spatial,
            temporal,
            head,
        ),
        check_vma=False,
    )
```

```python
import functools

import jax
import jax.numpy as jnp
from jax import lax
from jax.experimental import pallas as pl
from jax.experimental.pallas import tpu as pltpu
from jax.sharding import PartitionSpec as P

CHANNELS = 512
HIDDEN = 1152
CLASSES = 400
CHAN_IN = 256
WIDTHS = (384, 512, 256)
STARTS = (0, 384, 896)

EPSILON = 1e-05
ADAM_EPS = 1e-08
DECAY_RATE = 0.1
SMOOTHING = 0.1

AXES = ("dp", "outer")
BF = jnp.bfloat16
F32 = jnp.float32
MIB = 1 << 20
EXACT = lax.Precision.HIGHEST


def wide(column, times):
    return jnp.concatenate([column] * times, axis=1)


def dot_nn(left, right):
    return lax.dot_general(left, right, (((1,), (0,)), ((), ())), preferred_element_type=F32)


def dot_nt(left, right):
    return lax.dot_general(left, right, (((1,), (1,)), ((), ())), preferred_element_type=F32)


def dot_tn(left, right):
    return lax.dot_general(left, right, (((0,), (0,)), ((), ())), preferred_element_type=F32)


def to_owner_order(row, order):
    return lax.dot_general(
        row, order, (((1,), (0,)), ((), ())), precision=EXACT, preferred_element_type=F32
    )


def to_local_order(row, order):
    return lax.dot_general(
        row, order, (((1,), (1,)), ((), ())), precision=EXACT, preferred_element_type=F32
    )


def fold(value, step):
    return jnp.sum(value.reshape(value.shape[0] // step, step, value.shape[1]), axis=0)


def spread_row(ref, row):
    ref[...] = jnp.broadcast_to(row[None], ref.shape)


def whole(shape):
    return pl.BlockSpec(shape, lambda *_: (0,) * len(shape), pipeline_mode=pl.Buffered(1))


def result(shape):
    return pl.BlockSpec(shape, lambda *_: (0,) * len(shape))


def call(
    kernel, name, grid, in_specs, out_specs, out_shape, scratch=(), aliases=None, vmem=22, flops=0,
    gates=(), moved=20 * MIB,
):
    first, last = len(in_specs), len(in_specs) + len(gates)

    def gated(*refs):
        kernel(*refs[:first], *refs[last:])

    run = pl.pallas_call(
        gated,
        name=name,
        grid=grid,
        in_specs=list(in_specs) + [pl.BlockSpec(memory_space=pl.ANY)] * len(gates),
        out_specs=out_specs,
        out_shape=out_shape,
        scratch_shapes=list(scratch),
        input_output_aliases=aliases or {},
        compiler_params=pltpu.CompilerParams(vmem_limit_bytes=vmem * MIB),
        cost_estimate=pl.CostEstimate(flops=flops, bytes_accessed=moved, transcendentals=0),
    )
    return lambda *operands: run(*operands, *gates)


def fill_taps(pieces, w_ref):
    width = w_ref.shape[1]
    at = 0
    for piece in pieces:
        rows = piece.shape[0]
        for tap in range(9):
            w_ref[tap * CHANNELS + at : tap * CHANNELS + at + rows, :] = piece[
                :, tap * width : (tap + 1) * width
            ]
        at += rows


def save(w_ref, w_out, sem, step):
    copy = pltpu.make_async_copy(w_ref, w_out, sem)
    pl.when(step == 0)(copy.start)
    pl.when(step == pl.num_programs(0) - 1)(copy.wait)


def spatial_taps(group, cols_ref, w_ref, conv_ref):
    rows, depth = cols_ref.shape
    conv_ref[...] = dot_nn(cols_ref[...], w_ref[depth : 2 * depth])
    conv_ref[group:] += dot_nn(cols_ref[: rows - group], w_ref[:depth])
    conv_ref[: rows - group] += dot_nn(cols_ref[group:], w_ref[2 * depth :])


def add_sums(conv_ref, valid_ref, acc_ref):
    value = conv_ref[...]
    width = value.shape[1]
    kept = value * wide(valid_ref[...], width // 128)
    acc_ref[:, :width] += fold(kept, 8)
    acc_ref[:, width:] += fold(kept * value, 8)


def entry_kernel(count, side, clips, x_ref, valid_ref, *refs):
    pieces, refs = refs[:count], refs[count:]
    field_ref, cols_ref, conv_ref, acc_ref, w_out, w_ref, e_ref, sem = refs

    @pl.when(pl.program_id(0) == 0)
    def _():
        fill_taps(pieces, w_ref)
        at = 0
        for piece in pieces:
            rows = piece.shape[0]
            e_ref[at : at + rows, :] = piece[:, 9 * w_ref.shape[1] :]
            at += rows
        acc_ref[...] = jnp.zeros_like(acc_ref)

    save(w_ref, w_out, sem, pl.program_id(0))
    value = dot_nt(x_ref[...], e_ref[...]) * wide(valid_ref[...], CHANNELS // 128)
    field_ref[...] = value
    rows = value.shape[0]
    group = side * clips
    grid3 = value.reshape(rows // group, group, CHANNELS)
    edge = jnp.zeros((rows // group, clips, CHANNELS), F32)
    left = jnp.concatenate([edge, grid3[:, : group - clips]], axis=1).reshape(rows, CHANNELS)
    right = jnp.concatenate([grid3[:, clips:], edge], axis=1).reshape(rows, CHANNELS)
    cols_ref[:, :CHANNELS] = left.astype(BF)
    cols_ref[:, CHANNELS : 2 * CHANNELS] = value.astype(BF)
    cols_ref[:, 2 * CHANNELS :] = right.astype(BF)
    spatial_taps(group, cols_ref, w_ref, conv_ref)
    add_sums(conv_ref, valid_ref, acc_ref)


def spatial_kernel(count, group, cols_ref, valid_ref, *refs):
    pieces, (conv_ref, acc_ref, w_out, w_ref, sem) = refs[:count], refs[count:]

    @pl.when(pl.program_id(0) == 0)
    def _():
        fill_taps(pieces, w_ref)
        acc_ref[...] = jnp.zeros_like(acc_ref)

    save(w_ref, w_out, sem, pl.program_id(0))
    spatial_taps(group, cols_ref, w_ref, conv_ref)
    add_sums(conv_ref, valid_ref, acc_ref)


def last_spatial_kernel(count, group, cols_ref, valid_ref, keep_ref, one_ref, two_ref, *refs):
    pieces, refs = refs[:count], refs[count:]
    conv_ref, stats_ref, w_out, w_ref, acc_ref, size_ref, sem = refs
    step = pl.program_id(0)

    @pl.when(step == 0)
    def _():
        fill_taps(pieces, w_ref)
        acc_ref[...] = jnp.zeros_like(acc_ref)
        size_ref[...] = jnp.zeros_like(size_ref)

    save(w_ref, w_out, sem, step)
    spatial_taps(group, cols_ref, w_ref, conv_ref)
    add_sums(conv_ref, valid_ref, acc_ref)
    size_ref[...] += fold(valid_ref[...], 8)

    @pl.when(step == pl.num_programs(0) - 1)
    def _():
        parts = (one_ref, two_ref, acc_ref)
        sums = [part[:, : part.shape[1] // 2] for part in parts]
        squares = [part[:, part.shape[1] // 2 :] for part in parts]
        line = jnp.concatenate(sums + squares + [size_ref[...], fold(keep_ref[...], 8)], axis=1)
        spread_row(stats_ref, jnp.sum(line, axis=0, keepdims=True))


def temporal_kernel(
    count, frames, recv_ref, *refs
):
    convs, (valid_ref, valid_out_ref, gain_ref, shift_ref, order_ref), refs = (
        refs[:3], refs[3:8], refs[8:]
    )
    pieces, refs = refs[:count], refs[count:]
    first_ref, two_ref, stats_ref, coef_ref, head_ref, w_ref, first_all, acc_ref = refs
    step = pl.program_id(0)
    per = valid_ref.shape[0]

    @pl.when(step == 0)
    def _():
        at = 0
        for piece in pieces:
            rows = piece.shape[0]
            head_ref[at : at + rows, :] = piece[:, :CHANNELS]
            w_ref[at : at + rows, :] = piece[:, CHANNELS:]
            at += rows
        total = jnp.sum(recv_ref[...], axis=0)
        count_all = total[:, 2 * HIDDEN : 2 * HIDDEN + 128]
        wide_count = wide(count_all, HIDDEN // 128)
        mean = total[:, :HIDDEN] / wide_count
        variance = total[:, HIDDEN : 2 * HIDDEN] / wide_count - mean * mean
        coef_ref[...] = jnp.zeros_like(coef_ref)
        coef_ref[0:1, :HIDDEN] = mean
        coef_ref[1:2, :HIDDEN] = lax.rsqrt(variance + EPSILON)
        coef_ref[2:3, :HIDDEN] = gain_ref[...]
        coef_ref[3:4, :HIDDEN] = shift_ref[...]
        coef_ref[0:1, HIDDEN:] = count_all
        coef_ref[1:2, HIDDEN:] = total[:, 2 * HIDDEN + 128 :]
        acc_ref[...] = jnp.zeros_like(acc_ref)

    @pl.when(step < frames)
    def _():
        for conv_ref, start, width in zip(convs, STARTS, WIDTHS, strict=True):
            lanes = slice(start, start + width)
            normed = (conv_ref[...] - coef_ref[0:1, lanes]) * coef_ref[1:2, lanes]
            pre = coef_ref[2:3, lanes] * normed + coef_ref[3:4, lanes]
            first = (jnp.maximum(pre, 0.0) * wide(valid_ref[...], width // 128)).astype(BF)
            first_ref[:, lanes] = first
            first_all[pl.ds(pl.multiple_of(step * per, per), per), lanes] = first

    def frame(start, taps):
        pieces_at = [
            first_all[pl.ds(pl.multiple_of(start + k * per, per), per), :] for k in range(len(taps))
        ]
        lanes = slice(taps[0] * HIDDEN, (taps[-1] + 1) * HIDDEN)
        value = dot_nt(jnp.concatenate(pieces_at, axis=1), w_ref[:, lanes])
        two_ref[...] = value
        kept = value * wide(valid_out_ref[...], CHANNELS // 128)
        acc_ref[:, :CHANNELS] += fold(kept, 8)
        acc_ref[:, CHANNELS:] += fold(kept * value, 8)

    @pl.when(step == 1)
    def _():
        frame(0, (1, 2))

    @pl.when(jnp.logical_and(step > 1, step < frames))
    def _():
        frame((step - 2) * per, (0, 1, 2))

    @pl.when(step == frames)
    def _():
        frame((frames - 2) * per, (0, 1))
        sums = jnp.sum(acc_ref[...], axis=0, keepdims=True)
        parts = [
            to_owner_order(sums[:, :CHANNELS], order_ref[...]),
            to_owner_order(sums[:, CHANNELS:], order_ref[...]),
        ]
        spread_row(stats_ref, jnp.concatenate(parts, axis=1))


def head_kernel(
    clips, recv_ref, two_ref, field_ref, valid_ref, coef_ref, gain_ref, shift_ref, order_ref,
    head_ref, bias_ref, target_ref, keep_ref,
    mask_ref, dpool_ref, stats_ref, coef_two_ref, keep_grad_ref, send_grad_ref, acc_ref, size_ref,
):
    step = pl.program_id(0)

    @pl.when(step == 0)
    def _():
        total = jnp.sum(recv_ref[...], axis=0)
        count = wide(coef_ref[0:1, HIDDEN:], CHANNELS // 128)
        mean = to_local_order(total[:, :CHANNELS], order_ref[...]) / count
        square = to_local_order(total[:, CHANNELS:], order_ref[...]) / count
        coef_two_ref[...] = jnp.zeros_like(coef_two_ref)
        coef_two_ref[0:1, :] = mean
        coef_two_ref[1:2, :] = lax.rsqrt(square - mean * mean + EPSILON)
        coef_two_ref[2:3, :] = to_local_order(gain_ref[...], order_ref[...])
        coef_two_ref[3:4, :] = to_local_order(shift_ref[...], order_ref[...])
        acc_ref[...] = jnp.zeros_like(acc_ref)
        size_ref[...] = jnp.zeros_like(size_ref)

    valid = wide(valid_ref[...], CHANNELS // 128)
    normed = (two_ref[...] - coef_two_ref[0:1, :]) * coef_two_ref[1:2, :]
    pre = coef_two_ref[2:3, :] * normed + coef_two_ref[3:4, :] + field_ref[...]
    mask = jnp.where(pre > 0.0, valid, 0.0)
    mask_ref[...] = mask.astype(BF)
    acc_ref[0] += fold(jnp.maximum(pre, 0.0) * valid, clips)
    acc_ref[1] += fold(mask, clips)
    acc_ref[2] += fold(mask * normed, clips)
    size_ref[...] += fold(valid_ref[...], clips)

    @pl.when(step == pl.num_programs(0) - 1)
    def _():
        size = wide(size_ref[...], CHANNELS // 128)
        pooled_low = (acc_ref[0] / size).astype(BF)
        head = head_ref[...]
        logits = dot_nn(pooled_low, head) + bias_ref[...]
        shifted = logits - jnp.max(logits, axis=1, keepdims=True)
        log_prob = shifted - jnp.log(jnp.sum(jnp.exp(shifted), axis=1, keepdims=True))
        target = target_ref[...]
        per_clip = -jnp.sum(target * log_prob, axis=1, keepdims=True)
        keep = wide(keep_ref[...], CHANNELS // 128)
        loss = jnp.sum(keep * per_clip, axis=0, keepdims=True)
        kept = wide(coef_ref[1:2, HIDDEN:], CHANNELS // 128)
        d_logits = keep * (jnp.exp(log_prob) - target) / kept
        d_low = d_logits.astype(BF)
        grad = dot_tn(pooled_low.astype(F32), d_low.astype(F32)).astype(BF)
        half = grad.shape[0] // 2
        keep_grad_ref[...] = grad[:half]
        send_grad_ref[...] = grad[half:]
        d_pooled = dot_nt(d_low, head) / size
        dpool_ref[...] = d_pooled
        sums_one = jnp.sum(acc_ref[1] * d_pooled, axis=0, keepdims=True)
        sums_two = jnp.sum(acc_ref[2] * d_pooled, axis=0, keepdims=True)
        lane = lax.broadcasted_iota(jnp.int32, (1, CHANNELS), 1)
        parts = [
            to_owner_order(sums_one, order_ref[...]),
            to_owner_order(sums_two, order_ref[...]),
            jnp.where(lane < CLASSES, jnp.sum(d_logits, axis=0, keepdims=True), loss),
        ]
        spread_row(stats_ref, jnp.concatenate(parts, axis=1))


def first_back_kernel(
    count, frames, clips, recv_ref, two_ref, mask_ref, valid_ref, coef_ref, coef_two_ref, dpool_ref,
    order_ref, valid_out_ref, *refs
):
    convs, refs = refs[:3], refs[3:]
    pieces, refs = refs[:count], refs[count:]
    dtwo_ref, dpre_ref, stats_ref, total_ref, w_ref, dtwo_all, back_ref, acc_ref = refs
    step = pl.program_id(0)
    per = valid_ref.shape[0]

    @pl.when(step == 0)
    def _():
        at = 0
        for piece in pieces:
            rows = piece.shape[0]
            for t in range(3):
                w_ref[t * CHANNELS + at : t * CHANNELS + at + rows, :] = piece[
                    :, CHANNELS + t * HIDDEN : CHANNELS + (t + 1) * HIDDEN
                ]
            at += rows
        total = jnp.sum(recv_ref[...], axis=0)
        total_ref[...] = total
        each = wide(coef_ref[0:1, HIDDEN:], CHANNELS // 128)
        back_ref[0:1, :] = to_local_order(total[:, :CHANNELS], order_ref[...]) / each
        back_ref[1:2, :] = to_local_order(total[:, CHANNELS : 2 * CHANNELS], order_ref[...]) / each
        acc_ref[...] = jnp.zeros_like(acc_ref)

    @pl.when(step < frames)
    def _():
        valid = wide(valid_ref[...], CHANNELS // 128)
        gain = coef_two_ref[2:3, :]
        inverse = coef_two_ref[1:2, :]
        normed = (two_ref[...] - coef_two_ref[0:1, :]) * inverse
        mask = mask_ref[...].astype(F32)
        spread = jnp.broadcast_to(dpool_ref[...][None], (per // clips, clips, CHANNELS))
        d_pre = mask * spread.reshape(per, CHANNELS)
        low = (
            valid * (gain * inverse) * (d_pre - back_ref[0:1, :] - normed * back_ref[1:2, :])
        ).astype(BF)
        dtwo_ref[...] = low
        dtwo_all[pl.ds(pl.multiple_of(step * per, per), per), :] = low

    def frame(last, taps):
        pieces_at = [
            dtwo_all[pl.ds(pl.multiple_of(last - k * per, per), per), :] for k in range(len(taps))
        ]
        back = jnp.concatenate(pieces_at, axis=1)
        taps_rows = slice(taps[0] * CHANNELS, (taps[-1] + 1) * CHANNELS)
        for conv_ref, start, width in zip(convs, STARTS, WIDTHS, strict=True):
            lanes = slice(start, start + width)
            d_first = dot_nn(back, w_ref[taps_rows, lanes])
            normed = (conv_ref[...] - coef_ref[0:1, lanes]) * coef_ref[1:2, lanes]
            pre = coef_ref[2:3, lanes] * normed + coef_ref[3:4, lanes]
            d_pre = jnp.where(pre > 0.0, d_first, 0.0) * wide(valid_out_ref[...], width // 128)
            dpre_ref[:, lanes] = d_pre
            acc_ref[:, lanes] += fold(d_pre, 8)
            acc_ref[:, HIDDEN + start : HIDDEN + start + width] += fold(d_pre * normed, 8)

    @pl.when(step == 1)
    def _():
        frame(per, (0, 1))

    @pl.when(jnp.logical_and(step > 1, step < frames))
    def _():
        frame(step * per, (0, 1, 2))

    @pl.when(step == frames)
    def _():
        frame((frames - 1) * per, (1, 2))
        spread_row(stats_ref, jnp.sum(acc_ref[...], axis=0, keepdims=True))


def conv_back_kernel(
    recv_ref, conv_one, conv_two, conv_three, dpre_ref, valid_ref, coef_ref, out_ref, total_ref, back_ref
):
    @pl.when(pl.program_id(0) == 0)
    def _():
        total = jnp.sum(recv_ref[...], axis=0)
        total_ref[...] = total
        each = wide(coef_ref[0:1, HIDDEN:], HIDDEN // 128)
        back_ref[0:1, :] = total[:, :HIDDEN] / each
        back_ref[1:2, :] = total[:, HIDDEN:] / each

    for conv_ref, start, width in zip((conv_one, conv_two, conv_three), STARTS, WIDTHS, strict=True):
        lanes = slice(start, start + width)
        inverse = coef_ref[1:2, lanes]
        normed = (conv_ref[...] - coef_ref[0:1, lanes]) * inverse
        value = dpre_ref[:, lanes] - back_ref[0:1, lanes] - normed * back_ref[1:2, lanes]
        scale = coef_ref[2:3, lanes] * inverse
        out_ref[:, lanes] = (wide(valid_ref[...], width // 128) * scale * value).astype(BF)


def temporal_grad_kernel(per, dtwo_ref, first_ref, out_ref):
    rows = dtwo_ref.shape[0]

    def tap(low_out, low_in, size):
        left, right = dtwo_ref[low_out : low_out + size], first_ref[low_in : low_in + size]
        out_ref[...] = dot_tn(left, right).astype(BF)

    step = pl.program_id(0)
    pl.when(step == 0)(lambda: tap(per, 0, rows - per))
    pl.when(step == 1)(lambda: tap(0, 0, rows))
    pl.when(step == 2)(lambda: tap(0, per, rows - per))


def spatial_grad_kernel(tap_row, per, group, cols_ref, d_ref, out_ref):
    rows = d_ref.shape[0]
    if tap_row == 1:
        out_ref[...] = dot_tn(cols_ref[...], d_ref[...]).astype(BF)
        return
    left, right = (0, group) if tap_row == 0 else (group, 0)
    size = per - group
    cols = [cols_ref[f + left : f + left + size] for f in range(0, rows, per)]
    back = [d_ref[f + right : f + right + size] for f in range(0, rows, per)]
    grad = dot_tn(jnp.concatenate(cols, axis=0), jnp.concatenate(back, axis=0))
    out_ref[...] = grad.astype(BF)


def field_back_kernel(tap_col, per, group, clips, d_ref, *refs):
    weights, refs, sems = refs[:3], refs[3:-1], refs[-1]
    if tap_col == 1:
        out_ref, w_ref, pad_ref = refs
    elif tap_col == 0:
        acc_in_ref, out_ref, w_ref, pad_ref = refs
    else:
        (acc_in_ref, mask_ref, dpool_ref, valid_ref, x_ref, order_ref,
         out_ref, w_ref, pad_ref, grad_ref) = refs
    step = pl.program_id(0)

    @pl.when(step == 0)
    def _():
        copies = []
        for a in range(3):
            for j in range(3):
                copies.append(
                    pltpu.make_async_copy(
                        weights[j].at[pl.ds((3 * a + tap_col) * CHANNELS, CHANNELS), :],
                        w_ref.at[:, pl.ds(a * HIDDEN + STARTS[j], WIDTHS[j])],
                        sems.at[3 * a + j],
                    )
                )
        for copy in copies:
            copy.start()
        for copy in copies:
            copy.wait()
        pad_ref[:group] = jnp.zeros((group, HIDDEN), BF)
        pad_ref[group + per :] = jnp.zeros((group, HIDDEN), BF)

    pad_ref[group : group + per] = d_ref[...]
    left = jnp.concatenate(
        [pad_ref[(2 - a) * group : (2 - a) * group + per] for a in range(3)], axis=1
    )
    value = dot_nt(left, w_ref[...])
    if tap_col == 1:
        out_ref[...] = value
        return
    value = value.reshape(per // group, group, CHANNELS)
    edge = jnp.zeros((per // group, clips, CHANNELS), F32)
    if tap_col == 0:
        value = jnp.concatenate([value[:, clips:], edge], axis=1)
    else:
        value = jnp.concatenate([edge, value[:, : group - clips]], axis=1)
    value = acc_in_ref[...] + value.reshape(per, CHANNELS)
    if tap_col == 0:
        out_ref[...] = value
        return
    spread = jnp.broadcast_to(dpool_ref[...][None], (per // clips, clips, CHANNELS))
    value = value + mask_ref[...].astype(F32) * spread.reshape(per, CHANNELS)
    d_entry = (value * wide(valid_ref[...], CHANNELS // 128)).astype(BF)
    grad = dot_tn(d_entry, x_ref[...])

    @pl.when(step == 0)
    def _():
        grad_ref[...] = grad

    @pl.when(step > 0)
    def _():
        grad_ref[...] += grad

    @pl.when(step == pl.num_programs(0) - 1)
    def _():
        out_ref[...] = dot_tn(order_ref[...].astype(BF), grad_ref[...].astype(BF)).astype(BF)


def small_update_kernel(
    three_ref, four_ref, fix_ref, w_ref, first_ref, second_ref, w_out, first_out, second_out
):
    def part(lo, hi, grad):
        lanes = slice(lo, hi)
        w_out[:, lanes], first_out[:, lanes], second_out[:, lanes] = adamw(
            w_ref[:, lanes], grad, first_ref[:, lanes], second_ref[:, lanes],
            0.5, 0.0, fix_ref[:, :1],
        )

    at = 2 * HIDDEN
    part(0, HIDDEN, four_ref[:, HIDDEN:])
    part(HIDDEN, at, four_ref[:, :HIDDEN])
    part(at, at + CHANNELS, three_ref[:, CHANNELS : 2 * CHANNELS])
    part(at + CHANNELS, at + 2 * CHANNELS, three_ref[:, :CHANNELS])
    at += 2 * CHANNELS
    part(at, at + CLASSES, three_ref[:, 2 * CHANNELS : 2 * CHANNELS + CLASSES])


def wait_for(value, others):
    return lax.optimization_barrier((value, *others))[0]


def split_four(devices):
    def pairs(move):
        result = []
        for source in range(devices):
            z, x, core, y = source >> 3, (source >> 2) & 1, (source >> 1) & 1, source & 1
            z, x, core, y = move(z, x, core, y)
            result.append((source, ((z * 2 + x) * 2 + core) * 2 + y))
        return result

    along_z = [pairs(lambda z, x, c, y, k=k: ((z + k) % 4, x, c, y)) for k in range(4)]
    back_z = [pairs(lambda z, x, c, y, k=k: ((z - k) % 4, x, c, y)) for k in range(4)]
    early = pairs(lambda z, x, c, y: (z, 1 - x, c, y) if c == 0 else (z, x, c, 1 - y))
    late = pairs(lambda z, x, c, y: (z, x, c, 1 - y) if c == 0 else (z, 1 - x, c, y))
    core = pairs(lambda z, x, c, y: (z, x, 1 - c, y))
    return along_z, back_z, early, late, core


class Slice:
    def __init__(self, devices):
        self.devices = devices
        self.along_z, self.back_z, self.early, self.late, self.core = split_four(devices)

    def send(self, value, pairs):
        return lax.ppermute(value, AXES, pairs)

    def order(self, rows):
        channel = jnp.arange(CHANNELS)
        block, inside = channel // rows, channel % rows
        other, j, i, k = block >> 4, (block >> 3) & 1, (block >> 2) & 1, block & 3
        at, y = lax.axis_index("dp"), lax.axis_index("outer")
        core = (at & 1) ^ other
        x = ((at >> 1) & 1) ^ jnp.where(core == 0, i, j)
        y = y ^ jnp.where(core == 0, j, i)
        z = ((at >> 2) - k) & 3
        return (((z * 2 + x) * 2 + core) * 2 + y) * rows + inside

    def gather(self, shard, after=(), core_last=False):
        shard = wait_for(shard, after)
        if core_last:
            column = shard
            for k in (1, 2):
                came = self.send(column, self.along_z[k])
                after = yield
                column = jnp.concatenate([column, wait_for(came, after)], axis=0)
        else:
            came = [self.send(shard, self.along_z[k]) for k in (1, 2, 3)]
            after = yield
            column = jnp.concatenate([shard] + [wait_for(part, after) for part in came], axis=0)
        came = self.send(column, self.early)
        after = yield [column]
        half = jnp.concatenate([column, wait_for(came, after)], axis=0)
        rest = self.send(half, self.late)
        other = half if core_last else self.send(half, self.core)
        after = yield [half, other]
        rest = wait_for(rest, after)
        if core_last:
            other = self.send(wait_for(half, after), self.core)
        yield [half, rest, other, self.send(rest, self.core)]

    def add_halves(self, keep, came):
        half = keep.shape[0] // 2
        return keep[:half] + came[:half], keep[half:] + came[half:]

    def scatter(self, keep, send, extra=None):
        came = self.send(send, self.core)
        if extra is not None:
            came = jnp.concatenate([self.send(extra[1], self.core), came], axis=1)
        after = yield
        if extra is not None:
            keep = jnp.concatenate([extra[0], keep], axis=1)
        for pairs in (self.late, self.early, self.back_z[2], self.back_z[1]):
            keep, send = self.add_halves(keep, wait_for(came, after))
            came = self.send(send, pairs)
            after = yield [keep, send]
        yield [keep.astype(F32) + wait_for(came, after).astype(F32)]


class Plain:
    def __init__(self, devices):
        self.devices = devices

    def order(self, rows):
        return jnp.arange(CHANNELS)

    def gather(self, shard, after=(), core_last=False):
        result = [lax.all_gather(shard, AXES, axis=0, tiled=True)]
        yield
        if core_last:
            yield
        yield result
        yield [*result, *result]
        yield result

    def scatter(self, keep, send, extra=None):
        value = jnp.concatenate([keep, send], axis=0)
        if extra is not None:
            value = jnp.concatenate([jnp.concatenate(extra, axis=0), value], axis=1)
        result = [lax.psum_scatter(value.astype(F32), AXES, scatter_dimension=0, tiled=True)]
        while True:
            yield result


def share_rows(spread):
    return lax.all_to_all(spread, AXES, 0, 0)


def adamw(master, grad, first, second, rate, decay, correction):
    first_new = 0.5 * first + 0.5 * grad
    second_new = 0.5 * second + 0.5 * grad * grad
    master_new = master - rate * (
        first_new / correction / (jnp.sqrt(second_new / correction) + ADAM_EPS) + decay * master
    )
    return (master_new, first_new, second_new)


def on_device(
    links,
    clip_frames,
    valid_mask,
    labels,
    clip_keep,
    step_count,
    w_entry,
    w_spatial,
    w_temporal,
    w_head,
    small_params,
    entry_first,
    entry_second,
    spatial_first,
    spatial_second,
    temporal_first,
    temporal_second,
    head_first,
    head_second,
    small_first,
    small_second,
):
    clips, frames, height, breadth, _ = clip_frames.shape
    shard = w_spatial.shape[1]
    group = breadth * clips
    per = height * group
    rows = frames * per
    shape = jax.ShapeDtypeStruct

    def flat(taps):
        return taps.astype(BF).transpose(1, 0, 2).reshape(shard, -1)

    entry_t = w_entry.T
    temporal_t = w_temporal.transpose(0, 2, 1)
    head_pad = jnp.pad(w_head.astype(BF), ((0, 0), (0, CHANNELS - CLASSES)))
    index = links.order(shard)
    order = (index[:, None] == jnp.arange(CHANNELS)[None, :]).astype(F32)
    gain_one = small_params[None, :HIDDEN]
    shift_one = small_params[None, HIDDEN : 2 * HIDDEN]
    gain_two = small_params[None, 2 * HIDDEN : 2 * HIDDEN + CHANNELS]
    shift_two = small_params[None, 2 * HIDDEN + CHANNELS : 2 * HIDDEN + 2 * CHANNELS]
    bias = jnp.pad(
        small_params[None, 2 * HIDDEN + 2 * CHANNELS :],
        ((0, 0), (0, CHANNELS - CLASSES)),
        constant_values=-1e30,
    )
    x = clip_frames.transpose(1, 2, 3, 0, 4).reshape(rows, CHAN_IN)
    valid = valid_mask.astype(F32).transpose(1, 2, 3, 0)[..., None]
    valid = jnp.broadcast_to(valid, (*valid.shape[:4], 128)).reshape(rows, 128)
    keep = jnp.broadcast_to(clip_keep.astype(F32)[:, None], (clips, 128))
    lane = jnp.arange(CHANNELS)[None, :]
    target = jnp.where(
        lane < CLASSES,
        (1.0 - SMOOTHING) * (labels[:, None] == lane).astype(F32) + SMOOTHING / CLASSES,
        0.0,
    )

    fix = jnp.broadcast_to(1.0 - jnp.power(0.5, step_count[0].astype(F32)), (1, 128))
    small_rows = [small_params[None], small_first[None], small_second[None]]
    prepared = [order, gain_one, shift_one, gain_two, shift_two, bias, target, keep, fix]
    prepared += [*small_rows, x, valid]

    def part(j):
        return flat(w_spatial[:, :, STARTS[j] : STARTS[j] + WIDTHS[j]])

    load_mid = links.gather(jnp.concatenate([part(0), entry_t.astype(BF)], axis=1))
    next(load_mid)
    column_mid = load_mid.send([])
    load_top = links.gather(part(1), [*column_mid, *prepared])
    next(load_top)
    half_mid, other_mid = load_mid.send([])
    column_top = load_top.send([half_mid])
    load_low = links.gather(part(2), [*column_top, other_mid])
    next(load_low)
    head_time = jnp.concatenate([head_pad, flat(temporal_t)], axis=1)
    load_time = links.gather(head_time, [*column_top, other_mid], core_last=True)
    next(load_time)
    column_low = load_low.send([])
    ready = load_top.send(column_low)
    pieces_mid = load_mid.send([])
    count = len(pieces_mid)

    def at(width, where=lambda i: i):
        return pl.BlockSpec((per, width), lambda i: (where(i), 0))

    def piece_specs(pieces):
        return [whole(p.shape) for p in pieces]

    def now(i):
        return jnp.minimum(i, frames - 1)

    def before(i):
        return jnp.maximum(i - 1, 0)

    conv_flops = 2 * rows * 3 * CHANNELS * HIDDEN

    def sums(j):
        return result((8, 2 * WIDTHS[j])), shape((8, 2 * WIDTHS[j]), F32)

    def weights(j):
        return pltpu.HBM((9 * CHANNELS, WIDTHS[j]), BF)

    anywhere = pl.BlockSpec(memory_space=pl.ANY)
    field, cols, conv_one, sums_one, weights_one = call(
        functools.partial(entry_kernel, count, breadth, clips),
        "entry_and_first_range",
        (frames,),
        [at(CHAN_IN), at(128)] + piece_specs(pieces_mid),
        [at(CHANNELS), at(3 * CHANNELS), at(WIDTHS[0]), sums(0)[0], anywhere],
        [
            pltpu.HBM((rows, CHANNELS), F32),
            pltpu.HBM((rows, 3 * CHANNELS), BF),
            shape((rows, WIDTHS[0]), F32),
            sums(0)[1],
            weights(0),
        ],
        [
            pltpu.VMEM((9 * CHANNELS, WIDTHS[0]), BF),
            pltpu.VMEM((CHANNELS, CHAN_IN), BF),
            pltpu.SemaphoreType.DMA,
        ],
        vmem=24,
        flops=conv_flops,
        gates=[ready[0], *column_low],
    )(x, valid, *pieces_mid)
    ready = load_low.send([conv_one])
    pieces_top = load_top.send([conv_one])
    load_time.send([conv_one])
    conv_two, sums_two, weights_two = call(
        functools.partial(spatial_kernel, count, group),
        "second_range",
        (frames,),
        [at(3 * CHANNELS), at(128)] + piece_specs(pieces_top),
        [at(WIDTHS[1]), sums(1)[0], anywhere],
        [shape((rows, WIDTHS[1]), F32), sums(1)[1], weights(1)],
        [pltpu.VMEM((9 * CHANNELS, WIDTHS[1]), BF), pltpu.SemaphoreType.DMA],
        flops=conv_flops,
        gates=ready[:1],
    )(cols, valid, *pieces_top)
    pieces_low = load_low.send([conv_two])
    ready = load_time.send([conv_two])
    conv_three, stats, weights_three = call(
        functools.partial(last_spatial_kernel, count, group),
        "last_range",
        (frames,),
        [at(3 * CHANNELS), at(128), whole((clips, 128))]
        + [whole(sums_one.shape), whole(sums_two.shape)]
        + piece_specs(pieces_low),
        [at(WIDTHS[2]), result((links.devices, 1, 2 * HIDDEN + 256)), anywhere],
        [
            shape((rows, WIDTHS[2]), F32),
            shape((links.devices, 1, 2 * HIDDEN + 256), F32),
            weights(2),
        ],
        [
            pltpu.VMEM((9 * CHANNELS, WIDTHS[2]), BF),
            pltpu.VMEM((8, 2 * WIDTHS[2]), F32),
            pltpu.VMEM((8, 128), F32),
            pltpu.SemaphoreType.DMA,
        ],
        flops=conv_flops // 2,
        gates=ready[:1],
    )(cols, valid, keep, sums_one, sums_two, *pieces_low)
    ready = load_time.send([conv_three])
    convs = (conv_one, conv_two, conv_three)
    stats = wait_for(stats, ready[:1])
    all_stats = share_rows(stats)
    pieces_time = load_time.send([all_stats])

    first, two, stats_two, coef, head = call(
        functools.partial(temporal_kernel, count, frames),
        "norm_and_temporal",
        (frames + 1,),
        [whole(all_stats.shape)]
        + [at(width, now) for width in WIDTHS]
        + [at(128, now), at(128, before)]
        + [whole((1, HIDDEN))] * 2
        + [whole((CHANNELS, CHANNELS))]
        + piece_specs(pieces_time),
        [
            at(HIDDEN, now),
            at(CHANNELS, before),
            result((links.devices, 1, 2 * CHANNELS)),
            result((8, HIDDEN + 128)),
            result((CHANNELS, CHANNELS)),
        ],
        [
            pltpu.HBM((rows, HIDDEN), BF),
            shape((rows, CHANNELS), F32),
            shape((links.devices, 1, 2 * CHANNELS), F32),
            shape((8, HIDDEN + 128), F32),
            shape((CHANNELS, CHANNELS), BF),
        ],
        [
            pltpu.VMEM((CHANNELS, 3 * HIDDEN), BF),
            pltpu.VMEM((rows, HIDDEN), BF),
            pltpu.VMEM((8, 2 * CHANNELS), F32),
        ],
        vmem=26,
        flops=conv_flops,
    )(all_stats, *convs, valid, valid, gain_one, shift_one, order, *pieces_time)
    all_two = share_rows(stats_two)

    half = CHANNELS // 2
    mask, dpool, stats_three, coef_two, head_keep, head_send = call(
        functools.partial(head_kernel, clips),
        "norm_head_and_back",
        (frames,),
        [whole(all_two.shape), at(CHANNELS), at(CHANNELS), at(128), whole((8, HIDDEN + 128))]
        + [whole((1, CHANNELS))] * 2
        + [whole((CHANNELS, CHANNELS))] * 2
        + [whole((1, CHANNELS)), whole((clips, CHANNELS)), whole((clips, 128))],
        [
            at(CHANNELS),
            result((clips, CHANNELS)),
            result((links.devices, 1, 3 * CHANNELS)),
            result((8, CHANNELS)),
            result((half, CHANNELS)),
            result((half, CHANNELS)),
        ],
        [
            pltpu.HBM((rows, CHANNELS), BF),
            shape((clips, CHANNELS), F32),
            shape((links.devices, 1, 3 * CHANNELS), F32),
            shape((8, CHANNELS), F32),
            shape((half, CHANNELS), BF),
            shape((half, CHANNELS), BF),
        ],
        [pltpu.VMEM((3, clips, CHANNELS), F32), pltpu.VMEM((clips, 128), F32)],
    )(all_two, two, field, valid, coef, gain_two, shift_two, order, head, bias, target, keep)
    all_three = share_rows(stats_three)

    dtwo, dpre, stats_four, total_three = call(
        functools.partial(first_back_kernel, count, frames, clips),
        "temporal_back",
        (frames + 1,),
        [
            whole(all_three.shape),
            at(CHANNELS, now),
            at(CHANNELS, now),
            at(128, now),
            whole((8, HIDDEN + 128)),
            whole((8, CHANNELS)),
            whole((clips, CHANNELS)),
            whole((CHANNELS, CHANNELS)),
            at(128, before),
        ]
        + [at(width, before) for width in WIDTHS]
        + piece_specs(pieces_time),
        [at(CHANNELS, now), at(HIDDEN, before), result((links.devices, 1, 2 * HIDDEN)),
         result((1, 3 * CHANNELS))],
        [
            shape((rows, CHANNELS), BF),
            shape((rows, HIDDEN), F32),
            shape((links.devices, 1, 2 * HIDDEN), F32),
            shape((1, 3 * CHANNELS), F32),
        ],
        [
            pltpu.VMEM((3 * CHANNELS, HIDDEN), BF),
            pltpu.VMEM((rows, CHANNELS), BF),
            pltpu.VMEM((8, CHANNELS), F32),
            pltpu.VMEM((8, 2 * HIDDEN), F32),
        ],
        vmem=26,
        flops=conv_flops,
    )(all_three, two, mask, valid, coef, coef_two, dpool, order, valid, *convs, *pieces_time)
    all_four = share_rows(stats_four)

    taps_shape = shape((half, 3 * HIDDEN), BF)
    taps_spec = pl.BlockSpec((half, HIDDEN), lambda i: (0, i))

    def temporal_grad(part):
        return call(
            functools.partial(temporal_grad_kernel, per),
            "temporal_gradient",
            (3,),
            [pl.BlockSpec((rows, half), lambda i: (0, part)), whole((rows, HIDDEN))],
            taps_spec,
            taps_shape,
            flops=conv_flops // 2,
            gates=[all_four],
        )(dtwo, first)

    time_send = temporal_grad(1)
    time_keep = temporal_grad(0)

    scatter_time = links.scatter(time_keep, time_send, (head_keep, head_send))
    next(scatter_time)
    ready = scatter_time.send([time_keep])
    dconv, total_four = call(
        conv_back_kernel,
        "spatial_norm_back",
        (frames,),
        [whole(all_four.shape)]
        + [at(width) for width in WIDTHS]
        + [at(HIDDEN), at(128), whole((8, HIDDEN + 128))],
        [at(HIDDEN), result((1, 2 * HIDDEN))],
        [shape((rows, HIDDEN), BF), shape((1, 2 * HIDDEN), F32)],
        [pltpu.VMEM((8, HIDDEN), F32)],
        gates=ready,
    )(all_four, *convs, dpre, valid, coef)

    def spatial_grad(tap_row, part, gates):
        return call(
            functools.partial(spatial_grad_kernel, tap_row, per, group),
            "spatial_gradient",
            (3,),
            [pl.BlockSpec((rows, half), lambda i: (0, 2 * i + part)), whole((rows, HIDDEN))],
            taps_spec,
            taps_shape,
            flops=conv_flops // 2,
            gates=gates,
        )(cols, dconv)

    send = spatial_grad(1, 1, [])
    keep = spatial_grad(1, 0, [send])
    scatter_mid = links.scatter(keep, send)
    next(scatter_mid)
    ready = scatter_time.send([keep]) + scatter_mid.send([keep])
    send = spatial_grad(0, 1, ready)
    keep = spatial_grad(0, 0, [send])
    scatter_top = links.scatter(keep, send)
    next(scatter_top)
    ready = scatter_time.send([keep]) + scatter_mid.send([keep]) + scatter_top.send([keep])
    send = spatial_grad(2, 1, ready)
    keep = spatial_grad(2, 0, [send])
    scatter_low = links.scatter(keep, send)
    next(scatter_low)
    ready = scatter_time.send([keep]) + scatter_mid.send([keep])
    ready += scatter_top.send([keep]) + scatter_low.send([keep])

    def field_back(tap_col, gates, extra, extra_specs, out_spec, out_shape, scratch=()):
        return call(
            functools.partial(field_back_kernel, tap_col, per, group, clips),
            "field_back",
            (frames,),
            [at(HIDDEN)]
            + [anywhere] * 3
            + extra_specs,
            out_spec,
            out_shape,
            [
                pltpu.VMEM((CHANNELS, 3 * HIDDEN), BF),
                pltpu.VMEM((per + 2 * group, HIDDEN), BF),
                *scratch,
                pltpu.SemaphoreType.DMA((9,)),
            ],
            flops=conv_flops,
            gates=gates,
        )(dconv, weights_one, weights_two, weights_three, *extra)

    partial = pltpu.HBM((rows, CHANNELS), F32)
    back = field_back(1, ready, [], [], at(CHANNELS), partial)
    time_share = scatter_time.send([back])
    ready = scatter_mid.send([back]) + scatter_top.send([back]) + scatter_low.send([back])
    back = field_back(0, ready, [back], [at(CHANNELS)], at(CHANNELS), partial)
    share_mid = scatter_mid.send([back])
    ready = scatter_top.send([back]) + scatter_low.send([back])
    grad_entry = field_back(
        2,
        ready,
        [back, mask, dpool, valid, x, order],
        [
            at(CHANNELS),
            at(CHANNELS),
            whole((clips, CHANNELS)),
            at(128),
            at(CHAN_IN),
            whole((CHANNELS, CHANNELS)),
        ],
        result((CHANNELS, CHAN_IN)),
        shape((CHANNELS, CHAN_IN), BF),
        [pltpu.VMEM((CHANNELS, CHAN_IN), F32)],
    )
    entry_parts = lax.all_to_all(grad_entry.reshape(links.devices, shard, CHAN_IN), AXES, 0, 0)
    entry_share = jnp.sum(entry_parts.astype(F32), axis=0)
    share_top = scatter_top.send([grad_entry])
    scatter_low.send([grad_entry])
    share_low = scatter_low.send([])

    def taps(share):
        return share.reshape(shard, 3, HIDDEN).transpose(1, 0, 2)

    correction = fix[0, 0]
    total_three = wait_for(total_three, [grad_entry])
    loss = total_three[0, 2 * CHANNELS + CLASSES] / coef[1, HIDDEN]
    small_shape = shape(small_rows[0].shape, F32)
    small_out = call(
        small_update_kernel,
        "small_update",
        (),
        [whole(total_three.shape), whole(total_four.shape), whole(fix.shape)]
        + [whole(small_shape.shape)] * 3,
        [result(small_shape.shape)] * 3,
        [small_shape] * 3,
    )(total_three, total_four, fix, *small_rows)
    small_out = [row[0] for row in small_out]
    spatial_grad_share = jnp.concatenate(
        [taps(share[0]) for share in (share_top, share_mid, share_low)], axis=0
    )
    time_share = time_share[0]
    temporal_share = taps(time_share[:, CHANNELS:]).transpose(0, 2, 1)
    entry_out = adamw(
        w_entry, entry_share.T, entry_first, entry_second, 0.06, DECAY_RATE, correction
    )
    spatial_out = adamw(
        w_spatial, spatial_grad_share, spatial_first, spatial_second, 0.02, DECAY_RATE, correction
    )
    temporal_out = adamw(
        w_temporal, temporal_share, temporal_first, temporal_second, 0.02, DECAY_RATE, correction
    )
    head_out = adamw(
        w_head, time_share[:, :CLASSES], head_first, head_second, 0.05, DECAY_RATE, correction
    )
    return (
        loss,
        *entry_out,
        *spatial_out,
        *temporal_out,
        *head_out,
        *small_out,
        entry_out[0].astype(BF),
        spatial_out[0].astype(BF),
        temporal_out[0].astype(BF),
        head_out[0].astype(BF),
    )


def solution(mesh):
    devices = mesh.shape["dp"] * mesh.shape["outer"]
    small_slice = mesh.shape["dp"] == 16 and mesh.shape["outer"] == 2
    links = Slice(devices) if small_slice else Plain(devices)
    both = ("dp", "outer")
    entry, spatial, temporal, head = (
        P(None, both),
        P(None, both, None),
        P(None, None, both),
        P(both, None),
    )
    placed = (
        P(both, None, None, None, None),
        P(both, None, None, None),
        P(both),
        P(both),
        P(),
        entry,
        spatial,
        temporal,
        head,
        P(),
        entry,
        entry,
        spatial,
        spatial,
        temporal,
        temporal,
        head,
        head,
        P(),
        P(),
    )
    return jax.shard_map(
        functools.partial(on_device, links),
        mesh=mesh,
        in_specs=placed,
        out_specs=(
            P(),
            *([entry] * 3),
            *([spatial] * 3),
            *([temporal] * 3),
            *([head] * 3),
            P(),
            P(),
            P(),
            entry,
            spatial,
            temporal,
            head,
        ),
        check_vma=False,
    )
```

```python
import functools

import jax
import jax.numpy as jnp
from jax import lax
from jax.experimental import pallas as pl
from jax.experimental.pallas import tpu as pltpu
from jax.sharding import PartitionSpec as P

CHANNELS = 512
HIDDEN = 1152
CLASSES = 400
CHAN_IN = 256
WIDTHS = (384, 512, 256)
STARTS = (0, 384, 896)

EPSILON = 1e-05
ADAM_EPS = 1e-08
DECAY_RATE = 0.1
SMOOTHING = 0.1

AXES = ("dp", "outer")
BF = jnp.bfloat16
F32 = jnp.float32
MIB = 1 << 20


def wide(column, times):
    return jnp.concatenate([column] * times, axis=1)


def dot_nn(left, right):
    return lax.dot_general(left, right, (((1,), (0,)), ((), ())), preferred_element_type=F32)


def dot_nt(left, right):
    return lax.dot_general(left, right, (((1,), (1,)), ((), ())), preferred_element_type=F32)


def dot_tn(left, right):
    return lax.dot_general(left, right, (((0,), (0,)), ((), ())), preferred_element_type=F32)


def reorder(rows, order, axis):
    value = jnp.concatenate(
        rows + [jnp.zeros((8 - len(rows), rows[0].shape[1]), F32)], axis=0
    )
    high = value.astype(BF).astype(F32)
    middle = (value - high).astype(BF).astype(F32)
    low = value - high - middle
    parts = jnp.concatenate([high, middle, low], axis=0).astype(BF)
    moved = lax.dot_general(parts, order, (((1,), (axis,)), ((), ())), preferred_element_type=F32)
    moved = moved[:8] + moved[8:16] + moved[16:]
    return [moved[k : k + 1] for k in range(len(rows))]


def to_owner_order(rows, order):
    return reorder(rows, order, 0)


def to_local_order(rows, order):
    return reorder(rows, order, 1)


def fold(value, step):
    return jnp.sum(value.reshape(value.shape[0] // step, step, value.shape[1]), axis=0)


def spread_row(ref, row):
    ref[...] = jnp.broadcast_to(row[None], ref.shape)


def far(value):
    return pltpu.with_memory_space_constraint(value, pltpu.HBM)


def whole(shape):
    return pl.BlockSpec(shape, lambda *_: (0,) * len(shape), pipeline_mode=pl.Buffered(1))


def result(shape):
    return pl.BlockSpec(shape, lambda *_: (0,) * len(shape))


def call(
    kernel, name, grid, in_specs, out_specs, out_shape, scratch=(), aliases=None, vmem=22, flops=0,
    gates=(), moved=20 * MIB,
):
    first, last = len(in_specs), len(in_specs) + len(gates)

    def gated(*refs):
        kernel(*refs[:first], *refs[last:])

    run = pl.pallas_call(
        gated,
        name=name,
        grid=grid,
        in_specs=list(in_specs) + [pl.BlockSpec(memory_space=pl.ANY)] * len(gates),
        out_specs=out_specs,
        out_shape=out_shape,
        scratch_shapes=list(scratch),
        input_output_aliases=aliases or {},
        compiler_params=pltpu.CompilerParams(vmem_limit_bytes=vmem * MIB),
        cost_estimate=pl.CostEstimate(flops=flops, bytes_accessed=moved, transcendentals=0),
    )
    return lambda *operands: run(*operands, *gates)


def fill_taps(pieces, w_ref):
    width = w_ref.shape[1]
    at = 0
    for piece in pieces:
        rows = piece.shape[0]
        for tap in range(9):
            w_ref[tap * CHANNELS + at : tap * CHANNELS + at + rows, :] = piece[
                :, tap * width : (tap + 1) * width
            ]
        at += rows


def save(w_ref, w_out, sem, step):
    copy = pltpu.make_async_copy(w_ref, w_out, sem)
    pl.when(step == 0)(copy.start)
    pl.when(step == pl.num_programs(0) - 1)(copy.wait)


def spatial_taps(group, cols_ref, w_ref, conv_ref):
    rows, depth = cols_ref.shape
    conv_ref[...] = dot_nn(cols_ref[...], w_ref[depth : 2 * depth])
    conv_ref[group:] += dot_nn(cols_ref[: rows - group], w_ref[:depth])
    conv_ref[: rows - group] += dot_nn(cols_ref[group:], w_ref[2 * depth :])


def add_sums(conv_ref, valid_ref, acc_ref):
    value = conv_ref[...]
    width = value.shape[1]
    kept = value * wide(valid_ref[...], width // 128)
    acc_ref[:, :width] += fold(kept, 8)
    acc_ref[:, width:] += fold(kept * value, 8)


def entry_kernel(count, side, clips, x_ref, valid_ref, *refs):
    pieces, refs = refs[:count], refs[count:]
    field_ref, cols_ref, late_ref, conv_ref, acc_ref, w_out, w_ref, e_ref, sem = refs

    @pl.when(pl.program_id(0) == 0)
    def _():
        fill_taps(pieces, w_ref)
        at = 0
        for piece in pieces:
            rows = piece.shape[0]
            e_ref[at : at + rows, :] = piece[:, 9 * w_ref.shape[1] :]
            at += rows
        acc_ref[...] = jnp.zeros_like(acc_ref)

    save(w_ref, w_out, sem, pl.program_id(0))
    value = dot_nt(x_ref[...], e_ref[...]) * wide(valid_ref[...], CHANNELS // 128)
    field_ref[...] = value
    rows = value.shape[0]
    group = side * clips
    grid3 = value.reshape(rows // group, group, CHANNELS)
    edge = jnp.zeros((rows // group, clips, CHANNELS), F32)
    left = jnp.concatenate([edge, grid3[:, : group - clips]], axis=1).reshape(rows, CHANNELS)
    right = jnp.concatenate([grid3[:, clips:], edge], axis=1).reshape(rows, CHANNELS)
    cols_ref[:, :CHANNELS] = left.astype(BF)
    cols_ref[:, CHANNELS : 2 * CHANNELS] = value.astype(BF)
    cols_ref[:, 2 * CHANNELS :] = right.astype(BF)
    late_ref[...] = cols_ref[...]
    spatial_taps(group, cols_ref, w_ref, conv_ref)
    add_sums(conv_ref, valid_ref, acc_ref)


def spatial_kernel(count, group, cols_ref, valid_ref, *refs):
    pieces, (conv_ref, acc_ref, w_out, w_ref, sem) = refs[:count], refs[count:]

    @pl.when(pl.program_id(0) == 0)
    def _():
        fill_taps(pieces, w_ref)
        acc_ref[...] = jnp.zeros_like(acc_ref)

    save(w_ref, w_out, sem, pl.program_id(0))
    spatial_taps(group, cols_ref, w_ref, conv_ref)
    add_sums(conv_ref, valid_ref, acc_ref)


def last_spatial_kernel(count, group, cols_ref, valid_ref, keep_ref, one_ref, two_ref, *refs):
    pieces, refs = refs[:count], refs[count:]
    conv_ref, stats_ref, w_out, w_ref, acc_ref, size_ref, sem = refs
    step = pl.program_id(0)

    @pl.when(step == 0)
    def _():
        fill_taps(pieces, w_ref)
        acc_ref[...] = jnp.zeros_like(acc_ref)
        size_ref[...] = jnp.zeros_like(size_ref)

    save(w_ref, w_out, sem, step)
    spatial_taps(group, cols_ref, w_ref, conv_ref)
    add_sums(conv_ref, valid_ref, acc_ref)
    size_ref[...] += fold(valid_ref[...], 8)

    @pl.when(step == pl.num_programs(0) - 1)
    def _():
        parts = (one_ref, two_ref, acc_ref)
        sums = [part[:, : part.shape[1] // 2] for part in parts]
        squares = [part[:, part.shape[1] // 2 :] for part in parts]
        line = jnp.concatenate(sums + squares + [size_ref[...], fold(keep_ref[...], 8)], axis=1)
        spread_row(stats_ref, jnp.sum(line, axis=0, keepdims=True))


def temporal_kernel(
    count, frames, recv_ref, *refs
):
    convs, (valid_ref, valid_out_ref, gain_ref, shift_ref, order_ref), refs = (
        refs[:3], refs[3:8], refs[8:]
    )
    pieces, refs = refs[:count], refs[count:]
    first_ref, two_ref, stats_ref, coef_ref, head_ref, w_ref, first_all, acc_ref = refs
    step = pl.program_id(0)
    per = valid_ref.shape[0]

    @pl.when(step == 0)
    def _():
        at = 0
        for piece in pieces:
            rows = piece.shape[0]
            head_ref[at : at + rows, :] = piece[:, :CHANNELS]
            w_ref[at : at + rows, :] = piece[:, CHANNELS:]
            at += rows
        total = jnp.sum(recv_ref[...], axis=0)
        count_all = total[:, 2 * HIDDEN : 2 * HIDDEN + 128]
        wide_count = wide(count_all, HIDDEN // 128)
        mean = total[:, :HIDDEN] / wide_count
        variance = total[:, HIDDEN : 2 * HIDDEN] / wide_count - mean * mean
        coef_ref[...] = jnp.zeros_like(coef_ref)
        coef_ref[0:1, :HIDDEN] = mean
        coef_ref[1:2, :HIDDEN] = lax.rsqrt(variance + EPSILON)
        coef_ref[2:3, :HIDDEN] = gain_ref[...]
        coef_ref[3:4, :HIDDEN] = shift_ref[...]
        coef_ref[0:1, HIDDEN:] = count_all
        coef_ref[1:2, HIDDEN:] = total[:, 2 * HIDDEN + 128 :]
        acc_ref[...] = jnp.zeros_like(acc_ref)

    @pl.when(step < frames)
    def _():
        for conv_ref, start, width in zip(convs, STARTS, WIDTHS, strict=True):
            lanes = slice(start, start + width)
            normed = (conv_ref[...] - coef_ref[0:1, lanes]) * coef_ref[1:2, lanes]
            pre = coef_ref[2:3, lanes] * normed + coef_ref[3:4, lanes]
            first = (jnp.maximum(pre, 0.0) * wide(valid_ref[...], width // 128)).astype(BF)
            first_ref[:, lanes] = first
            first_all[pl.ds(pl.multiple_of(step * per, per), per), lanes] = first

    def frame(start, taps):
        pieces_at = [
            first_all[pl.ds(pl.multiple_of(start + k * per, per), per), :] for k in range(len(taps))
        ]
        lanes = slice(taps[0] * HIDDEN, (taps[-1] + 1) * HIDDEN)
        value = dot_nt(jnp.concatenate(pieces_at, axis=1), w_ref[:, lanes])
        two_ref[...] = value
        kept = value * wide(valid_out_ref[...], CHANNELS // 128)
        acc_ref[:, :CHANNELS] += fold(kept, 8)
        acc_ref[:, CHANNELS:] += fold(kept * value, 8)

    @pl.when(step == 1)
    def _():
        frame(0, (1, 2))

    @pl.when(jnp.logical_and(step > 1, step < frames))
    def _():
        frame((step - 2) * per, (0, 1, 2))

    @pl.when(step == frames)
    def _():
        frame((frames - 2) * per, (0, 1))
        sums = jnp.sum(acc_ref[...], axis=0, keepdims=True)
        parts = to_owner_order([sums[:, :CHANNELS], sums[:, CHANNELS:]], order_ref[...])
        spread_row(stats_ref, jnp.concatenate(parts, axis=1))


def head_kernel(
    clips, recv_ref, two_ref, field_ref, valid_ref, coef_ref, gain_ref, shift_ref, order_ref,
    head_ref, bias_ref, target_ref, keep_ref,
    mask_ref, dpool_ref, stats_ref, coef_two_ref, keep_grad_ref, send_grad_ref, acc_ref, size_ref,
):
    step = pl.program_id(0)

    @pl.when(step == 0)
    def _():
        total = jnp.sum(recv_ref[...], axis=0)
        count = wide(coef_ref[0:1, HIDDEN:], CHANNELS // 128)
        mean, square, gain, shift = to_local_order(
            [total[:, :CHANNELS] / count, total[:, CHANNELS:] / count, gain_ref[...], shift_ref[...]],
            order_ref[...],
        )
        coef_two_ref[...] = jnp.zeros_like(coef_two_ref)
        coef_two_ref[0:1, :] = mean
        coef_two_ref[1:2, :] = lax.rsqrt(square - mean * mean + EPSILON)
        coef_two_ref[2:3, :] = gain
        coef_two_ref[3:4, :] = shift
        acc_ref[...] = jnp.zeros_like(acc_ref)
        size_ref[...] = jnp.zeros_like(size_ref)

    valid = wide(valid_ref[...], CHANNELS // 128)
    normed = (two_ref[...] - coef_two_ref[0:1, :]) * coef_two_ref[1:2, :]
    pre = coef_two_ref[2:3, :] * normed + coef_two_ref[3:4, :] + field_ref[...]
    mask = jnp.where(pre > 0.0, valid, 0.0)
    mask_ref[...] = mask.astype(BF)
    acc_ref[0] += fold(jnp.maximum(pre, 0.0) * valid, clips)
    acc_ref[1] += fold(mask, clips)
    acc_ref[2] += fold(mask * normed, clips)
    size_ref[...] += fold(valid_ref[...], clips)

    @pl.when(step == pl.num_programs(0) - 1)
    def _():
        size = wide(size_ref[...], CHANNELS // 128)
        pooled_low = (acc_ref[0] / size).astype(BF)
        head = head_ref[...]
        logits = dot_nn(pooled_low, head) + bias_ref[...]
        shifted = logits - jnp.max(logits, axis=1, keepdims=True)
        log_prob = shifted - jnp.log(jnp.sum(jnp.exp(shifted), axis=1, keepdims=True))
        target = target_ref[...]
        per_clip = -jnp.sum(target * log_prob, axis=1, keepdims=True)
        keep = wide(keep_ref[...], CHANNELS // 128)
        loss = jnp.sum(keep * per_clip, axis=0, keepdims=True)
        kept = wide(coef_ref[1:2, HIDDEN:], CHANNELS // 128)
        d_logits = keep * (jnp.exp(log_prob) - target) / kept
        d_low = d_logits.astype(BF)
        grad = dot_tn(pooled_low.astype(F32), d_low.astype(F32)).astype(BF)
        half = grad.shape[0] // 2
        keep_grad_ref[...] = grad[:half]
        send_grad_ref[...] = grad[half:]
        d_pooled = dot_nt(d_low, head) / size
        dpool_ref[...] = d_pooled
        sums_one = jnp.sum(acc_ref[1] * d_pooled, axis=0, keepdims=True)
        sums_two = jnp.sum(acc_ref[2] * d_pooled, axis=0, keepdims=True)
        lane = lax.broadcasted_iota(jnp.int32, (1, CHANNELS), 1)
        parts = to_owner_order([sums_one, sums_two], order_ref[...]) + [
            jnp.where(lane < CLASSES, jnp.sum(d_logits, axis=0, keepdims=True), loss),
        ]
        spread_row(stats_ref, jnp.concatenate(parts, axis=1))


def first_back_kernel(
    count, frames, clips, recv_ref, two_ref, mask_ref, valid_ref, coef_ref, coef_two_ref, dpool_ref,
    order_ref, valid_out_ref, *refs
):
    convs, refs = refs[:3], refs[3:]
    pieces, refs = refs[:count], refs[count:]
    dtwo_ref, dpre_ref, stats_ref, total_ref, w_ref, dtwo_all, back_ref, acc_ref = refs
    step = pl.program_id(0)
    per = valid_ref.shape[0]

    @pl.when(step == 0)
    def _():
        at = 0
        for piece in pieces:
            rows = piece.shape[0]
            for t in range(3):
                w_ref[t * CHANNELS + at : t * CHANNELS + at + rows, :] = piece[
                    :, CHANNELS + t * HIDDEN : CHANNELS + (t + 1) * HIDDEN
                ]
            at += rows
        total = jnp.sum(recv_ref[...], axis=0)
        total_ref[...] = total
        each = wide(coef_ref[0:1, HIDDEN:], CHANNELS // 128)
        back_ref[0:1, :], back_ref[1:2, :] = to_local_order(
            [total[:, :CHANNELS] / each, total[:, CHANNELS : 2 * CHANNELS] / each], order_ref[...]
        )
        acc_ref[...] = jnp.zeros_like(acc_ref)

    @pl.when(step < frames)
    def _():
        valid = wide(valid_ref[...], CHANNELS // 128)
        gain = coef_two_ref[2:3, :]
        inverse = coef_two_ref[1:2, :]
        normed = (two_ref[...] - coef_two_ref[0:1, :]) * inverse
        mask = mask_ref[...].astype(F32)
        spread = jnp.broadcast_to(dpool_ref[...][None], (per // clips, clips, CHANNELS))
        d_pre = mask * spread.reshape(per, CHANNELS)
        low = (
            valid * (gain * inverse) * (d_pre - back_ref[0:1, :] - normed * back_ref[1:2, :])
        ).astype(BF)
        dtwo_ref[...] = low
        dtwo_all[pl.ds(pl.multiple_of(step * per, per), per), :] = low

    def frame(last, taps):
        pieces_at = [
            dtwo_all[pl.ds(pl.multiple_of(last - k * per, per), per), :] for k in range(len(taps))
        ]
        back = jnp.concatenate(pieces_at, axis=1)
        taps_rows = slice(taps[0] * CHANNELS, (taps[-1] + 1) * CHANNELS)
        for conv_ref, start, width in zip(convs, STARTS, WIDTHS, strict=True):
            lanes = slice(start, start + width)
            d_first = dot_nn(back, w_ref[taps_rows, lanes])
            normed = (conv_ref[...] - coef_ref[0:1, lanes]) * coef_ref[1:2, lanes]
            pre = coef_ref[2:3, lanes] * normed + coef_ref[3:4, lanes]
            d_pre = jnp.where(pre > 0.0, d_first, 0.0) * wide(valid_out_ref[...], width // 128)
            dpre_ref[:, lanes] = d_pre
            acc_ref[:, lanes] += fold(d_pre, 8)
            acc_ref[:, HIDDEN + start : HIDDEN + start + width] += fold(d_pre * normed, 8)

    @pl.when(step == 1)
    def _():
        frame(per, (0, 1))

    @pl.when(jnp.logical_and(step > 1, step < frames))
    def _():
        frame(step * per, (0, 1, 2))

    @pl.when(step == frames)
    def _():
        frame((frames - 1) * per, (1, 2))
        spread_row(stats_ref, jnp.sum(acc_ref[...], axis=0, keepdims=True))


def conv_back_kernel(
    recv_ref, conv_one, conv_two, conv_three, dpre_ref, valid_ref, coef_ref, out_ref, total_ref, back_ref
):
    @pl.when(pl.program_id(0) == 0)
    def _():
        total = jnp.sum(recv_ref[...], axis=0)
        total_ref[...] = total
        each = wide(coef_ref[0:1, HIDDEN:], HIDDEN // 128)
        back_ref[0:1, :] = total[:, :HIDDEN] / each
        back_ref[1:2, :] = total[:, HIDDEN:] / each

    for conv_ref, start, width in zip((conv_one, conv_two, conv_three), STARTS, WIDTHS, strict=True):
        lanes = slice(start, start + width)
        inverse = coef_ref[1:2, lanes]
        normed = (conv_ref[...] - coef_ref[0:1, lanes]) * inverse
        value = dpre_ref[:, lanes] - back_ref[0:1, lanes] - normed * back_ref[1:2, lanes]
        scale = coef_ref[2:3, lanes] * inverse
        out_ref[:, lanes] = (wide(valid_ref[...], width // 128) * scale * value).astype(BF)


def temporal_grad_kernel(per, dtwo_ref, first_ref, out_ref):
    rows = dtwo_ref.shape[0]

    def tap(low_out, low_in, size):
        left, right = dtwo_ref[low_out : low_out + size], first_ref[low_in : low_in + size]
        out_ref[...] = dot_tn(left, right).astype(BF)

    step = pl.program_id(0)
    pl.when(step == 0)(lambda: tap(per, 0, rows - per))
    pl.when(step == 1)(lambda: tap(0, 0, rows))
    pl.when(step == 2)(lambda: tap(0, per, rows - per))


def spatial_grad_kernel(tap_row, per, group, cols_ref, d_ref, out_ref):
    rows = d_ref.shape[0]
    if tap_row == 1:
        out_ref[...] = dot_tn(cols_ref[...], d_ref[...]).astype(BF)
        return
    left, right = (0, group) if tap_row == 0 else (group, 0)
    size = per - group
    cols = [cols_ref[f + left : f + left + size] for f in range(0, rows, per)]
    back = [d_ref[f + right : f + right + size] for f in range(0, rows, per)]
    grad = dot_tn(jnp.concatenate(cols, axis=0), jnp.concatenate(back, axis=0))
    out_ref[...] = grad.astype(BF)


def field_back_kernel(tap_col, per, group, clips, d_ref, *refs):
    weights, refs, sems = refs[:3], refs[3:-1], refs[-1]
    if tap_col == 1:
        out_ref, w_ref, pad_ref = refs
    elif tap_col == 0:
        acc_in_ref, out_ref, w_ref, pad_ref = refs
    else:
        (acc_in_ref, mask_ref, dpool_ref, valid_ref, x_ref, order_ref,
         out_ref, w_ref, pad_ref, grad_ref) = refs
    step = pl.program_id(0)

    @pl.when(step == 0)
    def _():
        copies = []
        for a in range(3):
            for j in range(3):
                copies.append(
                    pltpu.make_async_copy(
                        weights[j].at[pl.ds((3 * a + tap_col) * CHANNELS, CHANNELS), :],
                        w_ref.at[:, pl.ds(a * HIDDEN + STARTS[j], WIDTHS[j])],
                        sems.at[3 * a + j],
                    )
                )
        for copy in copies:
            copy.start()
        for copy in copies:
            copy.wait()
        pad_ref[:group] = jnp.zeros((group, HIDDEN), BF)
        pad_ref[group + per :] = jnp.zeros((group, HIDDEN), BF)

    pad_ref[group : group + per] = d_ref[...]
    left = jnp.concatenate(
        [pad_ref[(2 - a) * group : (2 - a) * group + per] for a in range(3)], axis=1
    )
    value = dot_nt(left, w_ref[...])
    if tap_col == 1:
        out_ref[...] = value
        return
    value = value.reshape(per // group, group, CHANNELS)
    edge = jnp.zeros((per // group, clips, CHANNELS), F32)
    if tap_col == 0:
        value = jnp.concatenate([value[:, clips:], edge], axis=1)
    else:
        value = jnp.concatenate([edge, value[:, : group - clips]], axis=1)
    value = acc_in_ref[...] + value.reshape(per, CHANNELS)
    if tap_col == 0:
        out_ref[...] = value
        return
    spread = jnp.broadcast_to(dpool_ref[...][None], (per // clips, clips, CHANNELS))
    value = value + mask_ref[...].astype(F32) * spread.reshape(per, CHANNELS)
    d_entry = (value * wide(valid_ref[...], CHANNELS // 128)).astype(BF)
    grad = dot_tn(d_entry, x_ref[...])

    @pl.when(step == 0)
    def _():
        grad_ref[...] = grad

    @pl.when(step > 0)
    def _():
        grad_ref[...] += grad

    @pl.when(step == pl.num_programs(0) - 1)
    def _():
        out_ref[...] = dot_tn(order_ref[...], grad_ref[...].astype(BF)).astype(BF)


def small_update_kernel(
    three_ref, four_ref, fix_ref, w_ref, first_ref, second_ref, w_out, first_out, second_out
):
    def part(lo, hi, grad):
        lanes = slice(lo, hi)
        w_out[:, lanes], first_out[:, lanes], second_out[:, lanes] = adamw(
            w_ref[:, lanes], grad, first_ref[:, lanes], second_ref[:, lanes],
            0.5, 0.0, fix_ref[:, :1],
        )

    at = 2 * HIDDEN
    part(0, HIDDEN, four_ref[:, HIDDEN:])
    part(HIDDEN, at, four_ref[:, :HIDDEN])
    part(at, at + CHANNELS, three_ref[:, CHANNELS : 2 * CHANNELS])
    part(at + CHANNELS, at + 2 * CHANNELS, three_ref[:, :CHANNELS])
    at += 2 * CHANNELS
    part(at, at + CLASSES, three_ref[:, 2 * CHANNELS : 2 * CHANNELS + CLASSES])


def wait_for(value, others):
    return lax.optimization_barrier((value, *others))[0]


def split_four(devices):
    def pairs(move):
        result = []
        for source in range(devices):
            z, x, core, y = source >> 3, (source >> 2) & 1, (source >> 1) & 1, source & 1
            z, x, core, y = move(z, x, core, y)
            result.append((source, ((z * 2 + x) * 2 + core) * 2 + y))
        return result

    along_z = [pairs(lambda z, x, c, y, k=k: ((z + k) % 4, x, c, y)) for k in range(4)]
    back_z = [pairs(lambda z, x, c, y, k=k: ((z - k) % 4, x, c, y)) for k in range(4)]
    early = pairs(lambda z, x, c, y: (z, 1 - x, c, y) if c == 0 else (z, x, c, 1 - y))
    late = pairs(lambda z, x, c, y: (z, x, c, 1 - y) if c == 0 else (z, 1 - x, c, y))
    core = pairs(lambda z, x, c, y: (z, x, 1 - c, y))
    return along_z, back_z, early, late, core


class Slice:
    def __init__(self, devices):
        self.devices = devices
        self.along_z, self.back_z, self.early, self.late, self.core = split_four(devices)

    def send(self, value, pairs):
        return lax.ppermute(value, AXES, pairs)

    def order(self, rows):
        channel = jnp.arange(CHANNELS)
        block, inside = channel // rows, channel % rows
        other, j, i, k = block >> 4, (block >> 3) & 1, (block >> 2) & 1, block & 3
        at, y = lax.axis_index("dp"), lax.axis_index("outer")
        core = (at & 1) ^ other
        x = ((at >> 1) & 1) ^ jnp.where(core == 0, i, j)
        y = y ^ jnp.where(core == 0, j, i)
        z = ((at >> 2) - k) & 3
        return (((z * 2 + x) * 2 + core) * 2 + y) * rows + inside

    def gather(self, shard, after=(), core_last=False):
        shard = wait_for(shard, after)
        if core_last:
            column = shard
            for k in (1, 2):
                came = self.send(column, self.along_z[k])
                after = yield
                column = jnp.concatenate([column, wait_for(came, after)], axis=0)
        else:
            came = [self.send(shard, self.along_z[k]) for k in (1, 2, 3)]
            after = yield
            column = jnp.concatenate([shard] + [wait_for(part, after) for part in came], axis=0)
        came = self.send(column, self.early)
        after = yield [column]
        half = jnp.concatenate([column, wait_for(came, after)], axis=0)
        rest = self.send(half, self.late)
        other = half if core_last else self.send(half, self.core)
        after = yield [half, other]
        rest = wait_for(rest, after)
        if core_last:
            other = self.send(wait_for(half, after), self.core)
        yield [half, rest, other, self.send(rest, self.core)]

    def add_halves(self, keep, came):
        half = keep.shape[0] // 2
        return keep[:half] + came[:half], keep[half:] + came[half:]

    def scatter(self, keep, send, extra=None):
        came = self.send(send, self.core)
        if extra is not None:
            came = jnp.concatenate([self.send(extra[1], self.core), came], axis=1)
        after = yield
        if extra is not None:
            keep = jnp.concatenate([extra[0], keep], axis=1)
        for pairs in (self.late, self.early, self.back_z[2], self.back_z[1]):
            keep, send = self.add_halves(keep, wait_for(came, after))
            came = self.send(send, pairs)
            after = yield [keep, send]
        yield [keep.astype(F32) + wait_for(came, after).astype(F32)]


class Plain:
    def __init__(self, devices):
        self.devices = devices

    def order(self, rows):
        return jnp.arange(CHANNELS)

    def gather(self, shard, after=(), core_last=False):
        result = [lax.all_gather(shard, AXES, axis=0, tiled=True)]
        yield
        if core_last:
            yield
        yield result
        yield [*result, *result]
        yield result

    def scatter(self, keep, send, extra=None):
        value = jnp.concatenate([keep, send], axis=0)
        if extra is not None:
            value = jnp.concatenate([jnp.concatenate(extra, axis=0), value], axis=1)
        result = [lax.psum_scatter(value.astype(F32), AXES, scatter_dimension=0, tiled=True)]
        while True:
            yield result


def share_rows(spread):
    return lax.all_to_all(spread, AXES, 0, 0)


def adamw(master, grad, first, second, rate, decay, correction):
    first_new = 0.5 * first + 0.5 * grad
    second_new = 0.5 * second + 0.5 * grad * grad
    master_new = master - rate * (
        first_new / correction / (jnp.sqrt(second_new / correction) + ADAM_EPS) + decay * master
    )
    return (master_new, first_new, second_new)


def on_device(
    links,
    clip_frames,
    valid_mask,
    labels,
    clip_keep,
    step_count,
    w_entry,
    w_spatial,
    w_temporal,
    w_head,
    small_params,
    entry_first,
    entry_second,
    spatial_first,
    spatial_second,
    temporal_first,
    temporal_second,
    head_first,
    head_second,
    small_first,
    small_second,
):
    clips, frames, height, breadth, _ = clip_frames.shape
    shard = w_spatial.shape[1]
    group = breadth * clips
    per = height * group
    rows = frames * per
    shape = jax.ShapeDtypeStruct

    def flat(taps):
        return taps.astype(BF).transpose(1, 0, 2).reshape(shard, -1)

    entry_t = w_entry.T
    temporal_t = w_temporal.transpose(0, 2, 1)
    head_pad = jnp.pad(w_head.astype(BF), ((0, 0), (0, CHANNELS - CLASSES)))
    index = links.order(shard)
    order = (index[:, None] == jnp.arange(CHANNELS)[None, :]).astype(BF)
    gain_one = small_params[None, :HIDDEN]
    shift_one = small_params[None, HIDDEN : 2 * HIDDEN]
    gain_two = small_params[None, 2 * HIDDEN : 2 * HIDDEN + CHANNELS]
    shift_two = small_params[None, 2 * HIDDEN + CHANNELS : 2 * HIDDEN + 2 * CHANNELS]
    bias = jnp.pad(
        small_params[None, 2 * HIDDEN + 2 * CHANNELS :],
        ((0, 0), (0, CHANNELS - CLASSES)),
        constant_values=-1e30,
    )
    x = clip_frames.transpose(1, 2, 3, 0, 4).reshape(rows, CHAN_IN)
    valid = valid_mask.astype(F32).transpose(1, 2, 3, 0)[..., None]
    valid = jnp.broadcast_to(valid, (*valid.shape[:4], 128)).reshape(rows, 128)
    keep = jnp.broadcast_to(clip_keep.astype(F32)[:, None], (clips, 128))
    lane = jnp.arange(CHANNELS)[None, :]
    target = jnp.where(
        lane < CLASSES,
        (1.0 - SMOOTHING) * (labels[:, None] == lane).astype(F32) + SMOOTHING / CLASSES,
        0.0,
    )

    fix = jnp.broadcast_to(1.0 - jnp.power(0.5, step_count[0].astype(F32)), (1, 128))
    small_rows = [small_params[None], small_first[None], small_second[None]]
    prepared = [order, gain_one, shift_one, gain_two, shift_two, bias, target, keep, fix]
    prepared += [*small_rows, x, valid]

    def part(j):
        return flat(w_spatial[:, :, STARTS[j] : STARTS[j] + WIDTHS[j]])

    load_mid = links.gather(jnp.concatenate([part(0), entry_t.astype(BF)], axis=1))
    next(load_mid)
    column_mid = load_mid.send([])
    load_top = links.gather(part(1), [*column_mid, *prepared])
    next(load_top)
    half_mid, other_mid = load_mid.send([])
    column_top = load_top.send([half_mid])
    load_low = links.gather(part(2), [*column_top, other_mid])
    next(load_low)
    head_time = jnp.concatenate([head_pad, flat(temporal_t)], axis=1)
    load_time = links.gather(head_time, [*column_top, other_mid], core_last=True)
    next(load_time)
    column_low = load_low.send([])
    ready = load_top.send(column_low)
    pieces_mid = load_mid.send([])
    count = len(pieces_mid)

    def at(width, where=lambda i: i):
        return pl.BlockSpec((per, width), lambda i: (where(i), 0))

    def piece_specs(pieces):
        return [whole(p.shape) for p in pieces]

    def now(i):
        return jnp.minimum(i, frames - 1)

    def before(i):
        return jnp.maximum(i - 1, 0)

    conv_flops = 2 * rows * 3 * CHANNELS * HIDDEN

    def sums(j):
        return result((8, 2 * WIDTHS[j])), shape((8, 2 * WIDTHS[j]), F32)

    def weights(j):
        return pltpu.HBM((9 * CHANNELS, WIDTHS[j]), BF)

    anywhere = pl.BlockSpec(memory_space=pl.ANY)
    field, cols, late_cols, conv_one, sums_one, weights_one = call(
        functools.partial(entry_kernel, count, breadth, clips),
        "entry_and_first_range",
        (frames,),
        [at(CHAN_IN), at(128)] + piece_specs(pieces_mid),
        [at(CHANNELS)] + [at(3 * CHANNELS)] * 2 + [at(WIDTHS[0]), sums(0)[0], anywhere],
        [
            pltpu.HBM((rows, CHANNELS), F32),
            shape((rows, 3 * CHANNELS), BF),
            pltpu.HBM((rows, 3 * CHANNELS), BF),
            shape((rows, WIDTHS[0]), F32),
            sums(0)[1],
            weights(0),
        ],
        [
            pltpu.VMEM((9 * CHANNELS, WIDTHS[0]), BF),
            pltpu.VMEM((CHANNELS, CHAN_IN), BF),
            pltpu.SemaphoreType.DMA,
        ],
        vmem=24,
        flops=conv_flops,
        gates=[ready[0], *column_low],
    )(x, valid, *pieces_mid)
    ready = load_low.send([conv_one])
    pieces_top = load_top.send([conv_one])
    load_time.send([conv_one])
    conv_two, sums_two, weights_two = call(
        functools.partial(spatial_kernel, count, group),
        "second_range",
        (frames,),
        [at(3 * CHANNELS), at(128)] + piece_specs(pieces_top),
        [at(WIDTHS[1]), sums(1)[0], anywhere],
        [shape((rows, WIDTHS[1]), F32), sums(1)[1], weights(1)],
        [pltpu.VMEM((9 * CHANNELS, WIDTHS[1]), BF), pltpu.SemaphoreType.DMA],
        flops=conv_flops,
        gates=ready[:1],
    )(cols, valid, *pieces_top)
    pieces_low = load_low.send([conv_two])
    ready = load_time.send([conv_two])
    conv_three, stats, weights_three = call(
        functools.partial(last_spatial_kernel, count, group),
        "last_range",
        (frames,),
        [at(3 * CHANNELS), at(128), whole((clips, 128))]
        + [whole(sums_one.shape), whole(sums_two.shape)]
        + piece_specs(pieces_low),
        [at(WIDTHS[2]), result((links.devices, 1, 2 * HIDDEN + 256)), anywhere],
        [
            shape((rows, WIDTHS[2]), F32),
            shape((links.devices, 1, 2 * HIDDEN + 256), F32),
            weights(2),
        ],
        [
            pltpu.VMEM((9 * CHANNELS, WIDTHS[2]), BF),
            pltpu.VMEM((8, 2 * WIDTHS[2]), F32),
            pltpu.VMEM((8, 128), F32),
            pltpu.SemaphoreType.DMA,
        ],
        flops=conv_flops // 2,
        gates=ready[:1],
    )(cols, valid, keep, sums_one, sums_two, *pieces_low)
    ready = load_time.send([conv_three])
    convs = (conv_one, conv_two, conv_three)
    stats = wait_for(stats, ready[:1])
    all_stats = share_rows(stats)
    pieces_time = load_time.send([all_stats])

    first, two, stats_two, coef, head = call(
        functools.partial(temporal_kernel, count, frames),
        "norm_and_temporal",
        (frames + 1,),
        [whole(all_stats.shape)]
        + [at(width, now) for width in WIDTHS]
        + [at(128, now), at(128, before)]
        + [whole((1, HIDDEN))] * 2
        + [whole((CHANNELS, CHANNELS))]
        + piece_specs(pieces_time),
        [
            at(HIDDEN, now),
            at(CHANNELS, before),
            result((links.devices, 1, 2 * CHANNELS)),
            result((8, HIDDEN + 128)),
            result((CHANNELS, CHANNELS)),
        ],
        [
            pltpu.HBM((rows, HIDDEN), BF),
            shape((rows, CHANNELS), F32),
            shape((links.devices, 1, 2 * CHANNELS), F32),
            shape((8, HIDDEN + 128), F32),
            shape((CHANNELS, CHANNELS), BF),
        ],
        [
            pltpu.VMEM((CHANNELS, 3 * HIDDEN), BF),
            pltpu.VMEM((rows, HIDDEN), BF),
            pltpu.VMEM((8, 2 * CHANNELS), F32),
        ],
        vmem=26,
        flops=conv_flops,
    )(all_stats, *convs, valid, valid, gain_one, shift_one, order, *pieces_time)
    all_two = share_rows(stats_two)

    half = CHANNELS // 2
    mask, dpool, stats_three, coef_two, head_keep, head_send = call(
        functools.partial(head_kernel, clips),
        "norm_head_and_back",
        (frames,),
        [whole(all_two.shape), at(CHANNELS), at(CHANNELS), at(128), whole((8, HIDDEN + 128))]
        + [whole((1, CHANNELS))] * 2
        + [whole((CHANNELS, CHANNELS))] * 2
        + [whole((1, CHANNELS)), whole((clips, CHANNELS)), whole((clips, 128))],
        [
            at(CHANNELS),
            result((clips, CHANNELS)),
            result((links.devices, 1, 3 * CHANNELS)),
            result((8, CHANNELS)),
            result((half, CHANNELS)),
            result((half, CHANNELS)),
        ],
        [
            pltpu.HBM((rows, CHANNELS), BF),
            shape((clips, CHANNELS), F32),
            shape((links.devices, 1, 3 * CHANNELS), F32),
            shape((8, CHANNELS), F32),
            shape((half, CHANNELS), BF),
            shape((half, CHANNELS), BF),
        ],
        [pltpu.VMEM((3, clips, CHANNELS), F32), pltpu.VMEM((clips, 128), F32)],
    )(all_two, two, field, valid, coef, gain_two, shift_two, order, head, bias, target, keep)
    all_three = share_rows(stats_three)

    dtwo, dpre, stats_four, total_three = call(
        functools.partial(first_back_kernel, count, frames, clips),
        "temporal_back",
        (frames + 1,),
        [
            whole(all_three.shape),
            at(CHANNELS, now),
            at(CHANNELS, now),
            at(128, now),
            whole((8, HIDDEN + 128)),
            whole((8, CHANNELS)),
            whole((clips, CHANNELS)),
            whole((CHANNELS, CHANNELS)),
            at(128, before),
        ]
        + [at(width, before) for width in WIDTHS]
        + piece_specs(pieces_time),
        [at(CHANNELS, now), at(HIDDEN, before), result((links.devices, 1, 2 * HIDDEN)),
         result((1, 3 * CHANNELS))],
        [
            shape((rows, CHANNELS), BF),
            shape((rows, HIDDEN), F32),
            shape((links.devices, 1, 2 * HIDDEN), F32),
            shape((1, 3 * CHANNELS), F32),
        ],
        [
            pltpu.VMEM((3 * CHANNELS, HIDDEN), BF),
            pltpu.VMEM((rows, CHANNELS), BF),
            pltpu.VMEM((8, CHANNELS), F32),
            pltpu.VMEM((8, 2 * HIDDEN), F32),
        ],
        vmem=26,
        flops=conv_flops,
    )(all_three, two, far(mask), valid, coef, coef_two, dpool, order, valid, *convs, *pieces_time)
    all_four = share_rows(stats_four)

    taps_shape = shape((half, 3 * HIDDEN), BF)
    taps_spec = pl.BlockSpec((half, HIDDEN), lambda i: (0, i))

    def temporal_grad(part):
        return call(
            functools.partial(temporal_grad_kernel, per),
            "temporal_gradient",
            (3,),
            [pl.BlockSpec((rows, half), lambda i: (0, part)), whole((rows, HIDDEN))],
            taps_spec,
            taps_shape,
            flops=conv_flops // 2,
            gates=[all_four],
        )(dtwo, first)

    time_send = temporal_grad(1)
    time_keep = temporal_grad(0)

    scatter_time = links.scatter(time_keep, time_send, (head_keep, head_send))
    next(scatter_time)
    ready = scatter_time.send([time_keep])
    dconv, total_four = call(
        conv_back_kernel,
        "spatial_norm_back",
        (frames,),
        [whole(all_four.shape)]
        + [at(width) for width in WIDTHS]
        + [at(HIDDEN), at(128), whole((8, HIDDEN + 128))],
        [at(HIDDEN), result((1, 2 * HIDDEN))],
        [shape((rows, HIDDEN), BF), shape((1, 2 * HIDDEN), F32)],
        [pltpu.VMEM((8, HIDDEN), F32)],
        gates=ready,
    )(all_four, *convs, dpre, valid, coef)

    def spatial_grad(tap_row, part, gates):
        return call(
            functools.partial(spatial_grad_kernel, tap_row, per, group),
            "spatial_gradient",
            (3,),
            [pl.BlockSpec((rows, half), lambda i: (0, 2 * i + part)), whole((rows, HIDDEN))],
            taps_spec,
            taps_shape,
            flops=conv_flops // 2,
            gates=gates,
        )(late_cols, dconv)

    send = spatial_grad(1, 1, [])
    keep = spatial_grad(1, 0, [send])
    scatter_mid = links.scatter(keep, send)
    next(scatter_mid)
    ready = scatter_time.send([keep]) + scatter_mid.send([keep])
    send = spatial_grad(0, 1, ready)
    keep = spatial_grad(0, 0, [send])
    scatter_top = links.scatter(keep, send)
    next(scatter_top)
    ready = scatter_time.send([keep]) + scatter_mid.send([keep]) + scatter_top.send([keep])
    send = spatial_grad(2, 1, ready)
    keep = spatial_grad(2, 0, [send])
    scatter_low = links.scatter(keep, send)
    next(scatter_low)
    ready = scatter_time.send([keep]) + scatter_mid.send([keep])
    ready += scatter_top.send([keep]) + scatter_low.send([keep])

    def field_back(tap_col, gates, extra, extra_specs, out_spec, out_shape, scratch=()):
        return call(
            functools.partial(field_back_kernel, tap_col, per, group, clips),
            "field_back",
            (frames,),
            [at(HIDDEN)]
            + [pl.BlockSpec(memory_space=pltpu.HBM)] * 3
            + extra_specs,
            out_spec,
            out_shape,
            [
                pltpu.VMEM((CHANNELS, 3 * HIDDEN), BF),
                pltpu.VMEM((per + 2 * group, HIDDEN), BF),
                *scratch,
                pltpu.SemaphoreType.DMA((9,)),
            ],
            flops=conv_flops,
            gates=gates,
        )(dconv, weights_one, weights_two, weights_three, *extra)

    partial = pltpu.HBM((rows, CHANNELS), F32)
    back = field_back(1, ready, [], [], at(CHANNELS), partial)
    time_share = scatter_time.send([back])
    ready = scatter_mid.send([back]) + scatter_top.send([back]) + scatter_low.send([back])
    back = field_back(0, ready, [far(back)], [at(CHANNELS)], at(CHANNELS), partial)
    share_mid = scatter_mid.send([back])
    ready = scatter_top.send([back]) + scatter_low.send([back])
    grad_entry = field_back(
        2,
        ready,
        [far(back), far(mask), dpool, valid, x, order],
        [
            at(CHANNELS),
            at(CHANNELS),
            whole((clips, CHANNELS)),
            at(128),
            at(CHAN_IN),
            whole((CHANNELS, CHANNELS)),
        ],
        result((CHANNELS, CHAN_IN)),
        shape((CHANNELS, CHAN_IN), BF),
        [pltpu.VMEM((CHANNELS, CHAN_IN), F32)],
    )
    entry_parts = lax.all_to_all(grad_entry.reshape(links.devices, shard, CHAN_IN), AXES, 0, 0)
    entry_share = jnp.sum(entry_parts.astype(F32), axis=0)
    share_top = scatter_top.send([grad_entry])
    scatter_low.send([grad_entry])
    share_low = scatter_low.send([])

    def taps(share):
        return share.reshape(shard, 3, HIDDEN).transpose(1, 0, 2)

    correction = fix[0, 0]
    total_three = wait_for(total_three, share_low)
    loss = total_three[0, 2 * CHANNELS + CLASSES] / coef[1, HIDDEN]
    small_shape = shape(small_rows[0].shape, F32)
    small_out = call(
        small_update_kernel,
        "small_update",
        (),
        [whole(total_three.shape), whole(total_four.shape), whole(fix.shape)]
        + [whole(small_shape.shape)] * 3,
        [result(small_shape.shape)] * 3,
        [small_shape] * 3,
    )(total_three, total_four, fix, *small_rows)
    small_out = [row[0] for row in small_out]
    spatial_grad_share = jnp.concatenate(
        [taps(share[0]) for share in (share_top, share_mid, share_low)], axis=0
    )
    time_share = time_share[0]
    temporal_share = taps(time_share[:, CHANNELS:]).transpose(0, 2, 1)
    entry_out = adamw(
        w_entry, entry_share.T, entry_first, entry_second, 0.06, DECAY_RATE, correction
    )
    spatial_out = adamw(
        w_spatial, spatial_grad_share, spatial_first, spatial_second, 0.02, DECAY_RATE, correction
    )
    temporal_out = adamw(
        w_temporal, temporal_share, temporal_first, temporal_second, 0.02, DECAY_RATE, correction
    )
    head_out = adamw(
        w_head, time_share[:, :CLASSES], head_first, head_second, 0.05, DECAY_RATE, correction
    )
    return (
        loss,
        *entry_out,
        *spatial_out,
        *temporal_out,
        *head_out,
        *small_out,
        entry_out[0].astype(BF),
        spatial_out[0].astype(BF),
        temporal_out[0].astype(BF),
        head_out[0].astype(BF),
    )


def solution(mesh):
    devices = mesh.shape["dp"] * mesh.shape["outer"]
    small_slice = mesh.shape["dp"] == 16 and mesh.shape["outer"] == 2
    links = Slice(devices) if small_slice else Plain(devices)
    both = ("dp", "outer")
    entry, spatial, temporal, head = (
        P(None, both),
        P(None, both, None),
        P(None, None, both),
        P(both, None),
    )
    placed = (
        P(both, None, None, None, None),
        P(both, None, None, None),
        P(both),
        P(both),
        P(),
        entry,
        spatial,
        temporal,
        head,
        P(),
        entry,
        entry,
        spatial,
        spatial,
        temporal,
        temporal,
        head,
        head,
        P(),
        P(),
    )
    return jax.shard_map(
        functools.partial(on_device, links),
        mesh=mesh,
        in_specs=placed,
        out_specs=(
            P(),
            *([entry] * 3),
            *([spatial] * 3),
            *([temporal] * 3),
            *([head] * 3),
            P(),
            P(),
            P(),
            entry,
            spatial,
            temporal,
            head,
        ),
        check_vma=False,
    )
```

```python
import functools

import jax
import jax.numpy as jnp
from jax import lax
from jax.experimental import pallas as pl
from jax.experimental.pallas import tpu as pltpu
from jax.sharding import PartitionSpec as P

CHANNELS = 512
HIDDEN = 1152
CLASSES = 400
CHAN_IN = 256
WIDTHS = (384, 512, 256)
STARTS = (0, 384, 896)

EPSILON = 1e-05
ADAM_EPS = 1e-08
DECAY_RATE = 0.1
SMOOTHING = 0.1

AXES = ("dp", "outer")
BF = jnp.bfloat16
F32 = jnp.float32
MIB = 1 << 20


def wide(column, times):
    return jnp.concatenate([column] * times, axis=1)


def dot_nn(left, right):
    return lax.dot_general(left, right, (((1,), (0,)), ((), ())), preferred_element_type=F32)


def dot_nt(left, right):
    return lax.dot_general(left, right, (((1,), (1,)), ((), ())), preferred_element_type=F32)


def dot_tn(left, right):
    return lax.dot_general(left, right, (((0,), (0,)), ((), ())), preferred_element_type=F32)


def reorder(rows, order, axis):
    value = jnp.concatenate(
        rows + [jnp.zeros((8 - len(rows), rows[0].shape[1]), F32)], axis=0
    )
    high = value.astype(BF).astype(F32)
    middle = (value - high).astype(BF).astype(F32)
    low = value - high - middle
    parts = jnp.concatenate([high, middle, low], axis=0).astype(BF)
    moved = lax.dot_general(parts, order, (((1,), (axis,)), ((), ())), preferred_element_type=F32)
    moved = moved[:8] + moved[8:16] + moved[16:]
    return [moved[k : k + 1] for k in range(len(rows))]


def to_owner_order(rows, order):
    return reorder(rows, order, 0)


def to_local_order(rows, order):
    return reorder(rows, order, 1)


def fold(value, step):
    return jnp.sum(value.reshape(value.shape[0] // step, step, value.shape[1]), axis=0)


def spread_row(ref, row):
    ref[...] = jnp.broadcast_to(row[None], ref.shape)


def far(value):
    return pltpu.with_memory_space_constraint(value, pltpu.HBM)


def whole(shape):
    return pl.BlockSpec(shape, lambda *_: (0,) * len(shape), pipeline_mode=pl.Buffered(1))


def result(shape):
    return pl.BlockSpec(shape, lambda *_: (0,) * len(shape))


def call(
    kernel, name, grid, in_specs, out_specs, out_shape, scratch=(), aliases=None, vmem=22, flops=0,
    gates=(), moved=20 * MIB,
):
    first, last = len(in_specs), len(in_specs) + len(gates)

    def gated(*refs):
        kernel(*refs[:first], *refs[last:])

    run = pl.pallas_call(
        gated,
        name=name,
        grid=grid,
        in_specs=list(in_specs) + [pl.BlockSpec(memory_space=pl.ANY)] * len(gates),
        out_specs=out_specs,
        out_shape=out_shape,
        scratch_shapes=list(scratch),
        input_output_aliases=aliases or {},
        compiler_params=pltpu.CompilerParams(vmem_limit_bytes=vmem * MIB),
        cost_estimate=pl.CostEstimate(flops=flops, bytes_accessed=moved, transcendentals=0),
    )
    return lambda *operands: run(*operands, *gates)


def fill_taps(pieces, w_ref):
    width = w_ref.shape[1]
    at = 0
    for piece in pieces:
        rows = piece.shape[0]
        for tap in range(9):
            w_ref[tap * CHANNELS + at : tap * CHANNELS + at + rows, :] = piece[
                :, tap * width : (tap + 1) * width
            ]
        at += rows


def save(w_ref, w_out, sem, step):
    copy = pltpu.make_async_copy(w_ref, w_out, sem)
    pl.when(step == 0)(copy.start)
    pl.when(step == pl.num_programs(0) - 1)(copy.wait)


def spatial_taps(group, cols_ref, w_ref, conv_ref):
    rows, depth = cols_ref.shape
    conv_ref[...] = dot_nn(cols_ref[...], w_ref[depth : 2 * depth])
    conv_ref[group:] += dot_nn(cols_ref[: rows - group], w_ref[:depth])
    conv_ref[: rows - group] += dot_nn(cols_ref[group:], w_ref[2 * depth :])


def add_sums(conv_ref, valid_ref, acc_ref):
    value = conv_ref[...]
    width = value.shape[1]
    kept = value * wide(valid_ref[...], width // 128)
    acc_ref[:, :width] += fold(kept, 8)
    acc_ref[:, width:] += fold(kept * value, 8)


def entry_kernel(count, side, clips, x_ref, valid_ref, *refs):
    pieces, refs = refs[:count], refs[count:]
    field_ref, cols_ref, late_ref, conv_ref, acc_ref, w_out, w_ref, e_ref, sem = refs

    @pl.when(pl.program_id(0) == 0)
    def _():
        fill_taps(pieces, w_ref)
        at = 0
        for piece in pieces:
            rows = piece.shape[0]
            e_ref[at : at + rows, :] = piece[:, 9 * w_ref.shape[1] :]
            at += rows
        acc_ref[...] = jnp.zeros_like(acc_ref)

    save(w_ref, w_out, sem, pl.program_id(0))
    value = dot_nt(x_ref[...], e_ref[...]) * wide(valid_ref[...], CHANNELS // 128)
    field_ref[...] = value
    rows = value.shape[0]
    group = side * clips
    grid3 = value.reshape(rows // group, group, CHANNELS)
    edge = jnp.zeros((rows // group, clips, CHANNELS), F32)
    left = jnp.concatenate([edge, grid3[:, : group - clips]], axis=1).reshape(rows, CHANNELS)
    right = jnp.concatenate([grid3[:, clips:], edge], axis=1).reshape(rows, CHANNELS)
    cols_ref[:, :CHANNELS] = left.astype(BF)
    cols_ref[:, CHANNELS : 2 * CHANNELS] = value.astype(BF)
    cols_ref[:, 2 * CHANNELS :] = right.astype(BF)
    late_ref[...] = cols_ref[...]
    spatial_taps(group, cols_ref, w_ref, conv_ref)
    add_sums(conv_ref, valid_ref, acc_ref)


def spatial_kernel(count, group, cols_ref, valid_ref, *refs):
    pieces, (conv_ref, acc_ref, w_out, w_ref, sem) = refs[:count], refs[count:]

    @pl.when(pl.program_id(0) == 0)
    def _():
        fill_taps(pieces, w_ref)
        acc_ref[...] = jnp.zeros_like(acc_ref)

    save(w_ref, w_out, sem, pl.program_id(0))
    spatial_taps(group, cols_ref, w_ref, conv_ref)
    add_sums(conv_ref, valid_ref, acc_ref)


def last_spatial_kernel(count, group, cols_ref, valid_ref, keep_ref, one_ref, two_ref, *refs):
    pieces, refs = refs[:count], refs[count:]
    conv_ref, stats_ref, w_out, w_ref, acc_ref, size_ref, sem = refs
    step = pl.program_id(0)

    @pl.when(step == 0)
    def _():
        fill_taps(pieces, w_ref)
        acc_ref[...] = jnp.zeros_like(acc_ref)
        size_ref[...] = jnp.zeros_like(size_ref)

    save(w_ref, w_out, sem, step)
    spatial_taps(group, cols_ref, w_ref, conv_ref)
    add_sums(conv_ref, valid_ref, acc_ref)
    size_ref[...] += fold(valid_ref[...], 8)

    @pl.when(step == pl.num_programs(0) - 1)
    def _():
        parts = (one_ref, two_ref, acc_ref)
        sums = [part[:, : part.shape[1] // 2] for part in parts]
        squares = [part[:, part.shape[1] // 2 :] for part in parts]
        line = jnp.concatenate(sums + squares + [size_ref[...], fold(keep_ref[...], 8)], axis=1)
        spread_row(stats_ref, jnp.sum(line, axis=0, keepdims=True))


def temporal_kernel(
    count, frames, recv_ref, *refs
):
    convs, (valid_ref, valid_out_ref, gain_ref, shift_ref, order_ref), refs = (
        refs[:3], refs[3:8], refs[8:]
    )
    pieces, refs = refs[:count], refs[count:]
    first_ref, two_ref, stats_ref, coef_ref, head_ref, w_ref, first_all, acc_ref = refs
    step = pl.program_id(0)
    per = valid_ref.shape[0]

    @pl.when(step == 0)
    def _():
        at = 0
        for piece in pieces:
            rows = piece.shape[0]
            head_ref[at : at + rows, :] = piece[:, :CHANNELS]
            w_ref[at : at + rows, :] = piece[:, CHANNELS:]
            at += rows
        total = jnp.sum(recv_ref[...], axis=0)
        count_all = total[:, 2 * HIDDEN : 2 * HIDDEN + 128]
        wide_count = wide(count_all, HIDDEN // 128)
        mean = total[:, :HIDDEN] / wide_count
        variance = total[:, HIDDEN : 2 * HIDDEN] / wide_count - mean * mean
        coef_ref[...] = jnp.zeros_like(coef_ref)
        coef_ref[0:1, :HIDDEN] = mean
        coef_ref[1:2, :HIDDEN] = lax.rsqrt(variance + EPSILON)
        coef_ref[2:3, :HIDDEN] = gain_ref[...]
        coef_ref[3:4, :HIDDEN] = shift_ref[...]
        coef_ref[0:1, HIDDEN:] = count_all
        coef_ref[1:2, HIDDEN:] = total[:, 2 * HIDDEN + 128 :]
        acc_ref[...] = jnp.zeros_like(acc_ref)

    @pl.when(step < frames)
    def _():
        for conv_ref, start, width in zip(convs, STARTS, WIDTHS, strict=True):
            lanes = slice(start, start + width)
            normed = (conv_ref[...] - coef_ref[0:1, lanes]) * coef_ref[1:2, lanes]
            pre = coef_ref[2:3, lanes] * normed + coef_ref[3:4, lanes]
            first = (jnp.maximum(pre, 0.0) * wide(valid_ref[...], width // 128)).astype(BF)
            first_ref[:, lanes] = first
            first_all[pl.ds(pl.multiple_of(step * per, per), per), lanes] = first

    def frame(start, taps):
        pieces_at = [
            first_all[pl.ds(pl.multiple_of(start + k * per, per), per), :] for k in range(len(taps))
        ]
        lanes = slice(taps[0] * HIDDEN, (taps[-1] + 1) * HIDDEN)
        value = dot_nt(jnp.concatenate(pieces_at, axis=1), w_ref[:, lanes])
        two_ref[...] = value
        kept = value * wide(valid_out_ref[...], CHANNELS // 128)
        acc_ref[:, :CHANNELS] += fold(kept, 8)
        acc_ref[:, CHANNELS:] += fold(kept * value, 8)

    @pl.when(step == 1)
    def _():
        frame(0, (1, 2))

    @pl.when(jnp.logical_and(step > 1, step < frames))
    def _():
        frame((step - 2) * per, (0, 1, 2))

    @pl.when(step == frames)
    def _():
        frame((frames - 2) * per, (0, 1))
        sums = jnp.sum(acc_ref[...], axis=0, keepdims=True)
        parts = to_owner_order([sums[:, :CHANNELS], sums[:, CHANNELS:]], order_ref[...])
        spread_row(stats_ref, jnp.concatenate(parts, axis=1))


def head_kernel(
    clips, recv_ref, two_ref, field_ref, valid_ref, coef_ref, gain_ref, shift_ref, order_ref,
    head_ref, bias_ref, target_ref, keep_ref,
    mask_ref, dpool_ref, stats_ref, coef_two_ref, keep_grad_ref, send_grad_ref, acc_ref, size_ref,
):
    step = pl.program_id(0)

    @pl.when(step == 0)
    def _():
        total = jnp.sum(recv_ref[...], axis=0)
        count = wide(coef_ref[0:1, HIDDEN:], CHANNELS // 128)
        mean, square, gain, shift = to_local_order(
            [total[:, :CHANNELS] / count, total[:, CHANNELS:] / count, gain_ref[...], shift_ref[...]],
            order_ref[...],
        )
        coef_two_ref[...] = jnp.zeros_like(coef_two_ref)
        coef_two_ref[0:1, :] = mean
        coef_two_ref[1:2, :] = lax.rsqrt(square - mean * mean + EPSILON)
        coef_two_ref[2:3, :] = gain
        coef_two_ref[3:4, :] = shift
        acc_ref[...] = jnp.zeros_like(acc_ref)
        size_ref[...] = jnp.zeros_like(size_ref)

    valid = wide(valid_ref[...], CHANNELS // 128)
    normed = (two_ref[...] - coef_two_ref[0:1, :]) * coef_two_ref[1:2, :]
    pre = coef_two_ref[2:3, :] * normed + coef_two_ref[3:4, :] + field_ref[...]
    mask = jnp.where(pre > 0.0, valid, 0.0)
    mask_ref[...] = mask.astype(BF)
    acc_ref[0] += fold(jnp.maximum(pre, 0.0) * valid, clips)
    acc_ref[1] += fold(mask, clips)
    acc_ref[2] += fold(mask * normed, clips)
    size_ref[...] += fold(valid_ref[...], clips)

    @pl.when(step == pl.num_programs(0) - 1)
    def _():
        size = wide(size_ref[...], CHANNELS // 128)
        pooled_low = (acc_ref[0] / size).astype(BF)
        head = head_ref[...]
        logits = dot_nn(pooled_low, head) + bias_ref[...]
        shifted = logits - jnp.max(logits, axis=1, keepdims=True)
        log_prob = shifted - jnp.log(jnp.sum(jnp.exp(shifted), axis=1, keepdims=True))
        target = target_ref[...]
        per_clip = -jnp.sum(target * log_prob, axis=1, keepdims=True)
        keep = wide(keep_ref[...], CHANNELS // 128)
        loss = jnp.sum(keep * per_clip, axis=0, keepdims=True)
        kept = wide(coef_ref[1:2, HIDDEN:], CHANNELS // 128)
        d_logits = keep * (jnp.exp(log_prob) - target) / kept
        d_low = d_logits.astype(BF)
        grad = dot_tn(pooled_low.astype(F32), d_low.astype(F32)).astype(BF)
        half = grad.shape[0] // 2
        keep_grad_ref[...] = grad[:half]
        send_grad_ref[...] = grad[half:]
        d_pooled = dot_nt(d_low, head) / size
        dpool_ref[...] = d_pooled
        sums_one = jnp.sum(acc_ref[1] * d_pooled, axis=0, keepdims=True)
        sums_two = jnp.sum(acc_ref[2] * d_pooled, axis=0, keepdims=True)
        lane = lax.broadcasted_iota(jnp.int32, (1, CHANNELS), 1)
        parts = to_owner_order([sums_one, sums_two], order_ref[...]) + [
            jnp.where(lane < CLASSES, jnp.sum(d_logits, axis=0, keepdims=True), loss),
        ]
        spread_row(stats_ref, jnp.concatenate(parts, axis=1))


def first_back_kernel(
    count, frames, clips, recv_ref, two_ref, mask_ref, valid_ref, coef_ref, coef_two_ref, dpool_ref,
    order_ref, valid_out_ref, *refs
):
    convs, refs = refs[:3], refs[3:]
    pieces, refs = refs[:count], refs[count:]
    dtwo_ref, dpre_ref, stats_ref, total_ref, w_ref, dtwo_all, back_ref, acc_ref = refs
    step = pl.program_id(0)
    per = valid_ref.shape[0]

    @pl.when(step == 0)
    def _():
        at = 0
        for piece in pieces:
            rows = piece.shape[0]
            for t in range(3):
                w_ref[t * CHANNELS + at : t * CHANNELS + at + rows, :] = piece[
                    :, CHANNELS + t * HIDDEN : CHANNELS + (t + 1) * HIDDEN
                ]
            at += rows
        total = jnp.sum(recv_ref[...], axis=0)
        total_ref[...] = total
        each = wide(coef_ref[0:1, HIDDEN:], CHANNELS // 128)
        back_ref[0:1, :], back_ref[1:2, :] = to_local_order(
            [total[:, :CHANNELS] / each, total[:, CHANNELS : 2 * CHANNELS] / each], order_ref[...]
        )
        acc_ref[...] = jnp.zeros_like(acc_ref)

    @pl.when(step < frames)
    def _():
        valid = wide(valid_ref[...], CHANNELS // 128)
        gain = coef_two_ref[2:3, :]
        inverse = coef_two_ref[1:2, :]
        normed = (two_ref[...] - coef_two_ref[0:1, :]) * inverse
        mask = mask_ref[...].astype(F32)
        spread = jnp.broadcast_to(dpool_ref[...][None], (per // clips, clips, CHANNELS))
        d_pre = mask * spread.reshape(per, CHANNELS)
        low = (
            valid * (gain * inverse) * (d_pre - back_ref[0:1, :] - normed * back_ref[1:2, :])
        ).astype(BF)
        dtwo_ref[...] = low
        dtwo_all[pl.ds(pl.multiple_of(step * per, per), per), :] = low

    def frame(last, taps):
        pieces_at = [
            dtwo_all[pl.ds(pl.multiple_of(last - k * per, per), per), :] for k in range(len(taps))
        ]
        back = jnp.concatenate(pieces_at, axis=1)
        taps_rows = slice(taps[0] * CHANNELS, (taps[-1] + 1) * CHANNELS)
        for conv_ref, start, width in zip(convs, STARTS, WIDTHS, strict=True):
            lanes = slice(start, start + width)
            d_first = dot_nn(back, w_ref[taps_rows, lanes])
            normed = (conv_ref[...] - coef_ref[0:1, lanes]) * coef_ref[1:2, lanes]
            pre = coef_ref[2:3, lanes] * normed + coef_ref[3:4, lanes]
            d_pre = jnp.where(pre > 0.0, d_first, 0.0) * wide(valid_out_ref[...], width // 128)
            dpre_ref[:, lanes] = d_pre
            acc_ref[:, lanes] += fold(d_pre, 8)
            acc_ref[:, HIDDEN + start : HIDDEN + start + width] += fold(d_pre * normed, 8)

    @pl.when(step == 1)
    def _():
        frame(per, (0, 1))

    @pl.when(jnp.logical_and(step > 1, step < frames))
    def _():
        frame(step * per, (0, 1, 2))

    @pl.when(step == frames)
    def _():
        frame((frames - 1) * per, (1, 2))
        spread_row(stats_ref, jnp.sum(acc_ref[...], axis=0, keepdims=True))


def conv_back_kernel(
    recv_ref, conv_one, conv_two, conv_three, dpre_ref, valid_ref, coef_ref, out_ref, total_ref, back_ref
):
    @pl.when(pl.program_id(0) == 0)
    def _():
        total = jnp.sum(recv_ref[...], axis=0)
        total_ref[...] = total
        each = wide(coef_ref[0:1, HIDDEN:], HIDDEN // 128)
        back_ref[0:1, :] = total[:, :HIDDEN] / each
        back_ref[1:2, :] = total[:, HIDDEN:] / each

    for conv_ref, start, width in zip((conv_one, conv_two, conv_three), STARTS, WIDTHS, strict=True):
        lanes = slice(start, start + width)
        inverse = coef_ref[1:2, lanes]
        normed = (conv_ref[...] - coef_ref[0:1, lanes]) * inverse
        value = dpre_ref[:, lanes] - back_ref[0:1, lanes] - normed * back_ref[1:2, lanes]
        scale = coef_ref[2:3, lanes] * inverse
        out_ref[:, lanes] = (wide(valid_ref[...], width // 128) * scale * value).astype(BF)


def temporal_grad_kernel(per, dtwo_ref, first_ref, out_ref):
    rows = dtwo_ref.shape[0]

    def tap(low_out, low_in, size):
        left, right = dtwo_ref[low_out : low_out + size], first_ref[low_in : low_in + size]
        out_ref[...] = dot_tn(left, right).astype(BF)

    step = pl.program_id(0)
    pl.when(step == 0)(lambda: tap(per, 0, rows - per))
    pl.when(step == 1)(lambda: tap(0, 0, rows))
    pl.when(step == 2)(lambda: tap(0, per, rows - per))


def spatial_grad_kernel(tap_row, per, group, cols_ref, d_ref, out_ref):
    rows = d_ref.shape[0]
    if tap_row == 1:
        out_ref[...] = dot_tn(cols_ref[...], d_ref[...]).astype(BF)
        return
    left, right = (0, group) if tap_row == 0 else (group, 0)
    size = per - group
    cols = [cols_ref[f + left : f + left + size] for f in range(0, rows, per)]
    back = [d_ref[f + right : f + right + size] for f in range(0, rows, per)]
    grad = dot_tn(jnp.concatenate(cols, axis=0), jnp.concatenate(back, axis=0))
    out_ref[...] = grad.astype(BF)


def field_back_kernel(tap_col, per, group, clips, d_ref, *refs):
    weights, refs, sems = refs[:3], refs[3:-1], refs[-1]
    if tap_col == 1:
        out_ref, w_ref, pad_ref = refs
    elif tap_col == 0:
        acc_in_ref, out_ref, w_ref, pad_ref = refs
    else:
        (acc_in_ref, mask_ref, dpool_ref, valid_ref, x_ref, order_ref,
         out_ref, w_ref, pad_ref, grad_ref) = refs
    step = pl.program_id(0)

    @pl.when(step == 0)
    def _():
        copies = []
        for a in range(3):
            for j in range(3):
                copies.append(
                    pltpu.make_async_copy(
                        weights[j].at[pl.ds((3 * a + tap_col) * CHANNELS, CHANNELS), :],
                        w_ref.at[:, pl.ds(a * HIDDEN + STARTS[j], WIDTHS[j])],
                        sems.at[3 * a + j],
                    )
                )
        for copy in copies:
            copy.start()
        for copy in copies:
            copy.wait()
        pad_ref[:group] = jnp.zeros((group, HIDDEN), BF)
        pad_ref[group + per :] = jnp.zeros((group, HIDDEN), BF)

    pad_ref[group : group + per] = d_ref[...]
    left = jnp.concatenate(
        [pad_ref[(2 - a) * group : (2 - a) * group + per] for a in range(3)], axis=1
    )
    value = dot_nt(left, w_ref[...])
    if tap_col == 1:
        out_ref[...] = value
        return
    value = value.reshape(per // group, group, CHANNELS)
    edge = jnp.zeros((per // group, clips, CHANNELS), F32)
    if tap_col == 0:
        value = jnp.concatenate([value[:, clips:], edge], axis=1)
    else:
        value = jnp.concatenate([edge, value[:, : group - clips]], axis=1)
    value = acc_in_ref[...] + value.reshape(per, CHANNELS)
    if tap_col == 0:
        out_ref[...] = value
        return
    spread = jnp.broadcast_to(dpool_ref[...][None], (per // clips, clips, CHANNELS))
    value = value + mask_ref[...].astype(F32) * spread.reshape(per, CHANNELS)
    d_entry = (value * wide(valid_ref[...], CHANNELS // 128)).astype(BF)
    grad = dot_tn(d_entry, x_ref[...])

    @pl.when(step == 0)
    def _():
        grad_ref[...] = grad

    @pl.when(step > 0)
    def _():
        grad_ref[...] += grad

    @pl.when(step == pl.num_programs(0) - 1)
    def _():
        out_ref[...] = dot_tn(order_ref[...], grad_ref[...].astype(BF)).astype(BF)


def small_update_kernel(
    three_ref, four_ref, fix_ref, w_ref, first_ref, second_ref, w_out, first_out, second_out
):
    def part(lo, hi, grad):
        lanes = slice(lo, hi)
        w_out[:, lanes], first_out[:, lanes], second_out[:, lanes] = adamw(
            w_ref[:, lanes], grad, first_ref[:, lanes], second_ref[:, lanes],
            0.5, 0.0, fix_ref[:, :1],
        )

    at = 2 * HIDDEN
    part(0, HIDDEN, four_ref[:, HIDDEN:])
    part(HIDDEN, at, four_ref[:, :HIDDEN])
    part(at, at + CHANNELS, three_ref[:, CHANNELS : 2 * CHANNELS])
    part(at + CHANNELS, at + 2 * CHANNELS, three_ref[:, :CHANNELS])
    at += 2 * CHANNELS
    part(at, at + CLASSES, three_ref[:, 2 * CHANNELS : 2 * CHANNELS + CLASSES])


def wait_for(value, others):
    return lax.optimization_barrier((value, *others))[0]


def split_four(devices):
    def pairs(move):
        result = []
        for source in range(devices):
            z, x, core, y = source >> 3, (source >> 2) & 1, (source >> 1) & 1, source & 1
            z, x, core, y = move(z, x, core, y)
            result.append((source, ((z * 2 + x) * 2 + core) * 2 + y))
        return result

    along_z = [pairs(lambda z, x, c, y, k=k: ((z + k) % 4, x, c, y)) for k in range(4)]
    back_z = [pairs(lambda z, x, c, y, k=k: ((z - k) % 4, x, c, y)) for k in range(4)]
    early = pairs(lambda z, x, c, y: (z, 1 - x, c, y) if c == 0 else (z, x, c, 1 - y))
    late = pairs(lambda z, x, c, y: (z, x, c, 1 - y) if c == 0 else (z, 1 - x, c, y))
    core = pairs(lambda z, x, c, y: (z, x, 1 - c, y))
    return along_z, back_z, early, late, core


class Slice:
    def __init__(self, devices):
        self.devices = devices
        self.along_z, self.back_z, self.early, self.late, self.core = split_four(devices)

    def send(self, value, pairs):
        return lax.ppermute(value, AXES, pairs)

    def order(self, rows):
        channel = jnp.arange(CHANNELS)
        block, inside = channel // rows, channel % rows
        other, j, i, k = block >> 4, (block >> 3) & 1, (block >> 2) & 1, block & 3
        at, y = lax.axis_index("dp"), lax.axis_index("outer")
        core = (at & 1) ^ other
        x = ((at >> 1) & 1) ^ jnp.where(core == 0, i, j)
        y = y ^ jnp.where(core == 0, j, i)
        z = ((at >> 2) - k) & 3
        return (((z * 2 + x) * 2 + core) * 2 + y) * rows + inside

    def gather(self, shard, after=(), core_last=False):
        shard = wait_for(shard, after)
        if core_last:
            column = shard
            for k in (1, 2):
                came = self.send(column, self.along_z[k])
                after = yield
                column = jnp.concatenate([column, wait_for(came, after)], axis=0)
        else:
            came = [self.send(shard, self.along_z[k]) for k in (1, 2, 3)]
            after = yield
            column = jnp.concatenate([shard] + [wait_for(part, after) for part in came], axis=0)
        came = self.send(column, self.early)
        after = yield [column]
        half = jnp.concatenate([column, wait_for(came, after)], axis=0)
        rest = self.send(half, self.late)
        other = half if core_last else self.send(half, self.core)
        after = yield [half, other]
        rest = wait_for(rest, after)
        if core_last:
            other = self.send(wait_for(half, after), self.core)
        yield [half, rest, other, self.send(rest, self.core)]

    def add_halves(self, keep, came):
        half = keep.shape[0] // 2
        return keep[:half] + came[:half], keep[half:] + came[half:]

    def scatter(self, keep, send, extra=None):
        came = self.send(send, self.core)
        if extra is not None:
            came = jnp.concatenate([self.send(extra[1], self.core), came], axis=1)
        after = yield
        if extra is not None:
            keep = jnp.concatenate([extra[0], keep], axis=1)
        for pairs in (self.late, self.early, self.back_z[2], self.back_z[1]):
            keep, send = self.add_halves(keep, wait_for(came, after))
            came = self.send(send, pairs)
            after = yield [keep, send]
        yield [keep.astype(F32) + wait_for(came, after).astype(F32)]


class Plain:
    def __init__(self, devices):
        self.devices = devices

    def order(self, rows):
        return jnp.arange(CHANNELS)

    def gather(self, shard, after=(), core_last=False):
        result = [lax.all_gather(shard, AXES, axis=0, tiled=True)]
        yield
        if core_last:
            yield
        yield result
        yield [*result, *result]
        yield result

    def scatter(self, keep, send, extra=None):
        value = jnp.concatenate([keep, send], axis=0)
        if extra is not None:
            value = jnp.concatenate([jnp.concatenate(extra, axis=0), value], axis=1)
        result = [lax.psum_scatter(value.astype(F32), AXES, scatter_dimension=0, tiled=True)]
        while True:
            yield result


def share_rows(spread):
    return lax.all_to_all(spread, AXES, 0, 0)


def adamw(master, grad, first, second, rate, decay, correction):
    first_new = 0.5 * first + 0.5 * grad
    second_new = 0.5 * second + 0.5 * grad * grad
    master_new = master - rate * (
        first_new / correction / (jnp.sqrt(second_new / correction) + ADAM_EPS) + decay * master
    )
    return (master_new, first_new, second_new)


def on_device(
    links,
    clip_frames,
    valid_mask,
    labels,
    clip_keep,
    step_count,
    w_entry,
    w_spatial,
    w_temporal,
    w_head,
    small_params,
    entry_first,
    entry_second,
    spatial_first,
    spatial_second,
    temporal_first,
    temporal_second,
    head_first,
    head_second,
    small_first,
    small_second,
):
    clips, frames, height, breadth, _ = clip_frames.shape
    shard = w_spatial.shape[1]
    group = breadth * clips
    per = height * group
    rows = frames * per
    shape = jax.ShapeDtypeStruct

    def flat(taps):
        return taps.astype(BF).transpose(1, 0, 2).reshape(shard, -1)

    entry_t = w_entry.T
    temporal_t = w_temporal.transpose(0, 2, 1)
    head_pad = jnp.pad(w_head.astype(BF), ((0, 0), (0, CHANNELS - CLASSES)))
    index = links.order(shard)
    order = (index[:, None] == jnp.arange(CHANNELS)[None, :]).astype(BF)
    gain_one = small_params[None, :HIDDEN]
    shift_one = small_params[None, HIDDEN : 2 * HIDDEN]
    gain_two = small_params[None, 2 * HIDDEN : 2 * HIDDEN + CHANNELS]
    shift_two = small_params[None, 2 * HIDDEN + CHANNELS : 2 * HIDDEN + 2 * CHANNELS]
    bias = jnp.pad(
        small_params[None, 2 * HIDDEN + 2 * CHANNELS :],
        ((0, 0), (0, CHANNELS - CLASSES)),
        constant_values=-1e30,
    )
    x = clip_frames.transpose(1, 2, 3, 0, 4).reshape(rows, CHAN_IN)
    valid = valid_mask.astype(F32).transpose(1, 2, 3, 0)[..., None]
    valid = jnp.broadcast_to(valid, (*valid.shape[:4], 128)).reshape(rows, 128)
    keep = jnp.broadcast_to(clip_keep.astype(F32)[:, None], (clips, 128))
    lane = jnp.arange(CHANNELS)[None, :]
    target = jnp.where(
        lane < CLASSES,
        (1.0 - SMOOTHING) * (labels[:, None] == lane).astype(F32) + SMOOTHING / CLASSES,
        0.0,
    )

    fix = jnp.broadcast_to(1.0 - jnp.power(0.5, step_count[0].astype(F32)), (1, 128))
    small_rows = [small_params[None], small_first[None], small_second[None]]
    prepared = [order, gain_one, shift_one, gain_two, shift_two, bias, target, keep, fix]
    prepared += [*small_rows, x, valid]

    def part(j):
        return flat(w_spatial[:, :, STARTS[j] : STARTS[j] + WIDTHS[j]])

    load_mid = links.gather(jnp.concatenate([part(0), entry_t.astype(BF)], axis=1))
    next(load_mid)
    column_mid = load_mid.send([])
    load_top = links.gather(part(1), [*column_mid, *prepared])
    next(load_top)
    half_mid, other_mid = load_mid.send([])
    column_top = load_top.send([half_mid])
    load_low = links.gather(part(2), [*column_top, other_mid])
    next(load_low)
    head_time = jnp.concatenate([head_pad, flat(temporal_t)], axis=1)
    load_time = links.gather(head_time, [*column_top, other_mid], core_last=True)
    next(load_time)
    column_low = load_low.send([])
    ready = load_top.send(column_low)
    load_time.send(column_low)
    pieces_mid = load_mid.send([])
    count = len(pieces_mid)

    def at(width, where=lambda i: i):
        return pl.BlockSpec((per, width), lambda i: (where(i), 0))

    def piece_specs(pieces):
        return [whole(p.shape) for p in pieces]

    def now(i):
        return jnp.minimum(i, frames - 1)

    def before(i):
        return jnp.maximum(i - 1, 0)

    conv_flops = 2 * rows * 3 * CHANNELS * HIDDEN

    def sums(j):
        return result((8, 2 * WIDTHS[j])), shape((8, 2 * WIDTHS[j]), F32)

    def weights(j):
        return pltpu.HBM((9 * CHANNELS, WIDTHS[j]), BF)

    anywhere = pl.BlockSpec(memory_space=pl.ANY)
    field, cols, late_cols, conv_one, sums_one, weights_one = call(
        functools.partial(entry_kernel, count, breadth, clips),
        "entry_and_first_range",
        (frames,),
        [at(CHAN_IN), at(128)] + piece_specs(pieces_mid),
        [at(CHANNELS)] + [at(3 * CHANNELS)] * 2 + [at(WIDTHS[0]), sums(0)[0], anywhere],
        [
            pltpu.HBM((rows, CHANNELS), F32),
            shape((rows, 3 * CHANNELS), BF),
            pltpu.HBM((rows, 3 * CHANNELS), BF),
            shape((rows, WIDTHS[0]), F32),
            sums(0)[1],
            weights(0),
        ],
        [
            pltpu.VMEM((9 * CHANNELS, WIDTHS[0]), BF),
            pltpu.VMEM((CHANNELS, CHAN_IN), BF),
            pltpu.SemaphoreType.DMA,
        ],
        vmem=24,
        flops=conv_flops,
        gates=[ready[0], *column_low],
    )(x, valid, *pieces_mid)
    ready = load_low.send([conv_one])
    pieces_top = load_top.send([conv_one])
    column_time = load_time.send([conv_one])
    conv_two, sums_two, weights_two = call(
        functools.partial(spatial_kernel, count, group),
        "second_range",
        (frames,),
        [at(3 * CHANNELS), at(128)] + piece_specs(pieces_top),
        [at(WIDTHS[1]), sums(1)[0], anywhere],
        [shape((rows, WIDTHS[1]), F32), sums(1)[1], weights(1)],
        [pltpu.VMEM((9 * CHANNELS, WIDTHS[1]), BF), pltpu.SemaphoreType.DMA],
        flops=conv_flops,
        gates=[ready[0], *column_time],
    )(cols, valid, *pieces_top)
    pieces_low = load_low.send([conv_two])
    ready = load_time.send([conv_two])
    conv_three, stats, weights_three = call(
        functools.partial(last_spatial_kernel, count, group),
        "last_range",
        (frames,),
        [at(3 * CHANNELS), at(128), whole((clips, 128))]
        + [whole(sums_one.shape), whole(sums_two.shape)]
        + piece_specs(pieces_low),
        [at(WIDTHS[2]), result((links.devices, 1, 2 * HIDDEN + 256)), anywhere],
        [
            shape((rows, WIDTHS[2]), F32),
            shape((links.devices, 1, 2 * HIDDEN + 256), F32),
            weights(2),
        ],
        [
            pltpu.VMEM((9 * CHANNELS, WIDTHS[2]), BF),
            pltpu.VMEM((8, 2 * WIDTHS[2]), F32),
            pltpu.VMEM((8, 128), F32),
            pltpu.SemaphoreType.DMA,
        ],
        flops=conv_flops // 2,
        gates=ready[:1],
    )(cols, valid, keep, sums_one, sums_two, *pieces_low)
    convs = (conv_one, conv_two, conv_three)
    stats = wait_for(stats, ready[:1])
    all_stats = share_rows(stats)
    pieces_time = load_time.send([all_stats])

    first, two, stats_two, coef, head = call(
        functools.partial(temporal_kernel, count, frames),
        "norm_and_temporal",
        (frames + 1,),
        [whole(all_stats.shape)]
        + [at(width, now) for width in WIDTHS]
        + [at(128, now), at(128, before)]
        + [whole((1, HIDDEN))] * 2
        + [whole((CHANNELS, CHANNELS))]
        + piece_specs(pieces_time),
        [
            at(HIDDEN, now),
            at(CHANNELS, before),
            result((links.devices, 1, 2 * CHANNELS)),
            result((8, HIDDEN + 128)),
            result((CHANNELS, CHANNELS)),
        ],
        [
            pltpu.HBM((rows, HIDDEN), BF),
            shape((rows, CHANNELS), F32),
            shape((links.devices, 1, 2 * CHANNELS), F32),
            shape((8, HIDDEN + 128), F32),
            shape((CHANNELS, CHANNELS), BF),
        ],
        [
            pltpu.VMEM((CHANNELS, 3 * HIDDEN), BF),
            pltpu.VMEM((rows, HIDDEN), BF),
            pltpu.VMEM((8, 2 * CHANNELS), F32),
        ],
        vmem=26,
        flops=conv_flops,
    )(all_stats, *convs, valid, valid, gain_one, shift_one, order, *pieces_time)
    all_two = share_rows(stats_two)

    half = CHANNELS // 2
    mask, dpool, stats_three, coef_two, head_keep, head_send = call(
        functools.partial(head_kernel, clips),
        "norm_head_and_back",
        (frames,),
        [whole(all_two.shape), at(CHANNELS), at(CHANNELS), at(128), whole((8, HIDDEN + 128))]
        + [whole((1, CHANNELS))] * 2
        + [whole((CHANNELS, CHANNELS))] * 2
        + [whole((1, CHANNELS)), whole((clips, CHANNELS)), whole((clips, 128))],
        [
            at(CHANNELS),
            result((clips, CHANNELS)),
            result((links.devices, 1, 3 * CHANNELS)),
            result((8, CHANNELS)),
            result((half, CHANNELS)),
            result((half, CHANNELS)),
        ],
        [
            pltpu.HBM((rows, CHANNELS), BF),
            shape((clips, CHANNELS), F32),
            shape((links.devices, 1, 3 * CHANNELS), F32),
            shape((8, CHANNELS), F32),
            shape((half, CHANNELS), BF),
            shape((half, CHANNELS), BF),
        ],
        [pltpu.VMEM((3, clips, CHANNELS), F32), pltpu.VMEM((clips, 128), F32)],
    )(all_two, two, field, valid, coef, gain_two, shift_two, order, head, bias, target, keep)
    all_three = share_rows(stats_three)

    dtwo, dpre, stats_four, total_three = call(
        functools.partial(first_back_kernel, count, frames, clips),
        "temporal_back",
        (frames + 1,),
        [
            whole(all_three.shape),
            at(CHANNELS, now),
            at(CHANNELS, now),
            at(128, now),
            whole((8, HIDDEN + 128)),
            whole((8, CHANNELS)),
            whole((clips, CHANNELS)),
            whole((CHANNELS, CHANNELS)),
            at(128, before),
        ]
        + [at(width, before) for width in WIDTHS]
        + piece_specs(pieces_time),
        [at(CHANNELS, now), at(HIDDEN, before), result((links.devices, 1, 2 * HIDDEN)),
         result((1, 3 * CHANNELS))],
        [
            shape((rows, CHANNELS), BF),
            shape((rows, HIDDEN), F32),
            shape((links.devices, 1, 2 * HIDDEN), F32),
            shape((1, 3 * CHANNELS), F32),
        ],
        [
            pltpu.VMEM((3 * CHANNELS, HIDDEN), BF),
            pltpu.VMEM((rows, CHANNELS), BF),
            pltpu.VMEM((8, CHANNELS), F32),
            pltpu.VMEM((8, 2 * HIDDEN), F32),
        ],
        vmem=26,
        flops=conv_flops,
    )(all_three, two, far(mask), valid, coef, coef_two, dpool, order, valid, *convs, *pieces_time)
    all_four = share_rows(stats_four)

    taps_shape = shape((half, 3 * HIDDEN), BF)
    taps_spec = pl.BlockSpec((half, HIDDEN), lambda i: (0, i))

    def temporal_grad(part):
        return call(
            functools.partial(temporal_grad_kernel, per),
            "temporal_gradient",
            (3,),
            [pl.BlockSpec((rows, half), lambda i: (0, part)), whole((rows, HIDDEN))],
            taps_spec,
            taps_shape,
            flops=conv_flops // 2,
            gates=[all_four],
        )(dtwo, first)

    time_send = temporal_grad(1)
    time_keep = temporal_grad(0)

    scatter_time = links.scatter(time_keep, time_send, (head_keep, head_send))
    next(scatter_time)
    ready = scatter_time.send([time_keep])
    dconv, total_four = call(
        conv_back_kernel,
        "spatial_norm_back",
        (frames,),
        [whole(all_four.shape)]
        + [at(width) for width in WIDTHS]
        + [at(HIDDEN), at(128), whole((8, HIDDEN + 128))],
        [at(HIDDEN), result((1, 2 * HIDDEN))],
        [shape((rows, HIDDEN), BF), shape((1, 2 * HIDDEN), F32)],
        [pltpu.VMEM((8, HIDDEN), F32)],
        gates=ready,
    )(all_four, *convs, dpre, valid, coef)

    def spatial_grad(tap_row, part, gates):
        return call(
            functools.partial(spatial_grad_kernel, tap_row, per, group),
            "spatial_gradient",
            (3,),
            [pl.BlockSpec((rows, half), lambda i: (0, 2 * i + part)), whole((rows, HIDDEN))],
            taps_spec,
            taps_shape,
            flops=conv_flops // 2,
            gates=gates,
        )(late_cols, dconv)

    send = spatial_grad(1, 1, [])
    keep = spatial_grad(1, 0, [send])
    scatter_mid = links.scatter(keep, send)
    next(scatter_mid)
    ready = scatter_time.send([keep]) + scatter_mid.send([keep])
    send = spatial_grad(0, 1, ready)
    keep = spatial_grad(0, 0, [send])
    scatter_top = links.scatter(keep, send)
    next(scatter_top)
    ready = scatter_time.send([keep]) + scatter_mid.send([keep]) + scatter_top.send([keep])
    send = spatial_grad(2, 1, ready)
    keep = spatial_grad(2, 0, [send])
    scatter_low = links.scatter(keep, send)
    next(scatter_low)
    ready = scatter_time.send([keep]) + scatter_mid.send([keep])
    ready += scatter_top.send([keep]) + scatter_low.send([keep])

    def field_back(tap_col, gates, extra, extra_specs, out_spec, out_shape, scratch=()):
        return call(
            functools.partial(field_back_kernel, tap_col, per, group, clips),
            "field_back",
            (frames,),
            [at(HIDDEN)]
            + [pl.BlockSpec(memory_space=pltpu.HBM)] * 3
            + extra_specs,
            out_spec,
            out_shape,
            [
                pltpu.VMEM((CHANNELS, 3 * HIDDEN), BF),
                pltpu.VMEM((per + 2 * group, HIDDEN), BF),
                *scratch,
                pltpu.SemaphoreType.DMA((9,)),
            ],
            flops=conv_flops,
            gates=gates,
        )(dconv, weights_one, weights_two, weights_three, *extra)

    partial = pltpu.HBM((rows, CHANNELS), F32)
    back = field_back(1, ready, [], [], at(CHANNELS), partial)
    time_share = scatter_time.send([back])
    ready = scatter_mid.send([back]) + scatter_top.send([back]) + scatter_low.send([back])
    back = field_back(0, ready, [far(back)], [at(CHANNELS)], at(CHANNELS), partial)
    share_mid = scatter_mid.send([back])
    ready = scatter_top.send([back]) + scatter_low.send([back])
    grad_entry = field_back(
        2,
        ready,
        [far(back), far(mask), dpool, valid, x, order],
        [
            at(CHANNELS),
            at(CHANNELS),
            whole((clips, CHANNELS)),
            at(128),
            at(CHAN_IN),
            whole((CHANNELS, CHANNELS)),
        ],
        result((CHANNELS, CHAN_IN)),
        shape((CHANNELS, CHAN_IN), BF),
        [pltpu.VMEM((CHANNELS, CHAN_IN), F32)],
    )
    entry_parts = lax.all_to_all(grad_entry.reshape(links.devices, shard, CHAN_IN), AXES, 0, 0)
    entry_share = jnp.sum(entry_parts.astype(F32), axis=0)
    share_top = scatter_top.send([grad_entry])
    scatter_low.send([grad_entry])
    share_low = scatter_low.send([])

    def taps(share):
        return share.reshape(shard, 3, HIDDEN).transpose(1, 0, 2)

    correction = fix[0, 0]
    total_three = wait_for(total_three, share_low)
    loss = total_three[0, 2 * CHANNELS + CLASSES] / coef[1, HIDDEN]
    small_shape = shape(small_rows[0].shape, F32)
    small_out = call(
        small_update_kernel,
        "small_update",
        (),
        [whole(total_three.shape), whole(total_four.shape), whole(fix.shape)]
        + [whole(small_shape.shape)] * 3,
        [result(small_shape.shape)] * 3,
        [small_shape] * 3,
    )(total_three, total_four, fix, *small_rows)
    small_out = [row[0] for row in small_out]
    spatial_grad_share = jnp.concatenate(
        [taps(share[0]) for share in (share_top, share_mid, share_low)], axis=0
    )
    time_share = time_share[0]
    temporal_share = taps(time_share[:, CHANNELS:]).transpose(0, 2, 1)
    entry_out = adamw(
        w_entry, entry_share.T, entry_first, entry_second, 0.06, DECAY_RATE, correction
    )
    spatial_out = adamw(
        w_spatial, spatial_grad_share, spatial_first, spatial_second, 0.02, DECAY_RATE, correction
    )
    temporal_out = adamw(
        w_temporal, temporal_share, temporal_first, temporal_second, 0.02, DECAY_RATE, correction
    )
    head_out = adamw(
        w_head, time_share[:, :CLASSES], head_first, head_second, 0.05, DECAY_RATE, correction
    )
    return (
        loss,
        *entry_out,
        *spatial_out,
        *temporal_out,
        *head_out,
        *small_out,
        entry_out[0].astype(BF),
        spatial_out[0].astype(BF),
        temporal_out[0].astype(BF),
        head_out[0].astype(BF),
    )


def solution(mesh):
    devices = mesh.shape["dp"] * mesh.shape["outer"]
    small_slice = mesh.shape["dp"] == 16 and mesh.shape["outer"] == 2
    links = Slice(devices) if small_slice else Plain(devices)
    both = ("dp", "outer")
    entry, spatial, temporal, head = (
        P(None, both),
        P(None, both, None),
        P(None, None, both),
        P(both, None),
    )
    placed = (
        P(both, None, None, None, None),
        P(both, None, None, None),
        P(both),
        P(both),
        P(),
        entry,
        spatial,
        temporal,
        head,
        P(),
        entry,
        entry,
        spatial,
        spatial,
        temporal,
        temporal,
        head,
        head,
        P(),
        P(),
    )
    return jax.shard_map(
        functools.partial(on_device, links),
        mesh=mesh,
        in_specs=placed,
        out_specs=(
            P(),
            *([entry] * 3),
            *([spatial] * 3),
            *([temporal] * 3),
            *([head] * 3),
            P(),
            P(),
            P(),
            entry,
            spatial,
            temporal,
            head,
        ),
        check_vma=False,
    )
```

```python
import functools

import jax
import jax.numpy as jnp
from jax import lax
from jax.experimental import pallas as pl
from jax.experimental.pallas import tpu as pltpu
from jax.sharding import PartitionSpec as P

CHANNELS = 512
HIDDEN = 1152
CLASSES = 400
CHAN_IN = 256
WIDTHS = (384, 512, 256)
STARTS = (0, 384, 896)

EPSILON = 1e-05
ADAM_EPS = 1e-08
DECAY_RATE = 0.1
SMOOTHING = 0.1

AXES = ("dp", "outer")
BF = jnp.bfloat16
F32 = jnp.float32
MIB = 1 << 20


def wide(column, times):
    return jnp.concatenate([column] * times, axis=1)


def dot_nn(left, right):
    return lax.dot_general(left, right, (((1,), (0,)), ((), ())), preferred_element_type=F32)


def dot_nt(left, right):
    return lax.dot_general(left, right, (((1,), (1,)), ((), ())), preferred_element_type=F32)


def dot_tn(left, right):
    return lax.dot_general(left, right, (((0,), (0,)), ((), ())), preferred_element_type=F32)


def reorder(rows, order, axis):
    value = jnp.concatenate(
        rows + [jnp.zeros((8 - len(rows), rows[0].shape[1]), F32)], axis=0
    )
    high = value.astype(BF).astype(F32)
    middle = (value - high).astype(BF).astype(F32)
    low = value - high - middle
    parts = jnp.concatenate([high, middle, low], axis=0).astype(BF)
    moved = lax.dot_general(parts, order, (((1,), (axis,)), ((), ())), preferred_element_type=F32)
    moved = moved[:8] + moved[8:16] + moved[16:]
    return [moved[k : k + 1] for k in range(len(rows))]


def to_owner_order(rows, order):
    return reorder(rows, order, 0)


def to_local_order(rows, order):
    return reorder(rows, order, 1)


def fold(value, step):
    return jnp.sum(value.reshape(value.shape[0] // step, step, value.shape[1]), axis=0)


def spread_row(ref, row):
    ref[...] = jnp.broadcast_to(row[None], ref.shape)


def far(value):
    return pltpu.with_memory_space_constraint(value, pltpu.HBM)


def whole(shape):
    return pl.BlockSpec(shape, lambda *_: (0,) * len(shape), pipeline_mode=pl.Buffered(1))


def result(shape):
    return pl.BlockSpec(shape, lambda *_: (0,) * len(shape))


def call(
    kernel, name, grid, in_specs, out_specs, out_shape, scratch=(), aliases=None, vmem=22, flops=0,
    gates=(), moved=20 * MIB,
):
    first, last = len(in_specs), len(in_specs) + len(gates)

    def gated(*refs):
        kernel(*refs[:first], *refs[last:])

    run = pl.pallas_call(
        gated,
        name=name,
        grid=grid,
        in_specs=list(in_specs) + [pl.BlockSpec(memory_space=pl.ANY)] * len(gates),
        out_specs=out_specs,
        out_shape=out_shape,
        scratch_shapes=list(scratch),
        input_output_aliases=aliases or {},
        compiler_params=pltpu.CompilerParams(vmem_limit_bytes=vmem * MIB),
        cost_estimate=pl.CostEstimate(flops=flops, bytes_accessed=moved, transcendentals=0),
    )
    return lambda *operands: run(*operands, *gates)


def fill_taps(pieces, w_ref):
    width = w_ref.shape[1]
    at = 0
    for piece in pieces:
        rows = piece.shape[0]
        for tap in range(9):
            w_ref[tap * CHANNELS + at : tap * CHANNELS + at + rows, :] = piece[
                :, tap * width : (tap + 1) * width
            ]
        at += rows


def save(w_ref, w_out, sem, step):
    copy = pltpu.make_async_copy(w_ref, w_out, sem)
    pl.when(step == 0)(copy.start)
    pl.when(step == pl.num_programs(0) - 1)(copy.wait)


def spatial_taps(group, cols_ref, w_ref, conv_ref):
    rows, depth = cols_ref.shape
    conv_ref[...] = dot_nn(cols_ref[...], w_ref[depth : 2 * depth])
    conv_ref[group:] += dot_nn(cols_ref[: rows - group], w_ref[:depth])
    conv_ref[: rows - group] += dot_nn(cols_ref[group:], w_ref[2 * depth :])


def add_sums(conv_ref, valid_ref, acc_ref):
    value = conv_ref[...]
    width = value.shape[1]
    kept = value * wide(valid_ref[...], width // 128)
    acc_ref[:, :width] += fold(kept, 8)
    acc_ref[:, width:] += fold(kept * value, 8)


def entry_kernel(count, side, clips, x_ref, valid_ref, *refs):
    pieces, refs = refs[:count], refs[count:]
    field_ref, cols_ref, late_ref, conv_ref, acc_ref, w_out, w_ref, e_ref, sem = refs

    @pl.when(pl.program_id(0) == 0)
    def _():
        fill_taps(pieces, w_ref)
        at = 0
        for piece in pieces:
            rows = piece.shape[0]
            e_ref[at : at + rows, :] = piece[:, 9 * w_ref.shape[1] :]
            at += rows
        acc_ref[...] = jnp.zeros_like(acc_ref)

    save(w_ref, w_out, sem, pl.program_id(0))
    value = dot_nt(x_ref[...], e_ref[...]) * wide(valid_ref[...], CHANNELS // 128)
    field_ref[...] = value
    rows = value.shape[0]
    group = side * clips
    grid3 = value.reshape(rows // group, group, CHANNELS)
    edge = jnp.zeros((rows // group, clips, CHANNELS), F32)
    left = jnp.concatenate([edge, grid3[:, : group - clips]], axis=1).reshape(rows, CHANNELS)
    right = jnp.concatenate([grid3[:, clips:], edge], axis=1).reshape(rows, CHANNELS)
    cols_ref[:, :CHANNELS] = left.astype(BF)
    cols_ref[:, CHANNELS : 2 * CHANNELS] = value.astype(BF)
    cols_ref[:, 2 * CHANNELS :] = right.astype(BF)
    late_ref[...] = cols_ref[...]
    spatial_taps(group, cols_ref, w_ref, conv_ref)
    add_sums(conv_ref, valid_ref, acc_ref)


def spatial_kernel(count, group, cols_ref, valid_ref, *refs):
    pieces, (conv_ref, acc_ref, w_out, w_ref, sem) = refs[:count], refs[count:]

    @pl.when(pl.program_id(0) == 0)
    def _():
        fill_taps(pieces, w_ref)
        acc_ref[...] = jnp.zeros_like(acc_ref)

    save(w_ref, w_out, sem, pl.program_id(0))
    spatial_taps(group, cols_ref, w_ref, conv_ref)
    add_sums(conv_ref, valid_ref, acc_ref)


def last_spatial_kernel(count, group, cols_ref, valid_ref, keep_ref, one_ref, two_ref, *refs):
    pieces, refs = refs[:count], refs[count:]
    conv_ref, stats_ref, w_out, w_ref, acc_ref, size_ref, sem = refs
    step = pl.program_id(0)

    @pl.when(step == 0)
    def _():
        fill_taps(pieces, w_ref)
        acc_ref[...] = jnp.zeros_like(acc_ref)
        size_ref[...] = jnp.zeros_like(size_ref)

    save(w_ref, w_out, sem, step)
    spatial_taps(group, cols_ref, w_ref, conv_ref)
    add_sums(conv_ref, valid_ref, acc_ref)
    size_ref[...] += fold(valid_ref[...], 8)

    @pl.when(step == pl.num_programs(0) - 1)
    def _():
        parts = (one_ref, two_ref, acc_ref)
        sums = [part[:, : part.shape[1] // 2] for part in parts]
        squares = [part[:, part.shape[1] // 2 :] for part in parts]
        line = jnp.concatenate(sums + squares + [size_ref[...], fold(keep_ref[...], 8)], axis=1)
        spread_row(stats_ref, jnp.sum(line, axis=0, keepdims=True))


def temporal_kernel(
    count, frames, recv_ref, *refs
):
    convs, (valid_ref, valid_out_ref, gain_ref, shift_ref, order_ref), refs = (
        refs[:3], refs[3:8], refs[8:]
    )
    pieces, refs = refs[:count], refs[count:]
    first_ref, two_ref, stats_ref, coef_ref, head_ref, w_ref, first_all, acc_ref = refs
    step = pl.program_id(0)
    per = valid_ref.shape[0]

    @pl.when(step == 0)
    def _():
        at = 0
        for piece in pieces:
            rows = piece.shape[0]
            head_ref[at : at + rows, :] = piece[:, :CHANNELS]
            w_ref[at : at + rows, :] = piece[:, CHANNELS:]
            at += rows
        total = jnp.sum(recv_ref[...], axis=0)
        count_all = total[:, 2 * HIDDEN : 2 * HIDDEN + 128]
        wide_count = wide(count_all, HIDDEN // 128)
        mean = total[:, :HIDDEN] / wide_count
        variance = total[:, HIDDEN : 2 * HIDDEN] / wide_count - mean * mean
        coef_ref[...] = jnp.zeros_like(coef_ref)
        coef_ref[0:1, :HIDDEN] = mean
        coef_ref[1:2, :HIDDEN] = lax.rsqrt(variance + EPSILON)
        coef_ref[2:3, :HIDDEN] = gain_ref[...]
        coef_ref[3:4, :HIDDEN] = shift_ref[...]
        coef_ref[0:1, HIDDEN:] = count_all
        coef_ref[1:2, HIDDEN:] = total[:, 2 * HIDDEN + 128 :]
        acc_ref[...] = jnp.zeros_like(acc_ref)

    @pl.when(step < frames)
    def _():
        for conv_ref, start, width in zip(convs, STARTS, WIDTHS, strict=True):
            lanes = slice(start, start + width)
            normed = (conv_ref[...] - coef_ref[0:1, lanes]) * coef_ref[1:2, lanes]
            pre = coef_ref[2:3, lanes] * normed + coef_ref[3:4, lanes]
            first = (jnp.maximum(pre, 0.0) * wide(valid_ref[...], width // 128)).astype(BF)
            first_ref[:, lanes] = first
            first_all[pl.ds(pl.multiple_of(step * per, per), per), lanes] = first

    def frame(start, taps):
        pieces_at = [
            first_all[pl.ds(pl.multiple_of(start + k * per, per), per), :] for k in range(len(taps))
        ]
        lanes = slice(taps[0] * HIDDEN, (taps[-1] + 1) * HIDDEN)
        value = dot_nt(jnp.concatenate(pieces_at, axis=1), w_ref[:, lanes])
        two_ref[...] = value
        kept = value * wide(valid_out_ref[...], CHANNELS // 128)
        acc_ref[:, :CHANNELS] += fold(kept, 8)
        acc_ref[:, CHANNELS:] += fold(kept * value, 8)

    @pl.when(step == 1)
    def _():
        frame(0, (1, 2))

    @pl.when(jnp.logical_and(step > 1, step < frames))
    def _():
        frame((step - 2) * per, (0, 1, 2))

    @pl.when(step == frames)
    def _():
        frame((frames - 2) * per, (0, 1))
        sums = jnp.sum(acc_ref[...], axis=0, keepdims=True)
        parts = to_owner_order([sums[:, :CHANNELS], sums[:, CHANNELS:]], order_ref[...])
        spread_row(stats_ref, jnp.concatenate(parts, axis=1))


def head_kernel(
    clips, recv_ref, two_ref, field_ref, valid_ref, coef_ref, gain_ref, shift_ref, order_ref,
    head_ref, bias_ref, target_ref, keep_ref,
    mask_ref, dpool_ref, stats_ref, coef_two_ref, keep_grad_ref, send_grad_ref, acc_ref, size_ref,
):
    step = pl.program_id(0)

    @pl.when(step == 0)
    def _():
        total = jnp.sum(recv_ref[...], axis=0)
        count = wide(coef_ref[0:1, HIDDEN:], CHANNELS // 128)
        mean, square, gain, shift = to_local_order(
            [total[:, :CHANNELS] / count, total[:, CHANNELS:] / count, gain_ref[...], shift_ref[...]],
            order_ref[...],
        )
        coef_two_ref[...] = jnp.zeros_like(coef_two_ref)
        coef_two_ref[0:1, :] = mean
        coef_two_ref[1:2, :] = lax.rsqrt(square - mean * mean + EPSILON)
        coef_two_ref[2:3, :] = gain
        coef_two_ref[3:4, :] = shift
        acc_ref[...] = jnp.zeros_like(acc_ref)
        size_ref[...] = jnp.zeros_like(size_ref)

    valid = wide(valid_ref[...], CHANNELS // 128)
    normed = (two_ref[...] - coef_two_ref[0:1, :]) * coef_two_ref[1:2, :]
    pre = coef_two_ref[2:3, :] * normed + coef_two_ref[3:4, :] + field_ref[...]
    mask = jnp.where(pre > 0.0, valid, 0.0)
    mask_ref[...] = mask.astype(BF)
    acc_ref[0] += fold(jnp.maximum(pre, 0.0) * valid, clips)
    acc_ref[1] += fold(mask, clips)
    acc_ref[2] += fold(mask * normed, clips)
    size_ref[...] += fold(valid_ref[...], clips)

    @pl.when(step == pl.num_programs(0) - 1)
    def _():
        size = wide(size_ref[...], CHANNELS // 128)
        pooled_low = (acc_ref[0] / size).astype(BF)
        head = head_ref[...]
        logits = dot_nn(pooled_low, head) + bias_ref[...]
        shifted = logits - jnp.max(logits, axis=1, keepdims=True)
        log_prob = shifted - jnp.log(jnp.sum(jnp.exp(shifted), axis=1, keepdims=True))
        target = target_ref[...]
        per_clip = -jnp.sum(target * log_prob, axis=1, keepdims=True)
        keep = wide(keep_ref[...], CHANNELS // 128)
        loss = jnp.sum(keep * per_clip, axis=0, keepdims=True)
        kept = wide(coef_ref[1:2, HIDDEN:], CHANNELS // 128)
        d_logits = keep * (jnp.exp(log_prob) - target) / kept
        d_low = d_logits.astype(BF)
        grad = dot_tn(pooled_low.astype(F32), d_low.astype(F32)).astype(BF)
        half = grad.shape[0] // 2
        keep_grad_ref[...] = grad[:half]
        send_grad_ref[...] = grad[half:]
        d_pooled = dot_nt(d_low, head) / size
        dpool_ref[...] = d_pooled
        sums_one = jnp.sum(acc_ref[1] * d_pooled, axis=0, keepdims=True)
        sums_two = jnp.sum(acc_ref[2] * d_pooled, axis=0, keepdims=True)
        lane = lax.broadcasted_iota(jnp.int32, (1, CHANNELS), 1)
        parts = to_owner_order([sums_one, sums_two], order_ref[...]) + [
            jnp.where(lane < CLASSES, jnp.sum(d_logits, axis=0, keepdims=True), loss),
        ]
        spread_row(stats_ref, jnp.concatenate(parts, axis=1))


def first_back_kernel(
    count, frames, clips, recv_ref, two_ref, mask_ref, valid_ref, coef_ref, coef_two_ref, dpool_ref,
    order_ref, valid_out_ref, *refs
):
    convs, refs = refs[:3], refs[3:]
    pieces, refs = refs[:count], refs[count:]
    dtwo_ref, dpre_ref, stats_ref, total_ref, w_ref, dtwo_all, back_ref, acc_ref = refs
    step = pl.program_id(0)
    per = valid_ref.shape[0]

    @pl.when(step == 0)
    def _():
        at = 0
        for piece in pieces:
            rows = piece.shape[0]
            for t in range(3):
                w_ref[t * CHANNELS + at : t * CHANNELS + at + rows, :] = piece[
                    :, CHANNELS + t * HIDDEN : CHANNELS + (t + 1) * HIDDEN
                ]
            at += rows
        total = jnp.sum(recv_ref[...], axis=0)
        total_ref[...] = total
        each = wide(coef_ref[0:1, HIDDEN:], CHANNELS // 128)
        back_ref[0:1, :], back_ref[1:2, :] = to_local_order(
            [total[:, :CHANNELS] / each, total[:, CHANNELS : 2 * CHANNELS] / each], order_ref[...]
        )
        acc_ref[...] = jnp.zeros_like(acc_ref)

    @pl.when(step < frames)
    def _():
        valid = wide(valid_ref[...], CHANNELS // 128)
        gain = coef_two_ref[2:3, :]
        inverse = coef_two_ref[1:2, :]
        normed = (two_ref[...] - coef_two_ref[0:1, :]) * inverse
        mask = mask_ref[...].astype(F32)
        spread = jnp.broadcast_to(dpool_ref[...][None], (per // clips, clips, CHANNELS))
        d_pre = mask * spread.reshape(per, CHANNELS)
        low = (
            valid * (gain * inverse) * (d_pre - back_ref[0:1, :] - normed * back_ref[1:2, :])
        ).astype(BF)
        dtwo_ref[...] = low
        dtwo_all[pl.ds(pl.multiple_of(step * per, per), per), :] = low

    def frame(last, taps):
        pieces_at = [
            dtwo_all[pl.ds(pl.multiple_of(last - k * per, per), per), :] for k in range(len(taps))
        ]
        back = jnp.concatenate(pieces_at, axis=1)
        taps_rows = slice(taps[0] * CHANNELS, (taps[-1] + 1) * CHANNELS)
        for conv_ref, start, width in zip(convs, STARTS, WIDTHS, strict=True):
            lanes = slice(start, start + width)
            d_first = dot_nn(back, w_ref[taps_rows, lanes])
            normed = (conv_ref[...] - coef_ref[0:1, lanes]) * coef_ref[1:2, lanes]
            pre = coef_ref[2:3, lanes] * normed + coef_ref[3:4, lanes]
            d_pre = jnp.where(pre > 0.0, d_first, 0.0) * wide(valid_out_ref[...], width // 128)
            dpre_ref[:, lanes] = d_pre
            acc_ref[:, lanes] += fold(d_pre, 8)
            acc_ref[:, HIDDEN + start : HIDDEN + start + width] += fold(d_pre * normed, 8)

    @pl.when(step == 1)
    def _():
        frame(per, (0, 1))

    @pl.when(jnp.logical_and(step > 1, step < frames))
    def _():
        frame(step * per, (0, 1, 2))

    @pl.when(step == frames)
    def _():
        frame((frames - 1) * per, (1, 2))
        spread_row(stats_ref, jnp.sum(acc_ref[...], axis=0, keepdims=True))


def conv_back_kernel(
    recv_ref, conv_one, conv_two, conv_three, dpre_ref, valid_ref, coef_ref, out_ref, total_ref, back_ref
):
    @pl.when(pl.program_id(0) == 0)
    def _():
        total = jnp.sum(recv_ref[...], axis=0)
        total_ref[...] = total
        each = wide(coef_ref[0:1, HIDDEN:], HIDDEN // 128)
        back_ref[0:1, :] = total[:, :HIDDEN] / each
        back_ref[1:2, :] = total[:, HIDDEN:] / each

    for conv_ref, start, width in zip((conv_one, conv_two, conv_three), STARTS, WIDTHS, strict=True):
        lanes = slice(start, start + width)
        inverse = coef_ref[1:2, lanes]
        normed = (conv_ref[...] - coef_ref[0:1, lanes]) * inverse
        value = dpre_ref[:, lanes] - back_ref[0:1, lanes] - normed * back_ref[1:2, lanes]
        scale = coef_ref[2:3, lanes] * inverse
        out_ref[:, lanes] = (wide(valid_ref[...], width // 128) * scale * value).astype(BF)


def temporal_grad_kernel(per, dtwo_ref, first_ref, out_ref):
    rows = dtwo_ref.shape[0]

    def tap(low_out, low_in, size):
        left, right = dtwo_ref[low_out : low_out + size], first_ref[low_in : low_in + size]
        out_ref[...] = dot_tn(left, right).astype(BF)

    step = pl.program_id(0)
    pl.when(step == 0)(lambda: tap(per, 0, rows - per))
    pl.when(step == 1)(lambda: tap(0, 0, rows))
    pl.when(step == 2)(lambda: tap(0, per, rows - per))


def spatial_grad_kernel(tap_row, per, group, cols_ref, d_ref, out_ref):
    rows = d_ref.shape[0]
    if tap_row == 1:
        out_ref[...] = dot_tn(cols_ref[...], d_ref[...]).astype(BF)
        return
    left, right = (0, group) if tap_row == 0 else (group, 0)
    size = per - group
    cols = [cols_ref[f + left : f + left + size] for f in range(0, rows, per)]
    back = [d_ref[f + right : f + right + size] for f in range(0, rows, per)]
    grad = dot_tn(jnp.concatenate(cols, axis=0), jnp.concatenate(back, axis=0))
    out_ref[...] = grad.astype(BF)


def field_back_kernel(tap_col, per, group, clips, d_ref, *refs):
    weights, refs, sems = refs[:3], refs[3:-1], refs[-1]
    if tap_col == 1:
        out_ref, w_ref, pad_ref = refs
    elif tap_col == 0:
        acc_in_ref, out_ref, w_ref, pad_ref = refs
    else:
        (acc_in_ref, mask_ref, dpool_ref, valid_ref, x_ref, order_ref,
         out_ref, w_ref, pad_ref, grad_ref) = refs
    step = pl.program_id(0)

    @pl.when(step == 0)
    def _():
        copies = []
        for a in range(3):
            for j in range(3):
                copies.append(
                    pltpu.make_async_copy(
                        weights[j].at[pl.ds((3 * a + tap_col) * CHANNELS, CHANNELS), :],
                        w_ref.at[:, pl.ds(a * HIDDEN + STARTS[j], WIDTHS[j])],
                        sems.at[3 * a + j],
                    )
                )
        for copy in copies:
            copy.start()
        for copy in copies:
            copy.wait()
        pad_ref[:group] = jnp.zeros((group, HIDDEN), BF)
        pad_ref[group + per :] = jnp.zeros((group, HIDDEN), BF)

    pad_ref[group : group + per] = d_ref[...]
    left = jnp.concatenate(
        [pad_ref[(2 - a) * group : (2 - a) * group + per] for a in range(3)], axis=1
    )
    value = dot_nt(left, w_ref[...])
    if tap_col == 1:
        out_ref[...] = value
        return
    value = value.reshape(per // group, group, CHANNELS)
    edge = jnp.zeros((per // group, clips, CHANNELS), F32)
    if tap_col == 0:
        value = jnp.concatenate([value[:, clips:], edge], axis=1)
    else:
        value = jnp.concatenate([edge, value[:, : group - clips]], axis=1)
    value = acc_in_ref[...] + value.reshape(per, CHANNELS)
    if tap_col == 0:
        out_ref[...] = value
        return
    spread = jnp.broadcast_to(dpool_ref[...][None], (per // clips, clips, CHANNELS))
    value = value + mask_ref[...].astype(F32) * spread.reshape(per, CHANNELS)
    d_entry = (value * wide(valid_ref[...], CHANNELS // 128)).astype(BF)
    grad = dot_tn(d_entry, x_ref[...])

    @pl.when(step == 0)
    def _():
        grad_ref[...] = grad

    @pl.when(step > 0)
    def _():
        grad_ref[...] += grad

    @pl.when(step == pl.num_programs(0) - 1)
    def _():
        out_ref[...] = dot_tn(order_ref[...], grad_ref[...].astype(BF)).astype(BF)


def small_update_kernel(
    three_ref, four_ref, fix_ref, w_ref, first_ref, second_ref, w_out, first_out, second_out
):
    def part(lo, hi, grad):
        lanes = slice(lo, hi)
        w_out[:, lanes], first_out[:, lanes], second_out[:, lanes] = adamw(
            w_ref[:, lanes], grad, first_ref[:, lanes], second_ref[:, lanes],
            0.5, 0.0, fix_ref[:, :1],
        )

    at = 2 * HIDDEN
    part(0, HIDDEN, four_ref[:, HIDDEN:])
    part(HIDDEN, at, four_ref[:, :HIDDEN])
    part(at, at + CHANNELS, three_ref[:, CHANNELS : 2 * CHANNELS])
    part(at + CHANNELS, at + 2 * CHANNELS, three_ref[:, :CHANNELS])
    at += 2 * CHANNELS
    part(at, at + CLASSES, three_ref[:, 2 * CHANNELS : 2 * CHANNELS + CLASSES])


def wait_for(value, others):
    return lax.optimization_barrier((value, *others))[0]


def split_four(devices):
    def pairs(move):
        result = []
        for source in range(devices):
            z, x, core, y = source >> 3, (source >> 2) & 1, (source >> 1) & 1, source & 1
            z, x, core, y = move(z, x, core, y)
            result.append((source, ((z * 2 + x) * 2 + core) * 2 + y))
        return result

    along_z = [pairs(lambda z, x, c, y, k=k: ((z + k) % 4, x, c, y)) for k in range(4)]
    back_z = [pairs(lambda z, x, c, y, k=k: ((z - k) % 4, x, c, y)) for k in range(4)]
    early = pairs(lambda z, x, c, y: (z, 1 - x, c, y) if c == 0 else (z, x, c, 1 - y))
    late = pairs(lambda z, x, c, y: (z, x, c, 1 - y) if c == 0 else (z, 1 - x, c, y))
    core = pairs(lambda z, x, c, y: (z, x, 1 - c, y))
    return along_z, back_z, early, late, core


class Slice:
    def __init__(self, devices):
        self.devices = devices
        self.along_z, self.back_z, self.early, self.late, self.core = split_four(devices)

    def send(self, value, pairs):
        return lax.ppermute(value, AXES, pairs)

    def order(self, rows):
        channel = jnp.arange(CHANNELS)
        block, inside = channel // rows, channel % rows
        other, j, i, k = block >> 4, (block >> 3) & 1, (block >> 2) & 1, block & 3
        at, y = lax.axis_index("dp"), lax.axis_index("outer")
        core = (at & 1) ^ other
        x = ((at >> 1) & 1) ^ jnp.where(core == 0, i, j)
        y = y ^ jnp.where(core == 0, j, i)
        z = ((at >> 2) - k) & 3
        return (((z * 2 + x) * 2 + core) * 2 + y) * rows + inside

    def gather(self, shard, after=(), core_last=False):
        shard = wait_for(shard, after)
        if core_last:
            column = shard
            for k in (1, 2):
                came = self.send(column, self.along_z[k])
                after = yield
                column = jnp.concatenate([column, wait_for(came, after)], axis=0)
        else:
            came = [self.send(shard, self.along_z[k]) for k in (1, 2, 3)]
            after = yield
            column = jnp.concatenate([shard] + [wait_for(part, after) for part in came], axis=0)
        came = self.send(column, self.early)
        after = yield [column]
        half = jnp.concatenate([column, wait_for(came, after)], axis=0)
        rest = self.send(half, self.late)
        other = half if core_last else self.send(half, self.core)
        after = yield [half, other]
        rest = wait_for(rest, after)
        if core_last:
            other = self.send(wait_for(half, after), self.core)
        yield [half, rest, other, self.send(rest, self.core)]

    def add_halves(self, keep, came):
        half = keep.shape[0] // 2
        return keep[:half] + came[:half], keep[half:] + came[half:]

    def scatter(self, keep, send, extra=None):
        came = self.send(send, self.core)
        if extra is not None:
            came = jnp.concatenate([self.send(extra[1], self.core), came], axis=1)
        after = yield
        if extra is not None:
            keep = jnp.concatenate([extra[0], keep], axis=1)
        for pairs in (self.late, self.early, self.back_z[2], self.back_z[1]):
            keep, send = self.add_halves(keep, wait_for(came, after))
            came = self.send(send, pairs)
            after = yield [keep, send]
        yield [keep.astype(F32) + wait_for(came, after).astype(F32)]


class Plain:
    def __init__(self, devices):
        self.devices = devices

    def order(self, rows):
        return jnp.arange(CHANNELS)

    def gather(self, shard, after=(), core_last=False):
        result = [lax.all_gather(shard, AXES, axis=0, tiled=True)]
        yield
        if core_last:
            yield
        yield result
        yield [*result, *result]
        yield result

    def scatter(self, keep, send, extra=None):
        value = jnp.concatenate([keep, send], axis=0)
        if extra is not None:
            value = jnp.concatenate([jnp.concatenate(extra, axis=0), value], axis=1)
        result = [lax.psum_scatter(value.astype(F32), AXES, scatter_dimension=0, tiled=True)]
        while True:
            yield result


def share_rows(spread):
    return lax.all_to_all(spread, AXES, 0, 0)


def adamw(master, grad, first, second, rate, decay, correction):
    first_new = 0.5 * first + 0.5 * grad
    second_new = 0.5 * second + 0.5 * grad * grad
    master_new = master - rate * (
        first_new / correction / (jnp.sqrt(second_new / correction) + ADAM_EPS) + decay * master
    )
    return (master_new, first_new, second_new)


def on_device(
    links,
    clip_frames,
    valid_mask,
    labels,
    clip_keep,
    step_count,
    w_entry,
    w_spatial,
    w_temporal,
    w_head,
    small_params,
    entry_first,
    entry_second,
    spatial_first,
    spatial_second,
    temporal_first,
    temporal_second,
    head_first,
    head_second,
    small_first,
    small_second,
):
    clips, frames, height, breadth, _ = clip_frames.shape
    shard = w_spatial.shape[1]
    group = breadth * clips
    per = height * group
    rows = frames * per
    shape = jax.ShapeDtypeStruct

    def flat(taps):
        return taps.astype(BF).transpose(1, 0, 2).reshape(shard, -1)

    entry_t = w_entry.T
    temporal_t = w_temporal.transpose(0, 2, 1)
    head_pad = jnp.pad(w_head.astype(BF), ((0, 0), (0, CHANNELS - CLASSES)))
    index = links.order(shard)
    order = (index[:, None] == jnp.arange(CHANNELS)[None, :]).astype(BF)
    gain_one = small_params[None, :HIDDEN]
    shift_one = small_params[None, HIDDEN : 2 * HIDDEN]
    gain_two = small_params[None, 2 * HIDDEN : 2 * HIDDEN + CHANNELS]
    shift_two = small_params[None, 2 * HIDDEN + CHANNELS : 2 * HIDDEN + 2 * CHANNELS]
    bias = jnp.pad(
        small_params[None, 2 * HIDDEN + 2 * CHANNELS :],
        ((0, 0), (0, CHANNELS - CLASSES)),
        constant_values=-1e30,
    )
    x = clip_frames.transpose(1, 2, 3, 0, 4).reshape(rows, CHAN_IN)
    valid = valid_mask.astype(F32).transpose(1, 2, 3, 0)[..., None]
    valid = jnp.broadcast_to(valid, (*valid.shape[:4], 128)).reshape(rows, 128)
    keep = jnp.broadcast_to(clip_keep.astype(F32)[:, None], (clips, 128))
    lane = jnp.arange(CHANNELS)[None, :]
    target = jnp.where(
        lane < CLASSES,
        (1.0 - SMOOTHING) * (labels[:, None] == lane).astype(F32) + SMOOTHING / CLASSES,
        0.0,
    )

    fix = jnp.broadcast_to(1.0 - jnp.power(0.5, step_count[0].astype(F32)), (1, 128))
    small_rows = [small_params[None], small_first[None], small_second[None]]
    prepared = [order, gain_one, shift_one, gain_two, shift_two, bias, target, keep, fix]
    prepared += [*small_rows, x, valid]

    def part(j):
        return flat(w_spatial[:, :, STARTS[j] : STARTS[j] + WIDTHS[j]])

    load_mid = links.gather(jnp.concatenate([part(0), entry_t.astype(BF)], axis=1))
    next(load_mid)
    column_mid = load_mid.send([])
    load_top = links.gather(part(1), [*column_mid, *prepared])
    next(load_top)
    half_mid, other_mid = load_mid.send([])
    column_top = load_top.send([half_mid])
    load_low = links.gather(part(2), [*column_top, other_mid])
    next(load_low)
    head_time = jnp.concatenate([head_pad, flat(temporal_t)], axis=1)
    load_time = links.gather(head_time, [*column_top, other_mid], core_last=True)
    next(load_time)
    column_low = load_low.send([])
    ready = load_top.send(column_low)
    load_time.send(column_low)
    pieces_mid = load_mid.send([])
    count = len(pieces_mid)

    def at(width, where=lambda i: i):
        return pl.BlockSpec((per, width), lambda i: (where(i), 0))

    def piece_specs(pieces):
        return [whole(p.shape) for p in pieces]

    def now(i):
        return jnp.minimum(i, frames - 1)

    def before(i):
        return jnp.maximum(i - 1, 0)

    conv_flops = 2 * rows * 3 * CHANNELS * HIDDEN

    def sums(j):
        return result((8, 2 * WIDTHS[j])), shape((8, 2 * WIDTHS[j]), F32)

    def weights(j):
        return pltpu.HBM((9 * CHANNELS, WIDTHS[j]), BF)

    anywhere = pl.BlockSpec(memory_space=pl.ANY)
    field, cols, late_cols, conv_one, sums_one, weights_one = call(
        functools.partial(entry_kernel, count, breadth, clips),
        "entry_and_first_range",
        (frames,),
        [at(CHAN_IN), at(128)] + piece_specs(pieces_mid),
        [at(CHANNELS)] + [at(3 * CHANNELS)] * 2 + [at(WIDTHS[0]), sums(0)[0], anywhere],
        [
            pltpu.HBM((rows, CHANNELS), F32),
            shape((rows, 3 * CHANNELS), BF),
            pltpu.HBM((rows, 3 * CHANNELS), BF),
            shape((rows, WIDTHS[0]), F32),
            sums(0)[1],
            weights(0),
        ],
        [
            pltpu.VMEM((9 * CHANNELS, WIDTHS[0]), BF),
            pltpu.VMEM((CHANNELS, CHAN_IN), BF),
            pltpu.SemaphoreType.DMA,
        ],
        vmem=24,
        flops=conv_flops,
        gates=[ready[0], *column_low],
    )(x, valid, *pieces_mid)
    ready = load_low.send([conv_one])
    pieces_top = load_top.send([conv_one])
    column_time = load_time.send([conv_one])
    conv_two, sums_two, weights_two = call(
        functools.partial(spatial_kernel, count, group),
        "second_range",
        (frames,),
        [at(3 * CHANNELS), at(128)] + piece_specs(pieces_top),
        [at(WIDTHS[1]), sums(1)[0], anywhere],
        [shape((rows, WIDTHS[1]), F32), sums(1)[1], weights(1)],
        [pltpu.VMEM((9 * CHANNELS, WIDTHS[1]), BF), pltpu.SemaphoreType.DMA],
        flops=conv_flops,
        gates=[ready[0], *column_time],
    )(cols, valid, *pieces_top)
    pieces_low = load_low.send([conv_two])
    ready = load_time.send([conv_two])
    conv_three, stats, weights_three = call(
        functools.partial(last_spatial_kernel, count, group),
        "last_range",
        (frames,),
        [at(3 * CHANNELS), at(128), whole((clips, 128))]
        + [whole(sums_one.shape), whole(sums_two.shape)]
        + piece_specs(pieces_low),
        [at(WIDTHS[2]), result((links.devices, 1, 2 * HIDDEN + 256)), anywhere],
        [
            shape((rows, WIDTHS[2]), F32),
            shape((links.devices, 1, 2 * HIDDEN + 256), F32),
            weights(2),
        ],
        [
            pltpu.VMEM((9 * CHANNELS, WIDTHS[2]), BF),
            pltpu.VMEM((8, 2 * WIDTHS[2]), F32),
            pltpu.VMEM((8, 128), F32),
            pltpu.SemaphoreType.DMA,
        ],
        flops=conv_flops // 2,
        gates=ready[:1],
    )(cols, valid, keep, sums_one, sums_two, *pieces_low)
    convs = (conv_one, conv_two, conv_three)
    stats = wait_for(stats, ready[:1])
    all_stats = share_rows(stats)
    pieces_time = load_time.send([all_stats])

    first, two, stats_two, coef, head = call(
        functools.partial(temporal_kernel, count, frames),
        "norm_and_temporal",
        (frames + 1,),
        [whole(all_stats.shape)]
        + [at(width, now) for width in WIDTHS]
        + [at(128, now), at(128, before)]
        + [whole((1, HIDDEN))] * 2
        + [whole((CHANNELS, CHANNELS))]
        + piece_specs(pieces_time),
        [
            at(HIDDEN, now),
            at(CHANNELS, before),
            result((links.devices, 1, 2 * CHANNELS)),
            result((8, HIDDEN + 128)),
            result((CHANNELS, CHANNELS)),
        ],
        [
            pltpu.HBM((rows, HIDDEN), BF),
            shape((rows, CHANNELS), F32),
            shape((links.devices, 1, 2 * CHANNELS), F32),
            shape((8, HIDDEN + 128), F32),
            shape((CHANNELS, CHANNELS), BF),
        ],
        [
            pltpu.VMEM((CHANNELS, 3 * HIDDEN), BF),
            pltpu.VMEM((rows, HIDDEN), BF),
            pltpu.VMEM((8, 2 * CHANNELS), F32),
        ],
        vmem=26,
        flops=conv_flops,
    )(all_stats, *convs, valid, valid, gain_one, shift_one, order, *pieces_time)
    all_two = share_rows(stats_two)

    half = CHANNELS // 2
    mask, dpool, stats_three, coef_two, head_keep, head_send = call(
        functools.partial(head_kernel, clips),
        "norm_head_and_back",
        (frames,),
        [whole(all_two.shape), at(CHANNELS), at(CHANNELS), at(128), whole((8, HIDDEN + 128))]
        + [whole((1, CHANNELS))] * 2
        + [whole((CHANNELS, CHANNELS))] * 2
        + [whole((1, CHANNELS)), whole((clips, CHANNELS)), whole((clips, 128))],
        [
            at(CHANNELS),
            result((clips, CHANNELS)),
            result((links.devices, 1, 3 * CHANNELS)),
            result((8, CHANNELS)),
            result((half, CHANNELS)),
            result((half, CHANNELS)),
        ],
        [
            pltpu.HBM((rows, CHANNELS), BF),
            shape((clips, CHANNELS), F32),
            shape((links.devices, 1, 3 * CHANNELS), F32),
            shape((8, CHANNELS), F32),
            shape((half, CHANNELS), BF),
            shape((half, CHANNELS), BF),
        ],
        [pltpu.VMEM((3, clips, CHANNELS), F32), pltpu.VMEM((clips, 128), F32)],
    )(all_two, two, field, valid, coef, gain_two, shift_two, order, head, bias, target, keep)
    all_three = share_rows(stats_three)

    dtwo, dpre, stats_four, total_three = call(
        functools.partial(first_back_kernel, count, frames, clips),
        "temporal_back",
        (frames + 1,),
        [
            whole(all_three.shape),
            at(CHANNELS, now),
            at(CHANNELS, now),
            at(128, now),
            whole((8, HIDDEN + 128)),
            whole((8, CHANNELS)),
            whole((clips, CHANNELS)),
            whole((CHANNELS, CHANNELS)),
            at(128, before),
        ]
        + [at(width, before) for width in WIDTHS]
        + piece_specs(pieces_time),
        [at(CHANNELS, now), at(HIDDEN, before), result((links.devices, 1, 2 * HIDDEN)),
         result((1, 3 * CHANNELS))],
        [
            shape((rows, CHANNELS), BF),
            shape((rows, HIDDEN), F32),
            shape((links.devices, 1, 2 * HIDDEN), F32),
            shape((1, 3 * CHANNELS), F32),
        ],
        [
            pltpu.VMEM((3 * CHANNELS, HIDDEN), BF),
            pltpu.VMEM((rows, CHANNELS), BF),
            pltpu.VMEM((8, CHANNELS), F32),
            pltpu.VMEM((8, 2 * HIDDEN), F32),
        ],
        vmem=26,
        flops=conv_flops,
    )(all_three, two, far(mask), valid, coef, coef_two, dpool, order, valid, *convs, *pieces_time)
    all_four = share_rows(stats_four)

    taps_shape = shape((half, 3 * HIDDEN), BF)
    taps_spec = pl.BlockSpec((half, HIDDEN), lambda i: (0, i))

    def temporal_grad(part):
        return call(
            functools.partial(temporal_grad_kernel, per),
            "temporal_gradient",
            (3,),
            [pl.BlockSpec((rows, half), lambda i: (0, part)), whole((rows, HIDDEN))],
            taps_spec,
            taps_shape,
            flops=conv_flops // 2,
            gates=[all_four],
        )(dtwo, first)

    time_send = temporal_grad(1)
    time_keep = temporal_grad(0)

    scatter_time = links.scatter(time_keep, time_send, (head_keep, head_send))
    next(scatter_time)
    ready = scatter_time.send([time_keep])
    dconv, total_four = call(
        conv_back_kernel,
        "spatial_norm_back",
        (frames,),
        [whole(all_four.shape)]
        + [at(width) for width in WIDTHS]
        + [at(HIDDEN), at(128), whole((8, HIDDEN + 128))],
        [at(HIDDEN), result((1, 2 * HIDDEN))],
        [shape((rows, HIDDEN), BF), shape((1, 2 * HIDDEN), F32)],
        [pltpu.VMEM((8, HIDDEN), F32)],
        gates=ready,
    )(all_four, *convs, dpre, valid, coef)

    def spatial_grad(tap_row, part, gates):
        return call(
            functools.partial(spatial_grad_kernel, tap_row, per, group),
            "spatial_gradient",
            (3,),
            [pl.BlockSpec((rows, half), lambda i: (0, 2 * i + part)), whole((rows, HIDDEN))],
            taps_spec,
            taps_shape,
            flops=conv_flops // 2,
            gates=gates,
        )(late_cols, dconv)

    send = spatial_grad(1, 1, [])
    keep = spatial_grad(1, 0, [send])
    scatter_mid = links.scatter(keep, send)
    next(scatter_mid)
    ready = scatter_time.send([keep]) + scatter_mid.send([keep])
    send = spatial_grad(0, 1, ready)
    keep = spatial_grad(0, 0, [send])
    scatter_top = links.scatter(keep, send)
    next(scatter_top)
    def field_back(tap_col, gates, extra, extra_specs, out_spec, out_shape, scratch=()):
        return call(
            functools.partial(field_back_kernel, tap_col, per, group, clips),
            "field_back",
            (frames,),
            [at(HIDDEN)]
            + [pl.BlockSpec(memory_space=pltpu.HBM)] * 3
            + extra_specs,
            out_spec,
            out_shape,
            [
                pltpu.VMEM((CHANNELS, 3 * HIDDEN), BF),
                pltpu.VMEM((per + 2 * group, HIDDEN), BF),
                *scratch,
                pltpu.SemaphoreType.DMA((9,)),
            ],
            flops=conv_flops,
            gates=gates,
        )(dconv, weights_one, weights_two, weights_three, *extra)

    partial = pltpu.HBM((rows, CHANNELS), F32)
    back = field_back(1, [keep], [], [], at(CHANNELS), partial)
    ready = scatter_time.send([back]) + scatter_mid.send([back]) + scatter_top.send([back])
    send = spatial_grad(2, 1, ready)
    keep = spatial_grad(2, 0, [send])
    scatter_low = links.scatter(keep, send)
    next(scatter_low)
    ready = scatter_time.send([keep]) + scatter_mid.send([keep])
    ready += scatter_top.send([keep]) + scatter_low.send([keep])
    back = field_back(0, ready, [far(back)], [at(CHANNELS)], at(CHANNELS), partial)
    time_share = scatter_time.send([back])
    ready = scatter_mid.send([back]) + scatter_top.send([back]) + scatter_low.send([back])
    grad_entry = field_back(
        2,
        ready,
        [far(back), far(mask), dpool, valid, x, order],
        [
            at(CHANNELS),
            at(CHANNELS),
            whole((clips, CHANNELS)),
            at(128),
            at(CHAN_IN),
            whole((CHANNELS, CHANNELS)),
        ],
        result((CHANNELS, CHAN_IN)),
        shape((CHANNELS, CHAN_IN), BF),
        [pltpu.VMEM((CHANNELS, CHAN_IN), F32)],
    )
    entry_parts = lax.all_to_all(grad_entry.reshape(links.devices, shard, CHAN_IN), AXES, 0, 0)
    entry_share = jnp.sum(entry_parts.astype(F32), axis=0)
    share_mid = scatter_mid.send([grad_entry])
    scatter_low.send([grad_entry])
    scatter_top.send([grad_entry])
    share_top = scatter_top.send([])
    scatter_low.send([])
    share_low = scatter_low.send([])

    def taps(share):
        return share.reshape(shard, 3, HIDDEN).transpose(1, 0, 2)

    correction = fix[0, 0]
    total_three = wait_for(total_three, share_low)
    loss = total_three[0, 2 * CHANNELS + CLASSES] / coef[1, HIDDEN]
    small_shape = shape(small_rows[0].shape, F32)
    small_out = call(
        small_update_kernel,
        "small_update",
        (),
        [whole(total_three.shape), whole(total_four.shape), whole(fix.shape)]
        + [whole(small_shape.shape)] * 3,
        [result(small_shape.shape)] * 3,
        [small_shape] * 3,
    )(total_three, total_four, fix, *small_rows)
    small_out = [row[0] for row in small_out]
    spatial_grad_share = jnp.concatenate(
        [taps(share[0]) for share in (share_top, share_mid, share_low)], axis=0
    )
    time_share = time_share[0]
    temporal_share = taps(time_share[:, CHANNELS:]).transpose(0, 2, 1)
    entry_out = adamw(
        w_entry, entry_share.T, entry_first, entry_second, 0.06, DECAY_RATE, correction
    )
    spatial_out = adamw(
        w_spatial, spatial_grad_share, spatial_first, spatial_second, 0.02, DECAY_RATE, correction
    )
    temporal_out = adamw(
        w_temporal, temporal_share, temporal_first, temporal_second, 0.02, DECAY_RATE, correction
    )
    head_out = adamw(
        w_head, time_share[:, :CLASSES], head_first, head_second, 0.05, DECAY_RATE, correction
    )
    return (
        loss,
        *entry_out,
        *spatial_out,
        *temporal_out,
        *head_out,
        *small_out,
        entry_out[0].astype(BF),
        spatial_out[0].astype(BF),
        temporal_out[0].astype(BF),
        head_out[0].astype(BF),
    )


def solution(mesh):
    devices = mesh.shape["dp"] * mesh.shape["outer"]
    small_slice = mesh.shape["dp"] == 16 and mesh.shape["outer"] == 2
    links = Slice(devices) if small_slice else Plain(devices)
    both = ("dp", "outer")
    entry, spatial, temporal, head = (
        P(None, both),
        P(None, both, None),
        P(None, None, both),
        P(both, None),
    )
    placed = (
        P(both, None, None, None, None),
        P(both, None, None, None),
        P(both),
        P(both),
        P(),
        entry,
        spatial,
        temporal,
        head,
        P(),
        entry,
        entry,
        spatial,
        spatial,
        temporal,
        temporal,
        head,
        head,
        P(),
        P(),
    )
    return jax.shard_map(
        functools.partial(on_device, links),
        mesh=mesh,
        in_specs=placed,
        out_specs=(
            P(),
            *([entry] * 3),
            *([spatial] * 3),
            *([temporal] * 3),
            *([head] * 3),
            P(),
            P(),
            P(),
            entry,
            spatial,
            temporal,
            head,
        ),
        check_vma=False,
    )
```
